32 devices in a mesh: section: 4 (over z), dp: 8 (over y, x, core).
Axes of the slice: x: 2, y: 2, z: 4, core: 2. Of those that a mesh axis runs over, the one named last changes fastest.
Arguments:
- pages_in: bfloat16 [16, 512, 768], P('dp'), may hold values from -6 to 6
- coords: int32 [16, 2, 512], P('dp'), may hold values from 0 to 999
- boxes: int32 [16, 16, 4], P('dp'), may hold values from 0 to 512, as said below
- qkv_weight: bfloat16 [2, 768, 2304], P(None, 'dp'), may hold values from -0.21875 to 0.21875
- attn_bias: bfloat16 [2, 3, 768], P(None, None, 'dp'), may hold values from -3 to 3
- pos_weight: bfloat16 [2, 768, 768], P(None, 'dp'), may hold values from -0.21875 to 0.21875
- out_weight: bfloat16 [2, 768, 768], P(None, 'dp'), may hold values from -2.5 to 2.5
- ffn_in: bfloat16 [2, 768, 3072], P(None, 'dp'), may hold values from -0.21875 to 0.21875
- ffn_in_bias: bfloat16 [2, 3072], P(None, 'dp'), may hold values from -3 to 3
- ffn_out: bfloat16 [2, 3072, 768], P(None, 'dp'), may hold values from -0.109375 to 0.109375
- ffn_out_bias: bfloat16 [2, 768], P(None, 'dp'), may hold values from -3 to 3
- ln_gain: bfloat16 [2, 2, 768], P(None, None, 'dp'), may hold values from 0.25 to 1.75
- ln_bias: bfloat16 [2, 2, 768], P(None, None, 'dp'), may hold values from -2 to 2
- cotangent: bfloat16 [16, 512, 768], P('dp'), may hold values from -6 to 6
Outputs:
- final: bfloat16 [16, 512, 768], P('dp', 'section')
- input_grad: float32 [16, 512, 768], P('dp', 'section')
- qkv_grad: float32 [2, 768, 2304], P(None, 'dp')
- attn_bias_grad: float32 [2, 3, 768], P(None, None, 'dp')
- pos_grad: float32 [2, 768, 768], P(None, 'dp')
- out_grad: float32 [2, 768, 768], P(None, 'dp')
- ffn_in_grad: float32 [2, 768, 3072], P(None, 'dp')
- ffn_in_bias_grad: float32 [2, 3072], P(None, 'dp')
- ffn_out_grad: float32 [2, 3072, 768], P(None, 'dp')
- ffn_out_bias_grad: float32 [2, 768], P(None, 'dp')
- ln_gain_grad: float32 [2, 2, 768], P(None, None, 'dp')
- ln_bias_grad: float32 [2, 2, 768], P(None, None, 'dp')
The draws below stay inside these ranges and needn't reach their ends.
Inputs may be any that keep to these rules, and one draw needn't show every extreme that they name: `boxes`: A box slot masks keys c to e - 1 for queries a to b - 1; a slot with a = b is empty. Each page has between 1 and 16 non-empty slots, and some page has all 16; key starts are 1 or more, so that key 0 is never masked; a box spans at most 256 queries and 256 keys.
All inputs are finite; a program needn't handle non-finite values.
Results may differ from the reference program's by a relative error of at most 0.019.
Values may be sent and summed in bfloat16 or wider, within the bound.
A program may use at most 256 MiB of HBM per device.

```python
import math
import jax
import jax.numpy as jnp
from jax import lax

D = 768
HEAD_DIM = 64
FF = 3072
L = 512
BOXES = 16
PAGES = 16


def draw_boxes(key, part):
    key = jax.random.fold_in(key, 7)
    subkeys = jax.random.split(key, 6)
    counts = jax.random.randint(subkeys[0], (PAGES,), 1, BOXES + 1)
    fullest = jax.random.randint(subkeys[1], (), 0, PAGES)
    page_ids = jnp.arange(PAGES, dtype=jnp.int32)
    counts = jnp.where(page_ids == fullest, BOXES, counts)
    row_start = jax.random.randint(subkeys[2], (PAGES, BOXES), 0, L)
    row_extent = jax.random.randint(subkeys[3], (PAGES, BOXES), 1, L // 2 + 1)
    col_start = jax.random.randint(subkeys[4], (PAGES, BOXES), 1, L)
    col_extent = jax.random.randint(subkeys[5], (PAGES, BOXES), 1, L // 2 + 1)
    slot_ids = jnp.arange(BOXES, dtype=jnp.int32)
    chosen = (page_ids[:, None] == fullest) & (slot_ids[None, :] == 0)
    row_start = jnp.where(chosen, 0, row_start)
    in_use = slot_ids[None, :] < counts[:, None]
    row_end = jnp.where(in_use, jnp.minimum(row_start + row_extent, L), row_start)
    col_end = jnp.minimum(col_start + col_extent, L)
    col_start = jnp.where(chosen, L - L // 2, col_start)
    col_end = jnp.where(chosen, L, col_end)
    return jnp.stack([row_start, row_end, col_start, col_end], axis=-1).astype(jnp.int32)


def set_ends(values, own_key, low, top_value):
    longest = values.shape.index(max(values.shape))
    spots = []
    for shift in (0, 1):
        where = [jax.random.randint(jax.random.fold_in(own_key, axis), (), 0, length) for axis, length in enumerate(values.shape)]
        where[longest] = (where[longest] + shift) % values.shape[longest]
        spots.append(tuple(where))
    return values.at[spots[0]].set(low).at[spots[1]].set(top_value)


def levels(key, shape, cuts, smallest, top_value):
    loudness, own = 1.0, jax.random.fold_in(key, 6)
    for dim, shards_of in cuts:
        heights = jnp.exp(jax.random.uniform(jax.random.fold_in(own, dim), (shards_of,), jnp.float32, smallest / len(cuts), top_value / len(cuts)))
        loudness = loudness * jnp.repeat(heights, shape[dim] // shards_of).reshape([-1 if axis == dim else 1 for axis in range(len(shape))])
    return loudness


def gaussian(key, dims, scale, bound, cuts=(), held_as=jnp.bfloat16):
    gain = levels(key, dims, cuts, -0.22, 0.18) if cuts else 1.0
    entries = jax.random.normal(key, dims, jnp.float32) * scale * gain
    return jnp.minimum(jnp.maximum(entries, -bound), bound).astype(held_as)


def setup_inputs(seed: int = 0) -> dict:
    keys = jax.random.split(jax.random.key(seed), 15)
    return {
        "pages_in": gaussian(keys[0], (PAGES, L, D), 1.0, 6.0, ((0, 8),)),
        "coords": set_ends(jax.random.randint(keys[1], (PAGES, 2, L), 0, 1000), jax.random.fold_in(keys[1], 1), 0, 999).astype(jnp.int32),
        "boxes": draw_boxes(jax.random.fold_in(keys[14], 71), 0),
        "qkv_weight": gaussian(keys[3], (2, D, 3 * D), D ** -0.5, 0.21875, ((1, 8),)),
        "attn_bias": gaussian(keys[4], (2, 3, D), 0.5, 3.0, ((2, 8),)),
        "pos_weight": gaussian(keys[5], (2, D, D), D ** -0.5, 0.21875, ((1, 8),)),
        "out_weight": gaussian(keys[6], (2, D, D), (max(D // 128, 1)) ** -0.5, 2.5, ((1, 8),)),
        "ffn_in": gaussian(keys[7], (2, D, FF), D ** -0.5, 0.21875, ((1, 8),)),
        "ffn_in_bias": gaussian(keys[8], (2, FF), 0.5, 3.0, ((1, 8),)),
        "ffn_out": gaussian(keys[9], (2, FF, D), FF ** -0.5, 0.109375, ((1, 8),)),
        "ffn_out_bias": gaussian(keys[10], (2, D), 0.5, 3.0, ((1, 8),)),
        "ln_gain": jnp.clip(1.0 + 0.15 * jax.random.normal(keys[11], (2, 2, D), jnp.float32), 0.25, 1.75).astype(jnp.bfloat16),
        "ln_bias": gaussian(keys[12], (2, 2, D), 0.3, 2.0, ((2, 8),)),
        "cotangent": gaussian(keys[13], (PAGES, L, D), 1.0, 6.0, ((0, 8),)),
    }


EPSILON = 1e-06
NEGATIVE = -1e+30

@jax.custom_vjp
def low(v):
    return lax.optimization_barrier(v.astype(jnp.bfloat16)).astype(jnp.float32)

@jax.custom_vjp
def low_back(v):
    return v

def low_keep(v):
    return (low(v), None)

def low_pass(kept, grad):
    return (grad,)

def back_keep(v):
    return (v, None)

def back_low(kept, grad):
    return (low(grad),)
low.defvjp(low_keep, low_pass)
low_back.defvjp(back_keep, back_low)

def both_ways(value):
    return low_back(low(value))

def highest(left_side, right_side):
    return jnp.dot(left_side, right_side, precision=lax.Precision.HIGHEST)

def sinusoid(coord_pair, model_width):
    quarter = model_width // 4
    frequency = jnp.exp(jnp.arange(quarter, dtype=jnp.float32) * (-math.log(10000.0) / quarter))
    pieces = []
    for coord_axis in range(2):
        angles = coord_pair[coord_axis].astype(jnp.float32)[:, None] * frequency[None, :]
        pieces.append(jnp.sin(angles))
        pieces.append(jnp.cos(angles))
    return jnp.concatenate(pieces, axis=1)

def visible_of(box_page, length):
    places = jnp.arange(length, dtype=jnp.int32)
    row_hit = ((places[None, :] >= box_page[:, 0:1]) & (places[None, :] < box_page[:, 1:2])).astype(jnp.float32)
    col_hit = ((places[None, :] >= box_page[:, 2:3]) & (places[None, :] < box_page[:, 3:4])).astype(jnp.float32)
    covered = jnp.dot(row_hit.T, col_hit, precision=lax.Precision.HIGHEST)
    return covered < 0.5

def layer_norm(summed, gain_row, offset_row):
    center = summed - lax.optimization_barrier(jnp.mean(summed, axis=-1, keepdims=True))
    spread = lax.optimization_barrier(jnp.mean(center * center, axis=-1, keepdims=True))
    return center * lax.rsqrt(spread + EPSILON) * gain_row + offset_row

def by_heads(matrix):
    return matrix.reshape(matrix.shape[0], matrix.shape[1] // HEAD_DIM, HEAD_DIM)

def attention_sub(hidden, placed_in, visible, qkv_full, pos_full, out_full, bias_full, gain_row, offset_row):
    model_width = hidden.shape[1]
    projected = highest(hidden, qkv_full)
    queries = by_heads(both_ways(projected[:, :model_width] + bias_full[0]))
    key_rows = by_heads(both_ways(projected[:, model_width:2 * model_width]))
    value_rows = by_heads(both_ways(projected[:, 2 * model_width:] + bias_full[1]))
    position_rows = by_heads(both_ways(highest(placed_in, pos_full)))
    left_side = jnp.concatenate([queries, queries, position_rows], axis=2)
    right_side = jnp.concatenate([key_rows, position_rows, key_rows], axis=2)
    score_scale = 1.0 / math.sqrt(3.0 * HEAD_DIM)
    scores = jnp.einsum('ihe,jhe->hij', left_side, right_side, precision=lax.Precision.HIGHEST) * score_scale
    masked = low_back(jnp.where(visible[None, :, :], scores, NEGATIVE))
    row_max = lax.optimization_barrier(jnp.max(masked, axis=2, keepdims=True))
    powered = jnp.exp(masked - row_max)
    attention = low(powered / lax.optimization_barrier(jnp.sum(powered, axis=2, keepdims=True)))
    mixed = jnp.einsum('hij,jhe->ihe', attention, value_rows, precision=lax.Precision.HIGHEST)
    context = both_ways(mixed.reshape(hidden.shape))
    branch = low_back(highest(context, out_full) + bias_full[2])
    return both_ways(layer_norm(hidden + branch, gain_row, offset_row))

def feed_sub(hidden, in_full, in_bias, down_full, down_bias, gain_row, offset_row):
    inner = low_back(highest(hidden, in_full) + in_bias)
    active = both_ways(jax.nn.gelu(inner, approximate=False))
    branch = low_back(highest(active, down_full) + down_bias)
    return both_ways(layer_norm(hidden + branch, gain_row, offset_row))

def reference(pages_in, coords, boxes, qkv_weight, attn_bias, pos_weight, out_weight, ffn_in, ffn_in_bias, ffn_out, ffn_out_bias, ln_gain, ln_bias, cotangent):
    params = tuple((array_item.astype(jnp.float32) for array_item in (qkv_weight, attn_bias, pos_weight, out_weight, ffn_in, ffn_in_bias, ffn_out, ffn_out_bias, ln_gain, ln_bias)))

    def forward(inputs, weights):
        qkv_full, bias_all, pos_full, out_full, in_full, in_bias, down_full, down_bias, gain_all, offset_all = weights

        def one_page(page_items):
            hidden, coord_pair, box_page = page_items
            placed_in = low(sinusoid(coord_pair, hidden.shape[1]))
            visible = visible_of(box_page, hidden.shape[0])
            for layer_index in range(2):
                hidden = attention_sub(hidden, placed_in, visible, qkv_full[layer_index], pos_full[layer_index], out_full[layer_index], bias_all[layer_index], gain_all[layer_index, 0], offset_all[layer_index, 0])
                hidden = feed_sub(hidden, in_full[layer_index], in_bias[layer_index], down_full[layer_index], down_bias[layer_index], gain_all[layer_index, 1], offset_all[layer_index, 1])
            return hidden
        return lax.map(jax.checkpoint(one_page), (inputs, coords, boxes))
    outputs, pullback = jax.vjp(forward, pages_in.astype(jnp.float32), params)
    input_grad, weight_grads = pullback(cotangent.astype(jnp.float32))
    return (outputs.astype(jnp.bfloat16), input_grad, weight_grads[0], weight_grads[1], weight_grads[2], weight_grads[3], weight_grads[4], weight_grads[5], weight_grads[6], weight_grads[7], weight_grads[8], weight_grads[9])
```

```python
from functools import partial
import math

import jax
import jax.numpy as jnp
from jax import lax
from jax.experimental import pallas as pl
from jax.experimental.pallas import tpu as pltpu
from jax.sharding import PartitionSpec as P

HEAD_DIM = 64
PAIR = 2 * HEAD_DIM
EPSILON = 1e-06
NEGATIVE = -1e30
LOG2E = math.log2(math.e)
SCORE_SCALE = 1.0 / math.sqrt(3.0 * HEAD_DIM)
MESH = pl.DeviceIdType.MESH
BF = jnp.bfloat16
F32 = jnp.float32


def dot_nn(a, b):
    return jnp.dot(a, b, preferred_element_type=F32)


def dot_nt(a, b):
    return lax.dot_general(a, b, (((1,), (1,)), ((), ())), preferred_element_type=F32)


def dot_tn(a, b):
    return lax.dot_general(a, b, (((0,), (0,)), ((), ())), preferred_element_type=F32)


def gelu_and_slope(x):
    bell = jnp.exp2(x * x * (-0.5 * LOG2E))
    t = 1.0 / (1.0 + (0.3275911 / math.sqrt(2.0)) * jnp.abs(x))
    series = t * (
        0.254829592
        + t * (-0.284496736 + t * (1.421413741 + t * (-1.453152027 + t * 1.061405429)))
    )
    tail = 0.5 * series * bell
    cdf = jnp.where(x >= 0.0, 1.0 - tail, tail)
    return x * cdf, cdf + x * bell * (1.0 / math.sqrt(2.0 * math.pi))


def pipeline_kernel(
    rows,
    pages,
    cot,
    place,
    hide,
    wa,
    wb,
    vec,
    final_o,
    igrad_o,
    dwa_o,
    dwb_o,
    small_o,
    h_in,
    g_in,
    h_out,
    g_out,
    saved,
    qkvp,
    kplus,
    context,
    zed,
    rstd,
    db,
    dc,
    dy,
    fin_in,
    ig_in,
    stage,
    fsend,
    frecv,
    bsend,
    brecv,
    fin_send,
    fin_recv,
    ig_send,
    ig_recv,
    stage_sem,
):
    sections = lax.axis_size("section")
    s = lax.axis_index("section")
    last = sections - 1
    micro, length, width = h_in.shape
    hidden = wa.shape[1]
    chunks = length // rows
    quarter = length // sections
    per_chunk = rows // quarter
    pairs = width // PAIR
    is_attn = s % 2 == 0

    barrier = pltpu.get_barrier_semaphore()
    for by in range(1, sections):
        pl.semaphore_signal(
            barrier, inc=1, device_id={"section": (s + by) % sections}, device_id_type=MESH
        )
    pl.semaphore_wait(barrier, sections - 1)

    def local_in(source, target, sem, m, c):
        span = pl.ds(pl.multiple_of(c * rows, rows), rows)
        return pltpu.make_async_copy(source.at[m, span], target.at[m, span], sem.at[m, c])

    def hop(source, target, send, recv, m, c, by):
        span = pl.ds(pl.multiple_of(c * rows, rows), rows)
        return pltpu.make_async_remote_copy(
            src_ref=source.at[m, span],
            dst_ref=target.at[m, span],
            send_sem=send.at[m, c],
            recv_sem=recv.at[m, c],
            device_id={"section": (s + by + sections) % sections},
            device_id_type=MESH,
        )

    def share(source, target, send, recv, m, j):
        span = pl.ds(pl.multiple_of(j * quarter, quarter), quarter)
        return pltpu.make_async_remote_copy(
            src_ref=source.at[m, span],
            dst_ref=target.at[m],
            send_sem=send.at[m, j],
            recv_sem=recv.at[m],
            device_id={"section": j},
            device_id_type=MESH,
        )

    @pl.when(s == 0)
    def _():
        for m in range(micro):
            for c in range(chunks):
                local_in(pages, h_in, frecv, m, c).start()

    @pl.when(s == last)
    def _():
        for m in range(micro):
            for c in range(chunks):
                local_in(cot, g_in, brecv, m, c).start()

    def wait_h(m, c):
        @pl.when(s == 0)
        def _():
            local_in(pages, h_in, frecv, m, c).wait()

        @pl.when(s != 0)
        def _():
            hop(h_out, h_in, fsend, frecv, m, c, 1).wait_recv()

    def wait_g(m, c):
        @pl.when(s == last)
        def _():
            local_in(cot, g_in, brecv, m, c).wait()

        @pl.when(s != last)
        def _():
            hop(g_out, g_in, bsend, brecv, m, c, -1).wait_recv()

    def send_h(m, c):
        @pl.when(s != last)
        def _():
            hop(h_out, h_in, fsend, frecv, m, c, 1).start()

        @pl.when(s == last)
        def _():
            for i in range(per_chunk):
                j = c * per_chunk + i

                @pl.when(j != s)
                def _():
                    share(h_out, fin_in, fin_send, fin_recv, m, j).start()

    def send_g(m, c):
        @pl.when(s != 0)
        def _():
            hop(g_out, g_in, bsend, brecv, m, c, -1).start()

        @pl.when(s == 0)
        def _():
            for i in range(per_chunk):
                j = c * per_chunk + i

                @pl.when(j != s)
                def _():
                    share(g_out, ig_in, ig_send, ig_recv, m, j).start()

    def span_of(c):
        return pl.ds(pl.multiple_of(c * rows, rows), rows)

    def norm_out(m, c, summed, gain, offset):
        span = span_of(c)
        mean = jnp.mean(summed, axis=1, keepdims=True)
        center = summed - mean
        spread = jnp.mean(center * center, axis=1, keepdims=True)
        inv = lax.rsqrt(spread + EPSILON)
        z = center * inv
        zed[m, span] = z
        rstd[m, span] = jnp.broadcast_to(inv, (rows, 128))
        h_out[m, span] = (z * gain + offset).astype(BF)
        send_h(m, c)

    def norm_back(m, c, gain, gain_at, bias_at):
        span = span_of(c)
        g = g_in[m, span].astype(F32)
        z = zed[m, span]
        inv = rstd[m, span][:, :1]
        u = g * gain
        mean_u = jnp.mean(u, axis=1, keepdims=True)
        mean_uz = jnp.mean(u * z, axis=1, keepdims=True)
        grad = (u - mean_u - z * mean_uz) * inv
        low = grad.astype(BF)
        db[m, span] = low
        small_o[1:2, width : 2 * width] += jnp.sum(g * z, axis=0, keepdims=True)
        small_o[1:2, 2 * width : 3 * width] += jnp.sum(g, axis=0, keepdims=True)
        at = bias_at
        small_o[at[0] : at[0] + 1, at[1] : at[1] + width] += jnp.sum(
            low.astype(F32), axis=0, keepdims=True
        )
        return grad, low

    small_o[...] = jnp.zeros_like(small_o)
    gain = vec[1:2, width : 2 * width]
    offset = vec[1:2, 2 * width : 3 * width]

    def flush(source, at_rows, at_cols, target, slot):
        return pltpu.make_async_copy(
            source, target.at[pl.ds(at_rows, width), pl.ds(at_cols, width)], stage_sem.at[slot]
        )

    @pl.when(is_attn)
    def _():
        lane = lax.broadcasted_iota(jnp.int32, (1, PAIR), 1) < HEAD_DIM
        lane2 = lax.broadcasted_iota(jnp.int32, (1, 2 * PAIR), 1) % PAIR < HEAD_DIM

        def places(idx, _):
            m, c = idx // chunks, idx % chunks
            span = span_of(c)
            qkvp[m, span, 3 * width :] = dot_nn(place[m, span], wa[:, 3 * width :]).astype(BF)
            return 0

        lax.fori_loop(0, micro * chunks, places, 0)

        def forward(m, _):
            def project(c, _):
                span = span_of(c)
                wait_h(m, c)
                h = h_in[m, span]
                q = dot_nn(h, wa[:, :width]) + vec[0:1, :width]
                qkvp[m, span, :width] = q.astype(BF)
                k = dot_nn(h, wa[:, width : 2 * width]).astype(BF)
                qkvp[m, span, width : 2 * width] = k
                kplus[m, span] = (
                    k.astype(F32) + qkvp[m, span, 3 * width :].astype(F32)
                ).astype(BF)
                v = dot_nn(h, wa[:, 2 * width : 3 * width]) + vec[0:1, width : 2 * width]
                qkvp[m, span, 2 * width : 3 * width] = v.astype(BF)
                return 0

            lax.fori_loop(0, chunks, project, 0)

            def attend(c, _):
                span = span_of(c)

                def heads(t, _):
                    off = pl.multiple_of(t * PAIR, PAIR)
                    left = jnp.concatenate(
                        [
                            qkvp[m, span, pl.ds(off, PAIR)],
                            qkvp[m, span, pl.ds(off + 3 * width, PAIR)],
                        ],
                        axis=1,
                    )
                    right = jnp.concatenate(
                        [kplus[m, :, pl.ds(off, PAIR)], qkvp[m, :, pl.ds(off + width, PAIR)]],
                        axis=1,
                    )
                    v = qkvp[m, :, pl.ds(off + 2 * width, PAIR)]
                    bias = hide[m, span].astype(F32)
                    mixed = []
                    for side in range(2):
                        mask = lane2 if side == 0 else jnp.logical_not(lane2)
                        part = jnp.where(mask, left, jnp.zeros_like(left))
                        score = dot_nt(part, right) * (SCORE_SCALE * LOG2E) + bias
                        top = jnp.max(score, axis=1, keepdims=True)
                        power = jnp.exp2(score - top)
                        total = jnp.sum(power, axis=1, keepdims=True)
                        prob = (power * (1.0 / total)).astype(BF)
                        at = pl.multiple_of((2 * t + side) * length, length)
                        saved[m, span, pl.ds(at, length)] = prob
                        mixed.append(dot_nn(prob, v))
                    context[m, span, pl.ds(off, PAIR)] = jnp.where(
                        lane, mixed[0], mixed[1]
                    ).astype(BF)
                    return 0

                lax.fori_loop(0, pairs, heads, 0)
                branch = dot_nn(context[m, span], wb[:width, :])
                summed = h_in[m, span].astype(F32) + branch + vec[0:1, 2 * width : 3 * width]
                norm_out(m, c, summed, gain, offset)
                return 0

            lax.fori_loop(0, chunks, attend, 0)
            return 0

        lax.fori_loop(0, micro, forward, 0)

        def backward(m, _):
            def enter(c, _):
                span = span_of(c)
                wait_g(m, c)
                grad, low = norm_back(m, c, gain, None, (0, 2 * width))
                dy[span] = grad
                dc[span] = dot_nt(low, wb[:width, :]).astype(BF)
                return 0

            lax.fori_loop(0, chunks, enter, 0)

            def heads(t, _):
                off = pl.multiple_of(t * PAIR, PAIR)
                left = jnp.concatenate(
                    [qkvp[m, :, pl.ds(off, PAIR)], qkvp[m, :, pl.ds(off + 3 * width, PAIR)]],
                    axis=1,
                )
                right = jnp.concatenate(
                    [kplus[m, :, pl.ds(off, PAIR)], qkvp[m, :, pl.ds(off + width, PAIR)]],
                    axis=1,
                )
                v = qkvp[m, :, pl.ds(off + 2 * width, PAIR)]
                grad_c = dc[:, pl.ds(off, PAIR)]
                got = []
                for side in range(2):
                    mask = lane if side == 0 else jnp.logical_not(lane)
                    at = pl.multiple_of((2 * t + side) * length, length)
                    prob = saved[m, :, pl.ds(at, length)]
                    wide_p = prob.astype(F32)
                    grad_p = dot_nt(jnp.where(mask, grad_c, jnp.zeros_like(grad_c)), v)
                    dot_row = jnp.sum(wide_p * grad_p, axis=1, keepdims=True)
                    grad_s = (wide_p * (grad_p - dot_row)).astype(BF)
                    got.append(
                        (dot_tn(prob, grad_c), dot_nn(grad_s, right), dot_tn(grad_s, left))
                    )
                grad_v = jnp.where(lane, got[0][0], got[1][0]).astype(BF)
                grad_l = jnp.where(lane2, got[0][1], got[1][1])
                grad_r = jnp.where(lane2, got[0][2], got[1][2])
                grad_q = (grad_l[:, :PAIR] * SCORE_SCALE).astype(BF)
                grad_k = ((grad_r[:, :PAIR] + grad_r[:, PAIR:]) * SCORE_SCALE).astype(BF)
                grad_pl = ((grad_l[:, PAIR:] + grad_r[:, :PAIR]) * SCORE_SCALE).astype(BF)
                qkvp[m, :, pl.ds(off, PAIR)] = grad_q
                qkvp[m, :, pl.ds(off + width, PAIR)] = grad_k
                qkvp[m, :, pl.ds(off + 2 * width, PAIR)] = grad_v
                qkvp[m, :, pl.ds(off + 3 * width, PAIR)] = grad_pl
                small_o[0:1, pl.ds(off, PAIR)] += jnp.sum(
                    grad_q.astype(F32), axis=0, keepdims=True
                )
                small_o[0:1, pl.ds(off + width, PAIR)] += jnp.sum(
                    grad_v.astype(F32), axis=0, keepdims=True
                )
                return 0

            lax.fori_loop(0, pairs, heads, 0)

            def leave(c, _):
                span = span_of(c)
                total = dy[span] + dot_nt(qkvp[m, span, : 3 * width], wa[:, : 3 * width])
                g_out[m, span] = total.astype(BF)
                send_g(m, c)
                return 0

            lax.fori_loop(0, chunks, leave, 0)
            return 0

        lax.fori_loop(0, micro, backward, 0)

    blocks = hidden // width

    @pl.when(jnp.logical_not(is_attn))
    def _():
        def forward(idx, _):
            m, c = idx // chunks, idx % chunks
            span = span_of(c)
            wait_h(m, c)
            h = h_in[m, span]
            summed = h.astype(F32) + vec[1:2, :width]
            for f in range(blocks):
                at = f * width
                inner = dot_nn(h, wa[:, at : at + width]) + vec[0:1, at : at + width]
                value, slope = gelu_and_slope(inner)
                low = value.astype(BF)
                saved[m, span, at : at + width] = low
                saved[m, span, hidden + at : hidden + at + width] = slope.astype(BF)
                summed = summed + dot_nn(low, wb[at : at + width, :])
            norm_out(m, c, summed, gain, offset)
            return 0

        lax.fori_loop(0, micro * chunks, forward, 0)

        def backward(idx, _):
            m, c = idx // chunks, idx % chunks
            span = span_of(c)
            wait_g(m, c)
            total, low = norm_back(m, c, gain, None, (1, 0))
            for f in range(blocks):
                at = f * width
                grad_a = dot_nt(low, wb[at : at + width, :]).astype(BF).astype(F32)
                slope = saved[m, span, hidden + at : hidden + at + width].astype(F32)
                grad_i = (grad_a * slope).astype(BF)
                saved[m, span, hidden + at : hidden + at + width] = grad_i
                small_o[0:1, at : at + width] += jnp.sum(
                    grad_i.astype(F32), axis=0, keepdims=True
                )
                total = total + dot_nt(grad_i, wa[:, at : at + width])
            g_out[m, span] = total.astype(BF)
            send_g(m, c)
            return 0

        lax.fori_loop(0, micro * chunks, backward, 0)

    tokens = micro * length

    def tall(ref, at):
        return ref[:, :, pl.ds(at, width)].reshape(tokens, width)

    def put(value, slot, at_rows, at_cols, target):
        stage[slot] = value.astype(BF)
        flush(stage.at[slot], at_rows, at_cols, target, slot).start()

    def drain(slot):
        flush(stage.at[slot], 0, 0, dwa_o, slot).wait()

    def write_all(n, value_of, target, by_rows):
        def step(i, _):
            slot = i % 2

            @pl.when(i >= 2)
            def _():
                drain(slot)

            at = pl.multiple_of(i * width, width)
            if by_rows:
                put(value_of(at), slot, at, 0, target)
            else:
                put(value_of(at), slot, 0, at, target)
            return 0

        lax.fori_loop(0, n, step, 0)
        for i in range(max(n - 2, 0), n):
            drain(i % 2)

    @pl.when(is_attn)
    def _():
        write_all(3, lambda at: dot_tn(tall(h_in, 0), tall(qkvp, at)), dwa_o, False)
        put(dot_tn(tall(place, 0), tall(qkvp, 3 * width)), 0, 0, 3 * width, dwa_o)
        put(dot_tn(tall(context, 0), tall(db, 0)), 1, 0, 0, dwb_o)
        drain(0)
        drain(1)

    @pl.when(jnp.logical_not(is_attn))
    def _():
        write_all(
            blocks,
            lambda at: dot_tn(tall(h_in, 0), tall(saved, pl.multiple_of(at + hidden, width))),
            dwa_o,
            False,
        )
        write_all(blocks, lambda at: dot_tn(tall(saved, at), tall(db, 0)), dwb_o, True)

    for m in range(micro):
        for c in range(chunks):

            @pl.when(s != last)
            def _():
                hop(h_out, h_in, fsend, frecv, m, c, 1).wait_send()

            @pl.when(s != 0)
            def _():
                hop(g_out, g_in, bsend, brecv, m, c, -1).wait_send()

    @pl.when(s == last)
    def _():
        for m in range(micro):
            for j in range(sections - 1):
                share(h_out, fin_in, fin_send, fin_recv, m, j).wait_send()
            final_o[m] = h_out[m, (sections - 1) * quarter :]

    @pl.when(s != last)
    def _():
        for m in range(micro):
            share(h_out, fin_in, fin_send, fin_recv, m, 0).wait_recv()
            final_o[m] = fin_in[m]

    @pl.when(s == 0)
    def _():
        for m in range(micro):
            for j in range(1, sections):
                share(g_out, ig_in, ig_send, ig_recv, m, j).wait_send()
            igrad_o[m] = g_out[m, :quarter].astype(F32)

    @pl.when(s != 0)
    def _():
        for m in range(micro):
            share(g_out, ig_in, ig_send, ig_recv, m, 1).wait_recv()
            igrad_o[m] = ig_in[m].astype(F32)


def pipeline(pages, cot, place, hide, wa, wb, vec):
    micro, length, width = pages.shape
    hidden = wa.shape[1]
    sections = lax.axis_size("section")
    rows = length // 2
    chunks = length // rows
    quarter = length // sections
    heads = width // HEAD_DIM
    wide = max(2 * hidden, heads * length)
    hbm = pl.BlockSpec(memory_space=pl.ANY)
    vmem = pl.BlockSpec(memory_space=pltpu.VMEM)
    act = (micro, length, width)
    dma = pltpu.SemaphoreType.DMA
    return pl.pallas_call(
        partial(pipeline_kernel, rows),
        out_shape=(
            jax.ShapeDtypeStruct((micro, quarter, width), BF),
            jax.ShapeDtypeStruct((micro, quarter, width), F32),
            jax.ShapeDtypeStruct((width, hidden), BF),
            jax.ShapeDtypeStruct((hidden, width), BF),
            jax.ShapeDtypeStruct((8, hidden), F32),
        ),
        in_specs=[hbm, hbm, vmem, vmem, vmem, vmem, vmem],
        out_specs=(vmem, vmem, hbm, hbm, vmem),
        scratch_shapes=[
            pltpu.VMEM(act, BF),
            pltpu.VMEM(act, BF),
            pltpu.VMEM(act, BF),
            pltpu.VMEM(act, BF),
            pltpu.VMEM((micro, length, wide), BF),
            pltpu.VMEM((micro, length, 4 * width), BF),
            pltpu.VMEM(act, BF),
            pltpu.VMEM(act, BF),
            pltpu.VMEM(act, F32),
            pltpu.VMEM((micro, length, 128), F32),
            pltpu.VMEM(act, BF),
            pltpu.VMEM((length, width), BF),
            pltpu.VMEM((length, width), F32),
            pltpu.VMEM((micro, quarter, width), BF),
            pltpu.VMEM((micro, quarter, width), BF),
            pltpu.VMEM((2, width, width), BF),
            dma((micro, chunks)),
            dma((micro, chunks)),
            dma((micro, chunks)),
            dma((micro, chunks)),
            dma((micro, sections)),
            dma((micro,)),
            dma((micro, sections)),
            dma((micro,)),
            dma((2,)),
        ],
        compiler_params=pltpu.CompilerParams(
            collective_id=0, has_side_effects=True, vmem_limit_bytes=63 * 1024 * 1024
        ),
        name="pipeline",
    )(pages, cot, place, hide, wa, wb, vec)


def sinusoid(coord_pair, model_width):
    quarter = model_width // 4
    frequency = jnp.exp(jnp.arange(quarter, dtype=F32) * (-math.log(10000.0) / quarter))
    angles = coord_pair.astype(F32)[:, :, :, None] * frequency
    waves = jnp.stack([jnp.sin(angles), jnp.cos(angles)], axis=3)
    pages, axes, length = coord_pair.shape
    return waves.transpose(0, 2, 1, 3, 4).reshape(pages, length, model_width).astype(BF)


def hidden_bias(boxes, length):
    spots = jnp.arange(length, dtype=jnp.int32)
    row_hit = (spots >= boxes[:, :, 0:1]) & (spots < boxes[:, :, 1:2])
    col_hit = (spots >= boxes[:, :, 2:3]) & (spots < boxes[:, :, 3:4])
    covered = jnp.einsum(
        "pbi,pbj->pij", row_hit.astype(BF), col_hit.astype(BF), preferred_element_type=F32
    )
    return jnp.where(covered < 0.5, 0.0, NEGATIVE).astype(BF)


def shards(
    pages_in,
    coords,
    boxes,
    qkv_weight,
    attn_bias,
    pos_weight,
    out_weight,
    ffn_in,
    ffn_in_bias,
    ffn_out,
    ffn_out_bias,
    ln_gain,
    ln_bias,
    cotangent,
):
    groups = lax.axis_size("dp")
    s = lax.axis_index("section")
    layer = s // 2
    is_attn = s % 2 == 0
    micro, length, width = pages_in.shape
    hidden = ffn_in.shape[2]
    part = width // groups
    part_h = hidden // groups

    def pick(array):
        return lax.dynamic_index_in_dim(array, layer, 0, keepdims=False)

    own_a = jnp.where(
        is_attn, jnp.concatenate([pick(qkv_weight), pick(pos_weight)], axis=1), pick(ffn_in)
    )
    own_b = jnp.where(
        is_attn, jnp.pad(pick(out_weight), ((0, part_h - part), (0, 0))), pick(ffn_out)
    )
    wa = lax.all_gather(own_a, "dp", axis=0, tiled=True)
    wb_all = lax.all_gather(own_b, "dp", axis=0, tiled=False)
    wb = jnp.where(
        is_attn,
        jnp.pad(wb_all[:, :part].reshape(width, width), ((0, hidden - width), (0, 0))),
        wb_all.reshape(hidden, width),
    )

    norm_row = jnp.where(is_attn, 0, 1)
    gain_own = lax.dynamic_index_in_dim(pick(ln_gain), norm_row, 0, keepdims=False)
    offset_own = lax.dynamic_index_in_dim(pick(ln_bias), norm_row, 0, keepdims=False)
    bias_own = jnp.where(
        is_attn,
        jnp.pad(pick(attn_bias).reshape(-1), (0, part_h - 3 * part)),
        pick(ffn_in_bias),
    )
    vec_own = jnp.concatenate([bias_own, pick(ffn_out_bias), gain_own, offset_own])
    vec_all = lax.all_gather(vec_own, "dp", axis=0, tiled=False).astype(F32)
    first = jnp.where(
        is_attn,
        jnp.pad(
            vec_all[:, : 3 * part].reshape(groups, 3, part).transpose(1, 0, 2).reshape(-1),
            (0, hidden - 3 * width),
        ),
        vec_all[:, :part_h].reshape(-1),
    )
    rest = vec_all[:, part_h:].reshape(groups, 3, part).transpose(1, 0, 2).reshape(-1)
    vec = jnp.pad(
        jnp.stack([first, jnp.pad(rest, (0, hidden - 3 * width))]), ((0, 6), (0, 0))
    )

    place = sinusoid(coords, width)
    hide = hidden_bias(boxes, length)

    final, igrad, dwa, dwb, small = pipeline(pages_in, cotangent, place, hide, wa, wb, vec)

    shard_a = lax.psum_scatter(dwa, "dp", scatter_dimension=0, tiled=True)
    dwb_cut = jnp.where(
        is_attn,
        jnp.pad(
            dwb[:width].reshape(groups, part, width), ((0, 0), (0, part_h - part), (0, 0))
        ),
        dwb.reshape(groups, part_h, width),
    )
    shard_b = lax.psum_scatter(dwb_cut, "dp", scatter_dimension=0, tiled=True).reshape(
        part_h, width
    )
    small_first = jnp.where(
        is_attn,
        jnp.pad(
            small[0, : 3 * width].reshape(3, groups, part).transpose(1, 0, 2).reshape(groups, -1),
            ((0, 0), (0, part_h - 3 * part)),
        ),
        small[0].reshape(groups, part_h),
    )
    small_rest = (
        small[1, : 3 * width].reshape(3, groups, part).transpose(1, 0, 2).reshape(groups, -1)
    )
    small_cut = jnp.concatenate([small_first, small_rest], axis=1)
    shard_s = lax.psum_scatter(small_cut, "dp", scatter_dimension=0, tiled=True).reshape(-1)

    all_a = lax.all_gather(shard_a, "section", axis=0, tiled=False)
    all_b = lax.all_gather(shard_b, "section", axis=0, tiled=False)
    all_s = lax.all_gather(shard_s, "section", axis=0, tiled=False)

    attn_a, feed_a = all_a[0::2], all_a[1::2]
    attn_s, feed_s = all_s[0::2], all_s[1::2]
    rest_s = all_s[:, part_h:].reshape(-1, 2, 3, part)
    return (
        final,
        igrad,
        attn_a[:, :, : 3 * width].astype(F32),
        attn_s[:, : 3 * part].reshape(-1, 3, part),
        attn_a[:, :, 3 * width :].astype(F32),
        all_b[0::2, :part].astype(F32),
        feed_a.astype(F32),
        feed_s[:, :part_h],
        all_b[1::2].astype(F32),
        feed_s[:, part_h : part_h + part],
        rest_s[:, :, 1],
        rest_s[:, :, 2],
    )


def solution(mesh):
    in_specs = (
        P("dp", None, None),
        P("dp", None, None),
        P("dp", None, None),
        P(None, "dp", None),
        P(None, None, "dp"),
        P(None, "dp", None),
        P(None, "dp", None),
        P(None, "dp", None),
        P(None, "dp"),
        P(None, "dp", None),
        P(None, "dp"),
        P(None, None, "dp"),
        P(None, None, "dp"),
        P("dp", None, None),
    )
    out_specs = (
        P("dp", "section", None),
        P("dp", "section", None),
        P(None, "dp", None),
        P(None, None, "dp"),
        P(None, "dp", None),
        P(None, "dp", None),
        P(None, "dp", None),
        P(None, "dp"),
        P(None, "dp", None),
        P(None, "dp"),
        P(None, None, "dp"),
        P(None, None, "dp"),
    )
    return jax.shard_map(shards, mesh=mesh, in_specs=in_specs, out_specs=out_specs, check_vma=False)
```

```python
from functools import partial
import math

import jax
import jax.numpy as jnp
from jax import lax
from jax.experimental import pallas as pl
from jax.experimental.pallas import tpu as pltpu
from jax.sharding import PartitionSpec as P

HEAD_DIM = 64
PAIR = 2 * HEAD_DIM
EPSILON = 1e-06
NEGATIVE = -1e30
LOG2E = math.log2(math.e)
SCORE_SCALE = 1.0 / math.sqrt(3.0 * HEAD_DIM)
MESH = pl.DeviceIdType.MESH
BF = jnp.bfloat16
F32 = jnp.float32


def dot_nn(a, b):
    return jnp.dot(a, b, preferred_element_type=F32)


def dot_nt(a, b):
    return lax.dot_general(a, b, (((1,), (1,)), ((), ())), preferred_element_type=F32)


def dot_tn(a, b):
    return lax.dot_general(a, b, (((0,), (0,)), ((), ())), preferred_element_type=F32)


def gelu_and_slope(x):
    bell = jnp.exp2(x * x * (-0.5 * LOG2E))
    t = 1.0 / (1.0 + (0.3275911 / math.sqrt(2.0)) * jnp.abs(x))
    series = t * (
        0.254829592
        + t * (-0.284496736 + t * (1.421413741 + t * (-1.453152027 + t * 1.061405429)))
    )
    tail = 0.5 * series * bell
    cdf = jnp.where(x >= 0.0, 1.0 - tail, tail)
    return x * cdf, cdf + x * bell * (1.0 / math.sqrt(2.0 * math.pi))


class Refs:
    def __init__(self, names, refs):
        self.__dict__.update(zip(names, refs, strict=True))


def pipeline_kernel(names, rows, fused, *refs):
    r = Refs(names, refs)
    h_in, g_in, h_out, g_out = r.h_in, r.g_in, r.h_out, r.g_out
    saved, qkvp, kplus, context, zed, rstd = r.saved, r.qkvp, r.kplus, r.context, r.zed, r.rstd
    db, dc, dy, w, place, hide = r.db, r.dc, r.dy, r.w, r.place, r.hide
    vec, colsum = r.vec, r.colsum
    sections = lax.axis_size("section")
    s = lax.axis_index("section")
    kind = s % 2
    layer = s // 2
    last = sections - 1
    micro, length, width = h_in.shape
    hidden = w.shape[0] // 2
    chunks = length // rows
    quarter = length // sections
    per_chunk = rows // quarter
    pairs = width // PAIR
    blocks = hidden // width
    is_attn = kind == 0
    is_feed = kind == 1

    if fused:
        d = lax.axis_index("dp")
        part = width // 8
        half = part // 2
        core, cx, cy = d % 2, (d // 2) % 2, d // 4
        chip = d // 2
        near_c = d + 1 - 2 * core
        near_x = d + 2 - 4 * cx
        near_y = d + 4 - 8 * cy
        diag = near_x + 4 - 8 * cy
        units = 5 + 3 * kind
        tail_units = 1 + 3 * kind

    barrier = pltpu.get_barrier_semaphore()
    for by in range(1, sections):
        pl.semaphore_signal(
            barrier, inc=1, device_id={"section": (s + by) % sections}, device_id_type=MESH
        )
    if fused:
        for near in (near_c, near_x, near_y):
            pl.semaphore_signal(barrier, inc=1, device_id={"dp": near}, device_id_type=MESH)
    pl.semaphore_wait(barrier, sections - 1 + (3 if fused else 0))

    def to_section(source, target, send, recv, at):
        return pltpu.make_async_remote_copy(
            src_ref=source,
            dst_ref=target,
            send_sem=send,
            recv_sem=recv,
            device_id={"section": at},
            device_id_type=MESH,
        )

    def to_near(source, target, send, recv, near):
        return pltpu.make_async_remote_copy(
            src_ref=source,
            dst_ref=target,
            send_sem=send,
            recv_sem=recv,
            device_id={"dp": near},
            device_id_type=MESH,
        )

    def span_of(c):
        return pl.ds(pl.multiple_of(c * rows, rows), rows)

    def local_in(source, target, sem, m, c):
        span = span_of(c)
        return pltpu.make_async_copy(source.at[m, span], target.at[m, span], sem.at[m, c])

    def hop(source, target, send, recv, m, c, by):
        span = span_of(c)
        return to_section(
            source.at[m, span],
            target.at[m, span],
            send.at[m, c],
            recv.at[m, c],
            (s + by + sections) % sections,
        )

    def share(source, target, send, recv, m, j):
        span = pl.ds(pl.multiple_of(j * quarter, quarter), quarter)
        return to_section(source.at[m, span], target.at[m], send.at[m, j], recv.at[m], j)

    @pl.when(s == 0)
    def _():
        for m in range(micro):
            for c in range(chunks):
                local_in(r.pages, h_in, r.frecv, m, c).start()

    @pl.when(s == last)
    def _():
        for m in range(micro):
            for c in range(chunks):
                local_in(r.cot, g_in, r.brecv, m, c).start()

    def wait_h(m, c):
        @pl.when(s == 0)
        def _():
            local_in(r.pages, h_in, r.frecv, m, c).wait()

        @pl.when(s != 0)
        def _():
            hop(h_out, h_in, r.fsend, r.frecv, m, c, 1).wait_recv()

    def wait_g(m, c):
        @pl.when(s == last)
        def _():
            local_in(r.cot, g_in, r.brecv, m, c).wait()

        @pl.when(s != last)
        def _():
            hop(g_out, g_in, r.bsend, r.brecv, m, c, -1).wait_recv()

    def send_h(m, c):
        @pl.when(s != last)
        def _():
            hop(h_out, h_in, r.fsend, r.frecv, m, c, 1).start()

        @pl.when(s == last)
        def _():
            for i in range(per_chunk):
                j = c * per_chunk + i

                @pl.when(j != s)
                def _():
                    share(h_out, r.fin_in, r.fin_send, r.fin_recv, m, j).start()

    def send_g(m, c):
        @pl.when(s != 0)
        def _():
            hop(g_out, g_in, r.bsend, r.brecv, m, c, -1).start()

        @pl.when(s == 0)
        def _():
            for i in range(per_chunk):
                j = c * per_chunk + i

                @pl.when(j != s)
                def _():
                    share(g_out, r.ig_in, r.ig_send, r.ig_recv, m, j).start()

    def block_of(i):
        return w[i * width : (i + 1) * width, :]

    if fused:

        def shard_rows(tail, i, shard, count, first=0):
            if tail:
                at = hidden + shard * (part + 3 * part * kind) + i * part + first
            else:
                at = i * width + shard * part + first
            return pl.ds(pl.multiple_of(at, half), count)

        def gather(tail, i, t, shard, near, count=None, first=0):
            span = shard_rows(tail, i, shard, count or part, first)
            u = 4 + i if tail else i
            return to_near(w.at[span], w.at[span], r.ag_send.at[u, t], r.ag_recv.at[u, t], near)

        def over_units(step):
            def head(i, _):
                step(False, i)
                return 0

            def rest(i, _):
                step(True, i)
                return 0

            lax.fori_loop(0, 4, head, 0)
            lax.fori_loop(0, tail_units, rest, 0)

        def own_copy(source, tail, i):
            u = 4 + i if tail else i
            return pltpu.make_async_copy(
                source, w.at[shard_rows(tail, i, d, part)], r.own_sem.at[u]
            )

        @pl.when(is_attn)
        def _():
            for i in range(3):
                own_copy(
                    r.qkv_w.at[layer, :, pl.ds(i * width, width)], False, i
                ).start()
            own_copy(r.pos_w.at[layer], False, 3).start()
            own_copy(r.out_w.at[layer], True, 0).start()

        @pl.when(is_feed)
        def _():
            for i in range(4):
                own_copy(r.in_w.at[layer, :, pl.ds(i * width, width)], False, i).start()
            for i in range(4):
                own_copy(r.down_w.at[layer, pl.ds(i * part, part), :], True, i).start()

        def first_round(tail, i):
            own_copy(r.pos_w.at[layer], tail, i).wait()
            gather(tail, i, 0, d, near_x).start()
            gather(tail, i, 1, d, near_y).start()
            gather(tail, i, 2, d, near_c).start()

        def second_round(tail, i):
            gather(tail, i, 0, near_x, near_x).wait_recv()
            gather(tail, i, 3, near_x, near_y, half, 0).start()
            gather(tail, i, 5, near_x, near_c).start()
            gather(tail, i, 1, near_y, near_y).wait_recv()
            gather(tail, i, 4, near_y, near_x, half, half).start()
            gather(tail, i, 6, near_y, near_c).start()

        def third_round(tail, i):
            gather(tail, i, 3, diag, near_y, half, 0).wait_recv()
            gather(tail, i, 4, diag, near_x, half, half).wait_recv()
            gather(tail, i, 7, diag, near_c).start()

        def last_round(tail, i):
            flip = 1 - 2 * core
            gather(tail, i, 2, near_c, near_c).wait_recv()
            gather(tail, i, 5, near_x + flip, near_c).wait_recv()
            gather(tail, i, 6, near_y + flip, near_c).wait_recv()
            gather(tail, i, 7, diag + flip, near_c).wait_recv()

        def gather_sent(tail, i):
            for t, (shard, near) in enumerate(((d, near_x), (d, near_y), (d, near_c))):
                gather(tail, i, t, shard, near).wait_send()
            gather(tail, i, 3, near_x, near_y, half, 0).wait_send()
            gather(tail, i, 4, near_y, near_x, half, half).wait_send()
            gather(tail, i, 5, near_x, near_c).wait_send()
            gather(tail, i, 6, near_y, near_c).wait_send()
            gather(tail, i, 7, diag, near_c).wait_send()

        over_units(first_round)

        v = r.vec_all
        v[cy, cx, core] = r.vec_own[...]
        swaps = [
            (v.at[cy, cx, core], v.at[cy, cx, 1 - core], near_c),
            (v.at[cy, cx], v.at[cy, 1 - cx], near_x),
            (v.at[cy], v.at[1 - cy], near_y),
        ]
        for t, (mine, theirs, near) in enumerate(swaps):
            to_near(mine, mine, r.v_send.at[t], r.v_recv.at[t], near).start()
            to_near(mine, theirs, r.v_send.at[t], r.v_recv.at[t], near).wait_recv()
        for dest in range(8):
            row = v[dest // 4, (dest // 2) % 2, dest % 2]
            at = dest * part

            @pl.when(is_attn)
            def _(row=row, at=at):
                for i in range(3):
                    vec[0:1, i * width + at : i * width + at + part] = row[i : i + 1, :part]

            @pl.when(is_feed)
            def _(row=row, dest=dest):
                for i in range(3):
                    lane_at = dest * 4 * part + i * 128
                    vec[0:1, lane_at : lane_at + 128] = row[i : i + 1, :]

            for i in range(3):
                vec[1:2, i * width + at : i * width + at + part] = row[3 + i : 4 + i, :part]

        over_units(second_round)
        over_units(third_round)
        over_units(last_round)
    else:
        whole = pltpu.make_async_copy(r.w_in, w, r.own_sem)
        whole.start()
        vec[...] = r.vec_in[...]
        whole.wait()

    def norm_out(m, c, summed, gain, offset):
        span = span_of(c)
        mean = jnp.mean(summed, axis=1, keepdims=True)
        center = summed - mean
        spread = jnp.mean(center * center, axis=1, keepdims=True)
        inv = lax.rsqrt(spread + EPSILON)
        z = center * inv
        zed[m, span] = z
        rstd[m, span] = jnp.broadcast_to(inv, (rows, 128))
        h_out[m, span] = (z * gain + offset).astype(BF)
        send_h(m, c)

    def norm_back(m, c, gain, bias_at):
        span = span_of(c)
        g = g_in[m, span].astype(F32)
        z = zed[m, span]
        inv = rstd[m, span][:, :1]
        u = g * gain
        mean_u = jnp.mean(u, axis=1, keepdims=True)
        mean_uz = jnp.mean(u * z, axis=1, keepdims=True)
        grad = (u - mean_u - z * mean_uz) * inv
        low = grad.astype(BF)
        db[m, span] = low
        colsum[1:2, width : 2 * width] += jnp.sum(g * z, axis=0, keepdims=True)
        colsum[1:2, 2 * width : 3 * width] += jnp.sum(g, axis=0, keepdims=True)
        at = bias_at
        colsum[at[0] : at[0] + 1, at[1] : at[1] + width] += jnp.sum(
            low.astype(F32), axis=0, keepdims=True
        )
        return grad, low

    colsum[...] = jnp.zeros_like(colsum)
    gain = vec[1:2, width : 2 * width]
    offset = vec[1:2, 2 * width : 3 * width]

    @pl.when(is_attn)
    def _():
        lane = lax.broadcasted_iota(jnp.int32, (1, PAIR), 1) < HEAD_DIM
        lane2 = lax.broadcasted_iota(jnp.int32, (1, 2 * PAIR), 1) % PAIR < HEAD_DIM

        def places(idx, _):
            m, c = idx // chunks, idx % chunks
            span = span_of(c)
            qkvp[m, span, 3 * width :] = dot_nn(place[m, span], block_of(3)).astype(BF)
            return 0

        lax.fori_loop(0, micro * chunks, places, 0)

        def forward(m, _):
            def project(c, _):
                span = span_of(c)
                wait_h(m, c)
                h = h_in[m, span]
                q = dot_nn(h, block_of(0)) + vec[0:1, :width]
                qkvp[m, span, :width] = q.astype(BF)
                k = dot_nn(h, block_of(1)).astype(BF)
                qkvp[m, span, width : 2 * width] = k
                kplus[m, span] = (
                    k.astype(F32) + qkvp[m, span, 3 * width :].astype(F32)
                ).astype(BF)
                v = dot_nn(h, block_of(2)) + vec[0:1, width : 2 * width]
                qkvp[m, span, 2 * width : 3 * width] = v.astype(BF)
                return 0

            lax.fori_loop(0, chunks, project, 0)

            def attend(c, _):
                span = span_of(c)

                def heads(t, _):
                    off = pl.multiple_of(t * PAIR, PAIR)
                    left = jnp.concatenate(
                        [
                            qkvp[m, span, pl.ds(off, PAIR)],
                            qkvp[m, span, pl.ds(off + 3 * width, PAIR)],
                        ],
                        axis=1,
                    )
                    right = jnp.concatenate(
                        [kplus[m, :, pl.ds(off, PAIR)], qkvp[m, :, pl.ds(off + width, PAIR)]],
                        axis=1,
                    )
                    v = qkvp[m, :, pl.ds(off + 2 * width, PAIR)]
                    bias = hide[m, span].astype(F32)
                    mixed = []
                    for side in range(2):
                        mask = lane2 if side == 0 else jnp.logical_not(lane2)
                        masked = jnp.where(mask, left, jnp.zeros_like(left))
                        score = dot_nt(masked, right) * (SCORE_SCALE * LOG2E) + bias
                        top = jnp.max(score, axis=1, keepdims=True)
                        power = jnp.exp2(score - top)
                        total = jnp.sum(power, axis=1, keepdims=True)
                        prob = (power * (1.0 / total)).astype(BF)
                        at = pl.multiple_of((2 * t + side) * length, length)
                        saved[m, span, pl.ds(at, length)] = prob
                        mixed.append(dot_nn(prob, v))
                    context[m, span, pl.ds(off, PAIR)] = jnp.where(
                        lane, mixed[0], mixed[1]
                    ).astype(BF)
                    return 0

                lax.fori_loop(0, pairs, heads, 0)
                branch = dot_nn(context[m, span], block_of(4))
                summed = h_in[m, span].astype(F32) + branch + vec[0:1, 2 * width : 3 * width]
                norm_out(m, c, summed, gain, offset)
                return 0

            lax.fori_loop(0, chunks, attend, 0)
            return 0

        lax.fori_loop(0, micro, forward, 0)

        def backward(m, _):
            def enter(c, _):
                span = span_of(c)
                wait_g(m, c)
                grad, low = norm_back(m, c, gain, (0, 2 * width))
                dy[span] = grad
                dc[span] = dot_nt(low, block_of(4)).astype(BF)
                return 0

            lax.fori_loop(0, chunks, enter, 0)

            def heads(t, _):
                off = pl.multiple_of(t * PAIR, PAIR)
                left = jnp.concatenate(
                    [qkvp[m, :, pl.ds(off, PAIR)], qkvp[m, :, pl.ds(off + 3 * width, PAIR)]],
                    axis=1,
                )
                right = jnp.concatenate(
                    [kplus[m, :, pl.ds(off, PAIR)], qkvp[m, :, pl.ds(off + width, PAIR)]],
                    axis=1,
                )
                v = qkvp[m, :, pl.ds(off + 2 * width, PAIR)]
                grad_c = dc[:, pl.ds(off, PAIR)]
                got = []
                for side in range(2):
                    mask = lane if side == 0 else jnp.logical_not(lane)
                    at = pl.multiple_of((2 * t + side) * length, length)
                    prob = saved[m, :, pl.ds(at, length)]
                    wide_p = prob.astype(F32)
                    grad_p = dot_nt(jnp.where(mask, grad_c, jnp.zeros_like(grad_c)), v)
                    dot_row = jnp.sum(wide_p * grad_p, axis=1, keepdims=True)
                    grad_s = (wide_p * (grad_p - dot_row)).astype(BF)
                    got.append(
                        (dot_tn(prob, grad_c), dot_nn(grad_s, right), dot_tn(grad_s, left))
                    )
                grad_v = jnp.where(lane, got[0][0], got[1][0]).astype(BF)
                grad_l = jnp.where(lane2, got[0][1], got[1][1])
                grad_r = jnp.where(lane2, got[0][2], got[1][2])
                grad_q = (grad_l[:, :PAIR] * SCORE_SCALE).astype(BF)
                grad_k = ((grad_r[:, :PAIR] + grad_r[:, PAIR:]) * SCORE_SCALE).astype(BF)
                grad_pl = ((grad_l[:, PAIR:] + grad_r[:, :PAIR]) * SCORE_SCALE).astype(BF)
                qkvp[m, :, pl.ds(off, PAIR)] = grad_q
                qkvp[m, :, pl.ds(off + width, PAIR)] = grad_k
                qkvp[m, :, pl.ds(off + 2 * width, PAIR)] = grad_v
                qkvp[m, :, pl.ds(off + 3 * width, PAIR)] = grad_pl
                colsum[0:1, pl.ds(off, PAIR)] += jnp.sum(
                    grad_q.astype(F32), axis=0, keepdims=True
                )
                colsum[0:1, pl.ds(off + width, PAIR)] += jnp.sum(
                    grad_v.astype(F32), axis=0, keepdims=True
                )
                return 0

            lax.fori_loop(0, pairs, heads, 0)

            def leave(c, _):
                span = span_of(c)
                total = dy[span]
                for i in range(3):
                    total = total + dot_nt(
                        qkvp[m, span, i * width : (i + 1) * width], block_of(i)
                    )
                g_out[m, span] = total.astype(BF)
                send_g(m, c)
                return 0

            lax.fori_loop(0, chunks, leave, 0)
            return 0

        lax.fori_loop(0, micro, backward, 0)

    @pl.when(is_feed)
    def _():
        def forward(idx, _):
            m, c = idx // chunks, idx % chunks
            span = span_of(c)
            wait_h(m, c)
            h = h_in[m, span]
            summed = h.astype(F32) + vec[1:2, :width]
            for f in range(blocks):
                at = f * width
                inner = dot_nn(h, block_of(f)) + vec[0:1, at : at + width]
                value, slope = gelu_and_slope(inner)
                low = value.astype(BF)
                saved[m, span, at : at + width] = low
                saved[m, span, hidden + at : hidden + at + width] = slope.astype(BF)
                summed = summed + dot_nn(low, block_of(blocks + f))
            norm_out(m, c, summed, gain, offset)
            return 0

        lax.fori_loop(0, micro * chunks, forward, 0)

        def backward(idx, _):
            m, c = idx // chunks, idx % chunks
            span = span_of(c)
            wait_g(m, c)
            total, low = norm_back(m, c, gain, (1, 0))
            for f in range(blocks):
                at = f * width
                grad_a = dot_nt(low, block_of(blocks + f)).astype(BF).astype(F32)
                slope = saved[m, span, hidden + at : hidden + at + width].astype(F32)
                grad_i = (grad_a * slope).astype(BF)
                saved[m, span, hidden + at : hidden + at + width] = grad_i
                colsum[0:1, at : at + width] += jnp.sum(
                    grad_i.astype(F32), axis=0, keepdims=True
                )
                total = total + dot_nt(grad_i, block_of(f))
            g_out[m, span] = total.astype(BF)
            send_g(m, c)
            return 0

        lax.fori_loop(0, micro * chunks, backward, 0)

    tokens = micro * length
    stage = r.stage

    def tall(ref, at):
        return ref[:, :, pl.ds(at, width)].reshape(tokens, width)

    if fused:
        table, own = r.table, r.own

        def spot(ref, e, by_chip):
            return ref.at[pl.ds(4, 4), e - 4] if by_chip else ref.at[e]

        def keep(e, by_chip):
            slot = e % 2
            return pltpu.make_async_copy(
                stage.at[slot, :, core], spot(own, e, by_chip), r.keep_sem.at[slot]
            )

        def give(e, by_chip):
            slot = e % 2
            return to_near(
                stage.at[slot, :, 1 - core],
                spot(table, e, by_chip),
                r.p0_send.at[slot],
                r.p0_recv.at[e],
                near_c,
            )

        def emit(e, value, by_chip):
            slot = e % 2

            @pl.when(e >= 2)
            def _():
                keep(e, by_chip).wait()
                give(e, by_chip).wait_send()

            low = value.astype(BF)
            if by_chip:
                for p in range(2):
                    for j in range(4):
                        at = (p * 4 + j) * part
                        stage[slot, j, p] = low[at : at + part]
            else:
                stage[slot] = low.reshape(4, 2, part, width)
            keep(e, by_chip).start()
            give(e, by_chip).start()

        def settle(e, by_chip):
            keep(e, by_chip).wait()
            give(e, by_chip).wait_send()

        def finish(count, by_chip):
            settle(count - 2, by_chip)
            settle(count - 1, by_chip)
    else:

        def flush(slot, at):
            return pltpu.make_async_copy(
                stage.at[slot], r.dw_o.at[pl.ds(at, width)], r.keep_sem.at[slot]
            )

        def emit(e, value, by_chip):
            slot = e % 2

            @pl.when(e >= 2)
            def _():
                flush(slot, 0).wait()

            stage[slot] = value.astype(BF)
            flush(slot, pl.multiple_of(e * width, width)).start()

        def finish(count, by_chip):
            flush(0, 0).wait()
            flush(1, 0).wait()

    @pl.when(is_attn)
    def _():
        def step(e, _):
            at = pl.multiple_of(e * width, width)
            emit(e, dot_tn(tall(h_in, 0), tall(qkvp, at)), False)
            return 0

        lax.fori_loop(0, 3, step, 0)
        emit(3, dot_tn(tall(place, 0), tall(qkvp, 3 * width)), False)
        emit(4, dot_tn(tall(context, 0), tall(db, 0)), False)
        finish(5, False)

    @pl.when(is_feed)
    def _():
        def step(e, _):
            at = pl.multiple_of(e * width + hidden, width)
            emit(e, dot_tn(tall(h_in, 0), tall(saved, at)), False)
            return 0

        lax.fori_loop(0, blocks, step, 0)

        def step_b(i, _):
            at = pl.multiple_of(i * width, width)
            emit(i + blocks, dot_tn(tall(saved, at), tall(db, 0)), True)
            return 0

        lax.fori_loop(0, blocks, step_b, 0)
        finish(2 * blocks, True)

    if not fused:
        r.small_o[...] = colsum[...]
    else:
        low_half, high_half = pl.ds(0, half), pl.ds(half, half)

        def fetch(u):
            slot = u % 2
            return pltpu.make_async_copy(own.at[u], stage.at[slot, :, 0], r.keep_sem.at[slot])

        def add(target, other):
            return (target.astype(F32) + other.astype(F32)).astype(BF)

        def one_x(u, y):
            return to_near(
                table.at[u, 2 * y + 1 - cx, low_half],
                r.land_x.at[u, y],
                r.p1x_send.at[u, y],
                r.p1x_recv.at[u, y],
                near_x,
            )

        def one_y(u):
            return to_near(
                table.at[u, pl.ds(2 - 2 * cy, 2), high_half],
                r.land_y.at[u],
                r.p1y_send.at[u],
                r.p1y_recv.at[u],
                near_y,
            )

        def two_y(u):
            return to_near(
                table.at[u, 2 - 2 * cy + cx, low_half],
                r.land_y2.at[u],
                r.p2y_send.at[u],
                r.p2y_recv.at[u],
                near_y,
            )

        def two_x(u):
            return to_near(
                table.at[u, 2 * cy + 1 - cx, high_half],
                r.land_x2.at[u],
                r.p2x_send.at[u],
                r.p2x_recv.at[u],
                near_x,
            )

        sm = r.small
        for dest in range(8):
            row = sm.at[dest // 4, (dest // 2) % 2, dest % 2]
            at = dest * part

            @pl.when(is_attn)
            def _(row=row, at=at):
                for i in range(3):
                    row[i : i + 1, :part] = colsum[0:1, i * width + at : i * width + at + part]

            @pl.when(is_feed)
            def _(row=row, dest=dest):
                for i in range(3):
                    lane_at = dest * 4 * part + i * 128
                    row[i : i + 1, :] = colsum[0:1, lane_at : lane_at + 128]

            for i in range(3):
                row[3 + i : 4 + i, :part] = colsum[1:2, i * width + at : i * width + at + part]
        small_c = to_near(
            sm.at[:, :, 1 - core], r.small_0, r.s_send.at[0], r.s_recv.at[0], near_c
        )
        small_x = to_near(
            sm.at[:, 1 - cx, core], r.small_1, r.s_send.at[1], r.s_recv.at[1], near_x
        )
        small_y = to_near(
            sm.at[1 - cy, cx, core], r.small_2, r.s_send.at[2], r.s_recv.at[2], near_y
        )
        small_c.start()

        fetch(0).start()

        def merge_core(u, _):
            @pl.when(u + 1 < units)
            def _():
                fetch(u + 1).start()

            @pl.when(u <= 4)
            def _():
                give(u, False).wait_recv()

            @pl.when(jnp.logical_and(u == 4, is_feed))
            def _():
                for e in range(5, 8):
                    give(e, True).wait_recv()

            fetch(u).wait()
            table[u] = add(table[u], stage[u % 2, :, 0])
            for y in range(2):
                one_x(u, y).start()
            one_y(u).start()
            return 0

        lax.fori_loop(0, units, merge_core, 0)

        small_c.wait_recv()
        for y in range(2):
            for x in range(2):
                sm[y, x, core] = sm[y, x, core] + r.small_0[y, x]
        small_x.start()

        def merge_one(u, _):
            for y in range(2):
                one_x(u, y).wait_recv()
                at = 2 * y + cx
                table[u, at, :half] = add(table[u, at, :half], r.land_x[u, y])
            two_y(u).start()
            one_y(u).wait_recv()
            for x in range(2):
                at = 2 * cy + x
                table[u, at, half:] = add(table[u, at, half:], r.land_y[u, x])
            two_x(u).start()
            return 0

        lax.fori_loop(0, units, merge_one, 0)

        small_x.wait_recv()
        for y in range(2):
            sm[y, cx, core] = sm[y, cx, core] + r.small_1[y]
        small_y.start()

        def left(u, by):
            return to_section(
                table.at[u, chip],
                r.all_w.at[s, u],
                r.left_send.at[by, u],
                r.all_recv.at[s, u],
                (s - by + sections) % sections,
            )

        def right_own(u):
            return to_section(
                table.at[u, chip],
                r.all_w.at[s, u],
                r.right_send.at[s, u],
                r.all_recv.at[s, u],
                (s + 1) % sections,
            )

        def right_on(t, u):
            return to_section(
                r.all_w.at[t, u],
                r.all_w.at[t, u],
                r.right_send.at[t, u],
                r.all_recv.at[t, u],
                (s + 1) % sections,
            )

        def mine(u):
            return pltpu.make_async_copy(table.at[u, chip], r.all_w.at[s, u], r.own_sem.at[u])

        def merge_two(u, _):
            two_y(u).wait_recv()
            table[u, chip, :half] = add(table[u, chip, :half], r.land_y2[u])
            two_x(u).wait_recv()
            table[u, chip, half:] = add(table[u, chip, half:], r.land_x2[u])

            @pl.when(s != last)
            def _():
                right_own(u).start()

            for by in range(1, sections):

                @pl.when(s >= by)
                def _(by=by):
                    left(u, by).start()

            mine(u).start()
            return 0

        lax.fori_loop(0, units, merge_two, 0)

        small_y.wait_recv()
        sm[cy, cx, core] = sm[cy, cx, core] + r.small_2[...]
        small_z = [
            to_section(
                sm.at[cy, cx, core],
                r.all_s.at[s],
                r.sz_send.at[by - 1],
                r.sz_recv.at[s],
                (s + by) % sections,
            )
            for by in range(1, sections)
        ]
        for copy in small_z:
            copy.start()

        for by in range(1, sections):

            @pl.when(s >= by)
            def _(by=by):
                t = s - by

                def relay(u, _):
                    right_on(t, u).wait_recv()

                    @pl.when(s != last)
                    def _():
                        right_on(t, u).start()

                    return 0

                lax.fori_loop(0, 5 + 3 * (t % 2), relay, 0)

        for by in range(1, sections):

            @pl.when(s + by < sections)
            def _(by=by):
                t = s + by

                def arrive(u, _):
                    right_on(t, u).wait_recv()
                    return 0

                lax.fori_loop(0, 5 + 3 * (t % 2), arrive, 0)

        for by in range(1, sections):
            t = (s + by) % sections
            to_section(
                sm.at[cy, cx, core],
                r.all_s.at[t],
                r.sz_send.at[by - 1],
                r.sz_recv.at[t],
                t,
            ).wait_recv()
        r.all_s[s] = sm[cy, cx, core]

        over_units(gather_sent)
        for t, (mine_v, theirs, near) in enumerate(swaps):
            to_near(mine_v, mine_v, r.v_send.at[t], r.v_recv.at[t], near).wait_send()
        small_c.wait_send()
        small_x.wait_send()
        small_y.wait_send()
        for copy in small_z:
            copy.wait_send()

        def sent(u, _):
            for y in range(2):
                one_x(u, y).wait_send()
            one_y(u).wait_send()
            two_y(u).wait_send()
            two_x(u).wait_send()
            mine(u).wait()

            @pl.when(s != last)
            def _():
                right_own(u).wait_send()

            for by in range(1, sections):

                @pl.when(s >= by)
                def _(by=by):
                    left(u, by).wait_send()

            return 0

        lax.fori_loop(0, units, sent, 0)
        for by in range(1, sections):

            @pl.when(jnp.logical_and(s >= by, s != last))
            def _(by=by):
                t = s - by

                def relayed(u, _):
                    right_on(t, u).wait_send()
                    return 0

                lax.fori_loop(0, 5 + 3 * (t % 2), relayed, 0)

    for m in range(micro):
        for c in range(chunks):

            @pl.when(s != last)
            def _():
                hop(h_out, h_in, r.fsend, r.frecv, m, c, 1).wait_send()

            @pl.when(s != 0)
            def _():
                hop(g_out, g_in, r.bsend, r.brecv, m, c, -1).wait_send()

    @pl.when(s == last)
    def _():
        for m in range(micro):
            for j in range(sections - 1):
                share(h_out, r.fin_in, r.fin_send, r.fin_recv, m, j).wait_send()
            r.final_o[m] = h_out[m, (sections - 1) * quarter :]

    @pl.when(s != last)
    def _():
        for m in range(micro):
            share(h_out, r.fin_in, r.fin_send, r.fin_recv, m, 0).wait_recv()
            r.final_o[m] = r.fin_in[m]

    @pl.when(s == 0)
    def _():
        for m in range(micro):
            for j in range(1, sections):
                share(g_out, r.ig_in, r.ig_send, r.ig_recv, m, j).wait_send()
            r.igrad_o[m] = g_out[m, :quarter].astype(F32)

    @pl.when(s != 0)
    def _():
        for m in range(micro):
            share(g_out, r.ig_in, r.ig_send, r.ig_recv, m, 1).wait_recv()
            r.igrad_o[m] = r.ig_in[m].astype(F32)


def pipeline(fused, hidden, inputs):
    micro, length, width = inputs["pages"].shape
    sections = lax.axis_size("section")
    rows = length // 2
    chunks = length // rows
    quarter = length // sections
    heads = width // HEAD_DIM
    wide = max(2 * hidden, heads * length)
    part = width // 8
    half = part // 2
    hbm = pl.BlockSpec(memory_space=pl.ANY)
    vmem = pl.BlockSpec(memory_space=pltpu.VMEM)
    act = (micro, length, width)
    dma = pltpu.SemaphoreType.DMA
    spec = {name: hbm for name in inputs}
    for name in ("place", "hide", "vec_in", "vec_own"):
        if name in spec:
            spec[name] = vmem
    outs = {
        "final_o": (vmem, (micro, quarter, width), BF),
        "igrad_o": (vmem, (micro, quarter, width), F32),
    }
    scratch = {
        "h_in": pltpu.VMEM(act, BF),
        "g_in": pltpu.VMEM(act, BF),
        "h_out": pltpu.VMEM(act, BF),
        "g_out": pltpu.VMEM(act, BF),
        "saved": pltpu.VMEM((micro, length, wide), BF),
        "qkvp": pltpu.VMEM((micro, length, 4 * width), BF),
        "kplus": pltpu.VMEM(act, BF),
        "context": pltpu.VMEM(act, BF),
        "zed": pltpu.VMEM(act, F32),
        "rstd": pltpu.VMEM((micro, length, 128), F32),
        "db": pltpu.VMEM(act, BF),
        "dc": pltpu.VMEM((length, width), BF),
        "dy": pltpu.VMEM((length, width), F32),
        "w": pltpu.VMEM((2 * hidden, width), BF),
        "vec": pltpu.VMEM((8, hidden), F32),
        "colsum": pltpu.VMEM((8, hidden), F32),
        "fin_in": pltpu.VMEM((micro, quarter, width), BF),
        "ig_in": pltpu.VMEM((micro, quarter, width), BF),
        "fsend": dma((micro, chunks)),
        "frecv": dma((micro, chunks)),
        "bsend": dma((micro, chunks)),
        "brecv": dma((micro, chunks)),
        "fin_send": dma((micro, sections)),
        "fin_recv": dma((micro,)),
        "ig_send": dma((micro, sections)),
        "ig_recv": dma((micro,)),
        "keep_sem": dma((2,)),
    }
    if fused:
        outs["all_w"] = (hbm, (sections, 8, part, width), BF)
        outs["all_s"] = (vmem, (sections, 8, 128), F32)
        outs["own"] = (hbm, (8, 4, part, width), BF)
        scratch.update(
            stage=pltpu.VMEM((2, 4, 2, part, width), BF),
            vec_all=pltpu.VMEM((2, 2, 2, 8, 128), F32),
            small=pltpu.VMEM((2, 2, 2, 8, 128), F32),
            small_0=pltpu.VMEM((2, 2, 8, 128), F32),
            small_1=pltpu.VMEM((2, 8, 128), F32),
            small_2=pltpu.VMEM((8, 128), F32),
            table=pltpu.VMEM((8, 4, part, width), BF),
            land_x=pltpu.VMEM((8, 2, half, width), BF),
            land_y=pltpu.VMEM((8, 2, half, width), BF),
            land_x2=pltpu.VMEM((8, half, width), BF),
            land_y2=pltpu.VMEM((8, half, width), BF),
            own_sem=dma((8,)),
            ag_send=dma((8, 8)),
            ag_recv=dma((8, 8)),
            v_send=dma((3,)),
            v_recv=dma((3,)),
            s_send=dma((3,)),
            s_recv=dma((3,)),
            sz_send=dma((sections - 1,)),
            sz_recv=dma((sections,)),
            p0_send=dma((2,)),
            p0_recv=dma((8,)),
            p1x_send=dma((8, 2)),
            p1x_recv=dma((8, 2)),
            p1y_send=dma((8,)),
            p1y_recv=dma((8,)),
            p2x_send=dma((8,)),
            p2x_recv=dma((8,)),
            p2y_send=dma((8,)),
            p2y_recv=dma((8,)),
            left_send=dma((sections, 8)),
            right_send=dma((sections, 8)),
            all_recv=dma((sections, 8)),
        )
    else:
        outs["dw_o"] = (hbm, (2 * hidden, width), BF)
        outs["small_o"] = (vmem, (8, hidden), F32)
        scratch.update(stage=pltpu.VMEM((2, width, width), BF), own_sem=dma)
    names = [*inputs, *outs, *scratch]
    got = pl.pallas_call(
        partial(pipeline_kernel, names, rows, fused),
        out_shape=tuple(jax.ShapeDtypeStruct(shape, kind) for _, shape, kind in outs.values()),
        in_specs=list(spec.values()),
        out_specs=tuple(where for where, _, _ in outs.values()),
        scratch_shapes=list(scratch.values()),
        compiler_params=pltpu.CompilerParams(
            collective_id=0, has_side_effects=True, vmem_limit_bytes=63 * 1024 * 1024
        ),
        name="pipeline",
    )(*inputs.values())
    return dict(zip(outs, got, strict=True))


def sinusoid(coord_pair, model_width):
    quarter = model_width // 4
    frequency = jnp.exp(jnp.arange(quarter, dtype=F32) * (-math.log(10000.0) / quarter))
    angles = coord_pair.astype(F32)[:, :, :, None] * frequency
    waves = jnp.stack([jnp.sin(angles), jnp.cos(angles)], axis=3)
    pages, axes, length = coord_pair.shape
    return waves.transpose(0, 2, 1, 3, 4).reshape(pages, length, model_width).astype(BF)


def hidden_bias(boxes, length):
    spots = jnp.arange(length, dtype=jnp.int32)
    row_hit = (spots >= boxes[:, :, 0:1]) & (spots < boxes[:, :, 1:2])
    col_hit = (spots >= boxes[:, :, 2:3]) & (spots < boxes[:, :, 3:4])
    covered = jnp.einsum(
        "pbi,pbj->pij", row_hit.astype(BF), col_hit.astype(BF), preferred_element_type=F32
    )
    return jnp.where(covered < 0.5, 0.0, NEGATIVE).astype(BF)


def shards(
    pages_in,
    coords,
    boxes,
    qkv_weight,
    attn_bias,
    pos_weight,
    out_weight,
    ffn_in,
    ffn_in_bias,
    ffn_out,
    ffn_out_bias,
    ln_gain,
    ln_bias,
    cotangent,
):
    groups = lax.axis_size("dp")
    s = lax.axis_index("section")
    layer = s // 2
    is_attn = s % 2 == 0
    micro, length, width = pages_in.shape
    hidden = ffn_in.shape[2]
    part = width // groups
    part_h = hidden // groups

    def pick(array):
        return lax.dynamic_index_in_dim(array, layer, 0, keepdims=False)

    norm_row = s % 2
    gain_own = lax.dynamic_index_in_dim(pick(ln_gain), norm_row, 0, keepdims=False)
    offset_own = lax.dynamic_index_in_dim(pick(ln_bias), norm_row, 0, keepdims=False)
    inputs = {
        "pages": pages_in,
        "cot": cotangent,
        "place": sinusoid(coords, width),
        "hide": hidden_bias(boxes, length),
    }
    if groups == 8:
        first = jnp.where(
            is_attn,
            jnp.pad(pick(attn_bias), ((0, 0), (0, 128 - part))),
            pick(ffn_in_bias).reshape(3, 128),
        )
        rest = jnp.pad(
            jnp.stack([pick(ffn_out_bias), gain_own, offset_own]), ((0, 0), (0, 128 - part))
        )
        inputs["vec_own"] = jnp.pad(
            jnp.concatenate([first, rest], axis=0).astype(F32), ((0, 2), (0, 0))
        )
        inputs.update(
            qkv_w=qkv_weight, pos_w=pos_weight, out_w=out_weight, in_w=ffn_in, down_w=ffn_out
        )
        got = pipeline(True, hidden, inputs)
        sections = lax.axis_size("section")
        shares, sums = got["all_w"], got["all_s"]
        attn, feed = shares[0::2], shares[1::2]
        layers = sections // 2

        def side_by_side(blocks):
            return blocks.transpose(0, 2, 1, 3).reshape(layers, part, -1).astype(F32)

        rest = sums[:, 3:6, :part].reshape(layers, 2, 3, part)
        return (
            got["final_o"],
            got["igrad_o"],
            side_by_side(attn[:, :3]),
            sums[0::2, :3, :part],
            attn[:, 3].astype(F32),
            attn[:, 4].astype(F32),
            side_by_side(feed[:, :4]),
            sums[1::2, :3].reshape(layers, part_h),
            feed[:, 4:].reshape(layers, part_h, width).astype(F32),
            rest[:, 1, 0],
            rest[:, :, 1],
            rest[:, :, 2],
        )

    own_a = jnp.where(
        is_attn, jnp.concatenate([pick(qkv_weight), pick(pos_weight)], axis=1), pick(ffn_in)
    )
    own_b = jnp.where(
        is_attn, jnp.pad(pick(out_weight), ((0, part_h - part), (0, 0))), pick(ffn_out)
    )
    wa = lax.all_gather(own_a, "dp", axis=0, tiled=True)
    wb_all = lax.all_gather(own_b, "dp", axis=0, tiled=False)
    wb = jnp.where(
        is_attn,
        jnp.pad(wb_all[:, :part].reshape(width, width), ((0, hidden - width), (0, 0))),
        wb_all.reshape(hidden, width),
    )
    bias_own = jnp.where(
        is_attn,
        jnp.pad(pick(attn_bias).reshape(-1), (0, part_h - 3 * part)),
        pick(ffn_in_bias),
    )
    vec_own = jnp.concatenate([bias_own, pick(ffn_out_bias), gain_own, offset_own])
    vec_all = lax.all_gather(vec_own, "dp", axis=0, tiled=False).astype(F32)
    first = jnp.where(
        is_attn,
        jnp.pad(
            vec_all[:, : 3 * part].reshape(groups, 3, part).transpose(1, 0, 2).reshape(-1),
            (0, hidden - 3 * width),
        ),
        vec_all[:, :part_h].reshape(-1),
    )
    rest = vec_all[:, part_h:].reshape(groups, 3, part).transpose(1, 0, 2).reshape(-1)
    inputs["vec_in"] = jnp.pad(
        jnp.stack([first, jnp.pad(rest, (0, hidden - 3 * width))]), ((0, 6), (0, 0))
    )
    wide_blocks = wa.reshape(width, hidden // width, width).transpose(1, 0, 2)
    inputs["w_in"] = jnp.concatenate([wide_blocks.reshape(hidden, width), wb], axis=0)
    got = pipeline(False, hidden, inputs)
    final, igrad, dw, small = got["final_o"], got["igrad_o"], got["dw_o"], got["small_o"]
    dwa = dw[:hidden].reshape(hidden // width, width, width).transpose(1, 0, 2)
    dwa = dwa.reshape(width, hidden)
    dwb = dw[hidden:]

    shard_a = lax.psum_scatter(dwa, "dp", scatter_dimension=0, tiled=True)
    dwb_cut = jnp.where(
        is_attn,
        jnp.pad(
            dwb[:width].reshape(groups, part, width), ((0, 0), (0, part_h - part), (0, 0))
        ),
        dwb.reshape(groups, part_h, width),
    )
    shard_b = lax.psum_scatter(dwb_cut, "dp", scatter_dimension=0, tiled=True).reshape(
        part_h, width
    )
    small_first = jnp.where(
        is_attn,
        jnp.pad(
            small[0, : 3 * width].reshape(3, groups, part).transpose(1, 0, 2).reshape(groups, -1),
            ((0, 0), (0, part_h - 3 * part)),
        ),
        small[0].reshape(groups, part_h),
    )
    small_rest = (
        small[1, : 3 * width].reshape(3, groups, part).transpose(1, 0, 2).reshape(groups, -1)
    )
    small_cut = jnp.concatenate([small_first, small_rest], axis=1)
    shard_s = lax.psum_scatter(small_cut, "dp", scatter_dimension=0, tiled=True).reshape(-1)

    all_a = lax.all_gather(shard_a, "section", axis=0, tiled=False)
    all_b = lax.all_gather(shard_b, "section", axis=0, tiled=False)
    all_s = lax.all_gather(shard_s, "section", axis=0, tiled=False)

    attn_a, feed_a = all_a[0::2], all_a[1::2]
    attn_s, feed_s = all_s[0::2], all_s[1::2]
    rest_s = all_s[:, part_h:].reshape(-1, 2, 3, part)
    return (
        final,
        igrad,
        attn_a[:, :, : 3 * width].astype(F32),
        attn_s[:, : 3 * part].reshape(-1, 3, part),
        attn_a[:, :, 3 * width :].astype(F32),
        all_b[0::2, :part].astype(F32),
        feed_a.astype(F32),
        feed_s[:, :part_h],
        all_b[1::2].astype(F32),
        feed_s[:, part_h : part_h + part],
        rest_s[:, :, 1],
        rest_s[:, :, 2],
    )


def solution(mesh):
    in_specs = (
        P("dp", None, None),
        P("dp", None, None),
        P("dp", None, None),
        P(None, "dp", None),
        P(None, None, "dp"),
        P(None, "dp", None),
        P(None, "dp", None),
        P(None, "dp", None),
        P(None, "dp"),
        P(None, "dp", None),
        P(None, "dp"),
        P(None, None, "dp"),
        P(None, None, "dp"),
        P("dp", None, None),
    )
    out_specs = (
        P("dp", "section", None),
        P("dp", "section", None),
        P(None, "dp", None),
        P(None, None, "dp"),
        P(None, "dp", None),
        P(None, "dp", None),
        P(None, "dp", None),
        P(None, "dp"),
        P(None, "dp", None),
        P(None, "dp"),
        P(None, None, "dp"),
        P(None, None, "dp"),
    )
    return jax.shard_map(shards, mesh=mesh, in_specs=in_specs, out_specs=out_specs, check_vma=False)
```

```python
from functools import partial
import math

import jax
import jax.numpy as jnp
import numpy as np
from jax import lax
from jax.experimental import pallas as pl
from jax.experimental.pallas import tpu as pltpu
from jax.sharding import PartitionSpec as P

HEAD_DIM = 64
PAIR = 2 * HEAD_DIM
EPSILON = 1e-06
NEGATIVE = -1e30
LOG2E = math.log2(math.e)
SCORE_SCALE = 1.0 / math.sqrt(3.0 * HEAD_DIM)
MESH = pl.DeviceIdType.MESH
BF = jnp.bfloat16
F32 = jnp.float32


def dot_nn(a, b):
    return jnp.dot(a, b, preferred_element_type=F32)


def dot_nt(a, b):
    return lax.dot_general(a, b, (((1,), (1,)), ((), ())), preferred_element_type=F32)


def dot_tn(a, b):
    return lax.dot_general(a, b, (((0,), (0,)), ((), ())), preferred_element_type=F32)


def gelu_and_slope(x):
    bell = jnp.exp2(x * x * (-0.5 * LOG2E))
    t = 1.0 / (1.0 + (0.3275911 / math.sqrt(2.0)) * jnp.abs(x))
    series = t * (
        0.254829592
        + t * (-0.284496736 + t * (1.421413741 + t * (-1.453152027 + t * 1.061405429)))
    )
    tail = 0.5 * series * bell
    cdf = jnp.where(x >= 0.0, 1.0 - tail, tail)
    return x * cdf, cdf + x * bell * (1.0 / math.sqrt(2.0 * math.pi))


TURN_TERMS = [
    (-1.0) ** n * (2.0 * math.pi) ** (2 * n + 1) / math.factorial(2 * n + 1) for n in range(6)
]


def sine_of_turns(turns):
    rest = turns - jnp.floor(turns + 0.5)
    size = 0.25 - jnp.abs(jnp.abs(rest) - 0.25)
    square = size * size
    series = TURN_TERMS[5]
    for term in TURN_TERMS[4::-1]:
        series = series * square + term
    return jnp.where(rest < 0.0, -size, size) * series


def turns_per_unit(width):
    quarter = width // 4
    wave = 10000.0 ** (-np.arange(quarter) / quarter) / (2.0 * math.pi)
    table = np.zeros((2, width))
    table[0, : 2 * quarter] = np.tile(wave, 2)
    table[1, 2 * quarter :] = np.tile(wave, 2)
    return jnp.asarray(table, F32)


class Refs:
    def __init__(self, names, refs):
        self.__dict__.update(zip(names, refs, strict=True))


def pipeline_kernel(names, rows, fused, *refs):
    r = Refs(names, refs)
    h_in, g_in, h_out, g_out = r.h_in, r.g_in, r.h_out, r.g_out
    saved, qkvp, kplus, context, zed, rstd = r.saved, r.qkvp, r.kplus, r.context, r.zed, r.rstd
    db, w, place, hide = r.db, r.w, r.place, r.hide
    vec, colsum = r.vec, r.colsum
    sections = lax.axis_size("section")
    s = lax.axis_index("section")
    kind = s % 2
    layer = s // 2
    last = sections - 1
    micro, length, width = h_in.shape
    hidden = w.shape[0] // 2
    chunks = length // rows
    big = 2 * rows
    bigs = length // big
    quarter = length // sections
    pairs = width // PAIR
    blocks = hidden // width
    is_attn = kind == 0
    is_feed = kind == 1

    if fused:
        d = lax.axis_index("dp")
        part = width // 8
        half = part // 2
        core, cx, cy = d % 2, (d // 2) % 2, d // 4
        chip = d // 2
        near_c = d + 1 - 2 * core
        near_x = d + 2 - 4 * cx
        near_y = d + 4 - 8 * cy
        diag = near_x + 4 - 8 * cy
        units = 5 + 3 * kind
        tail_units = 1 + 3 * kind

        def peer(t):
            tc, tx, ty = t % 2, (t // 2) % 2, t // 4
            return (
                d + tc * (1 - 2 * core) + 2 * tx * (1 - 2 * cx) + 4 * ty * (1 - 2 * cy)
            )

    barrier = pltpu.get_barrier_semaphore()
    for by in range(1, sections):
        pl.semaphore_signal(
            barrier, inc=1, device_id={"section": (s + by) % sections}, device_id_type=MESH
        )
    if fused:
        for t in range(1, 8):
            pl.semaphore_signal(barrier, inc=1, device_id={"dp": peer(t)}, device_id_type=MESH)
    pl.semaphore_wait(barrier, sections - 1 + (7 if fused else 0))

    def to_section(source, target, send, recv, at):
        return pltpu.make_async_remote_copy(
            src_ref=source,
            dst_ref=target,
            send_sem=send,
            recv_sem=recv,
            device_id={"section": at},
            device_id_type=MESH,
        )

    def to_near(source, target, send, recv, near):
        return pltpu.make_async_remote_copy(
            src_ref=source,
            dst_ref=target,
            send_sem=send,
            recv_sem=recv,
            device_id={"dp": near},
            device_id_type=MESH,
        )

    def span_of(c, size=rows):
        return pl.ds(pl.multiple_of(c * size, size), size)

    def local_in(source, target, sem, m, c):
        span = span_of(c)
        return pltpu.make_async_copy(source.at[m, span], target.at[m, span], sem.at[m, c])

    def hop(source, target, send, recv, m, c, by):
        span = span_of(c)
        return to_section(
            source.at[m, span],
            target.at[m, span],
            send.at[m, c],
            recv.at[m, c],
            (s + by + sections) % sections,
        )

    def share(source, target, send, recv, m, j):
        span = pl.ds(pl.multiple_of(j * quarter, quarter), quarter)
        return to_section(source.at[m, span], target.at[m], send.at[m, j], recv.at[m], j)

    @pl.when(s == 0)
    def _():
        for m in range(micro):
            for c in range(chunks):
                local_in(r.pages, h_in, r.frecv, m, c).start()

    @pl.when(s == last)
    def _():
        for m in range(micro):
            for c in range(chunks):
                local_in(r.cot, g_in, r.brecv, m, c).start()

    def wait_h(m, c):
        @pl.when(s == 0)
        def _():
            local_in(r.pages, h_in, r.frecv, m, c).wait()

        @pl.when(s != 0)
        def _():
            hop(h_out, h_in, r.fsend, r.frecv, m, c, 1).wait_recv()

    def wait_g(m, c):
        @pl.when(s == last)
        def _():
            local_in(r.cot, g_in, r.brecv, m, c).wait()

        @pl.when(s != last)
        def _():
            hop(g_out, g_in, r.bsend, r.brecv, m, c, -1).wait_recv()

    def send_h(m, c):
        @pl.when(s != last)
        def _():
            hop(h_out, h_in, r.fsend, r.frecv, m, c, 1).start()

        @pl.when(jnp.logical_and(jnp.logical_and(s == last, c != s), m < micro - 1))
        def _():
            share(h_out, r.fin_in, r.fin_send, r.fin_recv, m, c).start()

    def send_g(m, c):
        @pl.when(s != 0)
        def _():
            hop(g_out, g_in, r.bsend, r.brecv, m, c, -1).start()

        @pl.when(jnp.logical_and(s == 0, c != s))
        def _():
            share(g_out, r.ig_in, r.ig_send, r.ig_recv, m, c).start()

    def block_of(i):
        return w[i * width : (i + 1) * width, :]

    def spots():
        columns = lax.broadcasted_iota(jnp.int32, (1, width), 1)
        phase = jnp.where((columns // (width // 4)) % 2 == 1, 0.25, 0.0)
        tokens_at = lax.broadcasted_iota(jnp.int32, (length, r.boxes.shape[2]), 0)

        def page(m, _):
            turns = lax.dot_general(
                r.coords[m].astype(F32),
                r.waves[...],
                (((0,), (0,)), ((), ())),
                precision=lax.Precision.HIGHEST,
                preferred_element_type=F32,
            )
            place[m] = sine_of_turns(turns + phase).astype(BF)
            box = r.boxes[m]

            def hit(low, high):
                inside = jnp.logical_and(
                    tokens_at >= box[low : low + 1], tokens_at < box[high : high + 1]
                )
                return jnp.where(inside, 1.0, 0.0)

            covered = dot_nt(hit(0, 1), hit(2, 3))
            hide[m] = jnp.where(covered < 0.5, 0.0, NEGATIVE).astype(BF)
            return 0

        lax.fori_loop(0, micro, page, 0)

    if fused:

        def shard_rows(tail, i, shard, count, first=0):
            if tail:
                at = hidden + shard * (part + 3 * part * kind) + i * part + first
            else:
                at = i * width + shard * part + first
            return pl.ds(pl.multiple_of(at, half), count)

        def gather(tail, i, t, shard, near, count=None, first=0):
            span = shard_rows(tail, i, shard, count or part, first)
            u = 4 + i if tail else i
            return to_near(w.at[span], w.at[span], r.ag_send.at[u, t], r.ag_recv.at[u, t], near)

        def over_units(step):
            def head(i, _):
                step(False, i)
                return 0

            def rest(i, _):
                step(True, i)
                return 0

            lax.fori_loop(0, 4, head, 0)
            lax.fori_loop(0, tail_units, rest, 0)

        def own_copy(source, tail, i):
            u = 4 + i if tail else i
            return pltpu.make_async_copy(
                source, w.at[shard_rows(tail, i, d, part)], r.own_sem.at[u]
            )

        @pl.when(is_attn)
        def _():
            for i in range(3):
                own_copy(
                    r.qkv_w.at[layer, :, pl.ds(i * width, width)], False, i
                ).start()
            own_copy(r.pos_w.at[layer], False, 3).start()
            own_copy(r.out_w.at[layer], True, 0).start()

        @pl.when(is_feed)
        def _():
            for i in range(4):
                own_copy(r.in_w.at[layer, :, pl.ds(i * width, width)], False, i).start()
            for i in range(4):
                own_copy(r.down_w.at[layer, pl.ds(i * part, part), :], True, i).start()

        def first_round(tail, i):
            own_copy(r.pos_w.at[layer], tail, i).wait()
            gather(tail, i, 0, d, near_x).start()
            gather(tail, i, 1, d, near_y).start()
            gather(tail, i, 2, d, near_c).start()

        def second_round(tail, i):
            gather(tail, i, 0, near_x, near_x).wait_recv()
            gather(tail, i, 3, near_x, near_y, half, 0).start()
            gather(tail, i, 5, near_x, near_c).start()
            gather(tail, i, 1, near_y, near_y).wait_recv()
            gather(tail, i, 4, near_y, near_x, half, half).start()
            gather(tail, i, 6, near_y, near_c).start()

        def third_round(tail, i):
            gather(tail, i, 3, diag, near_y, half, 0).wait_recv()
            gather(tail, i, 4, diag, near_x, half, half).wait_recv()
            gather(tail, i, 7, diag, near_c).start()

        def last_round(tail, i):
            flip = 1 - 2 * core
            gather(tail, i, 2, near_c, near_c).wait_recv()
            gather(tail, i, 5, near_x + flip, near_c).wait_recv()
            gather(tail, i, 6, near_y + flip, near_c).wait_recv()
            gather(tail, i, 7, diag + flip, near_c).wait_recv()

        def gather_sent(tail, i):
            for t, (shard, near) in enumerate(((d, near_x), (d, near_y), (d, near_c))):
                gather(tail, i, t, shard, near).wait_send()
            gather(tail, i, 3, near_x, near_y, half, 0).wait_send()
            gather(tail, i, 4, near_y, near_x, half, half).wait_send()
            gather(tail, i, 5, near_x, near_c).wait_send()
            gather(tail, i, 6, near_y, near_c).wait_send()
            gather(tail, i, 7, diag, near_c).wait_send()

        def of_layer(ref):
            whole = ref[...].astype(F32)
            row = whole[0:1]
            for i in range(1, whole.shape[0]):
                row = jnp.where(layer == i, whole[i : i + 1], row)
            return row

        mine_v = r.vec_all.at[d]
        pair = jnp.concatenate([r.gain_w[layer], r.offset_w[layer]], axis=0).astype(F32)
        mine_v[3:4, :part] = of_layer(r.down_b)
        mine_v[4:5, :part] = jnp.where(is_attn, pair[0:1], pair[1:2])
        mine_v[5:6, :part] = jnp.where(is_attn, pair[2:3], pair[3:4])

        @pl.when(is_attn)
        def _():
            for i in range(3):
                mine_v[i : i + 1, :part] = of_layer(r.attn_b.at[i])

        @pl.when(is_feed)
        def _():
            row = of_layer(r.in_b)
            for i in range(3):
                mine_v[i : i + 1, :] = row[:, i * 128 : (i + 1) * 128]

        def vec_copy(t, source):
            return to_near(
                mine_v, r.vec_all.at[source], r.v_send.at[t - 1], r.v_recv.at[t - 1], peer(t)
            )

        for t in range(1, 8):
            vec_copy(t, d).start()
        over_units(first_round)

        @pl.when(is_attn)
        def _():
            spots()

        for t in range(1, 8):
            vec_copy(t, peer(t)).wait_recv()
        for dest in range(8):
            row = r.vec_all[dest]
            at = dest * part

            @pl.when(is_attn)
            def _(row=row, at=at):
                for i in range(3):
                    vec[0:1, i * width + at : i * width + at + part] = row[i : i + 1, :part]

            @pl.when(is_feed)
            def _(row=row, dest=dest):
                for i in range(3):
                    lane_at = dest * 4 * part + i * 128
                    vec[0:1, lane_at : lane_at + 128] = row[i : i + 1, :]

            for i in range(3):
                vec[1:2, i * width + at : i * width + at + part] = row[3 + i : 4 + i, :part]

        over_units(second_round)
        over_units(third_round)
        over_units(last_round)
    else:
        whole = pltpu.make_async_copy(r.w_in, w, r.own_sem)
        whole.start()
        vec[...] = r.vec_in[...]
        spots()
        whole.wait()

    def norm_out(m, c, summed, gain, offset, size=rows):
        span = span_of(c, size)
        mean = jnp.mean(summed, axis=1, keepdims=True)
        center = summed - mean
        spread = jnp.mean(center * center, axis=1, keepdims=True)
        inv = lax.rsqrt(spread + EPSILON)
        z = center * inv
        zed[m, span] = z
        rstd[m, span] = jnp.broadcast_to(inv, (size, 128))
        h_out[m, span] = (z * gain + offset).astype(BF)
        for i in range(size // rows):
            send_h(m, c * (size // rows) + i)

    def norm_back(m, c, gain, bias_at, size=rows):
        span = span_of(c, size)
        g = g_in[m, span].astype(F32)
        z = zed[m, span]
        inv = rstd[m, span][:, :1]
        u = g * gain
        mean_u = jnp.mean(u, axis=1, keepdims=True)
        mean_uz = jnp.mean(u * z, axis=1, keepdims=True)
        grad = (u - mean_u - z * mean_uz) * inv
        low = grad.astype(BF)
        db[m, span] = low
        colsum[1:2, width : 2 * width] += jnp.sum(g * z, axis=0, keepdims=True)
        colsum[1:2, 2 * width : 3 * width] += jnp.sum(g, axis=0, keepdims=True)
        at = bias_at
        colsum[at[0] : at[0] + 1, at[1] : at[1] + width] += jnp.sum(
            low.astype(F32), axis=0, keepdims=True
        )
        return grad, low

    colsum[...] = jnp.zeros_like(colsum)
    gain = vec[1:2, width : 2 * width]
    offset = vec[1:2, 2 * width : 3 * width]

    @pl.when(is_attn)
    def _():
        lane = lax.broadcasted_iota(jnp.int32, (1, PAIR), 1) < HEAD_DIM
        lane2 = lax.broadcasted_iota(jnp.int32, (1, 2 * PAIR), 1) % PAIR < HEAD_DIM

        def places(idx, _):
            m, c = idx // bigs, idx % bigs
            span = span_of(c, big)
            qkvp[m, span, 3 * width :] = dot_nn(place[m, span], block_of(3)).astype(BF)
            return 0

        lax.fori_loop(0, micro * bigs, places, 0)

        def forward(m, _):
            def project(c, _):
                span = span_of(c, big)
                wait_h(m, 2 * c)
                wait_h(m, 2 * c + 1)
                h = h_in[m, span]
                q = dot_nn(h, block_of(0)) + vec[0:1, :width]
                qkvp[m, span, :width] = q.astype(BF)
                k = dot_nn(h, block_of(1)).astype(BF)
                qkvp[m, span, width : 2 * width] = k
                kplus[m, span] = (
                    k.astype(F32) + qkvp[m, span, 3 * width :].astype(F32)
                ).astype(BF)
                v = dot_nn(h, block_of(2)) + vec[0:1, width : 2 * width]
                qkvp[m, span, 2 * width : 3 * width] = v.astype(BF)
                return 0

            lax.fori_loop(0, bigs, project, 0)

            def attend(c, _):
                span = span_of(c, big)

                def heads(t, _):
                    off = pl.multiple_of(t * PAIR, PAIR)
                    left = jnp.concatenate(
                        [
                            qkvp[m, span, pl.ds(off, PAIR)],
                            qkvp[m, span, pl.ds(off + 3 * width, PAIR)],
                        ],
                        axis=1,
                    )
                    right = jnp.concatenate(
                        [kplus[m, :, pl.ds(off, PAIR)], qkvp[m, :, pl.ds(off + width, PAIR)]],
                        axis=1,
                    )
                    v = qkvp[m, :, pl.ds(off + 2 * width, PAIR)]
                    bias = hide[m, span].astype(F32)
                    mixed = []
                    for side in range(2):
                        mask = lane2 if side == 0 else jnp.logical_not(lane2)
                        masked = jnp.where(mask, left, jnp.zeros_like(left))
                        score = dot_nt(masked, right) * (SCORE_SCALE * LOG2E) + bias
                        top = jnp.max(score, axis=1, keepdims=True)
                        power = jnp.exp2(score - top)
                        total = jnp.sum(power, axis=1, keepdims=True)
                        prob = (power * (1.0 / total)).astype(BF)
                        at = pl.multiple_of((2 * t + side) * length, length)
                        saved[m, span, pl.ds(at, length)] = prob
                        mixed.append(dot_nn(prob, v))
                    context[m, span, pl.ds(off, PAIR)] = jnp.where(
                        lane, mixed[0], mixed[1]
                    ).astype(BF)
                    return 0

                lax.fori_loop(0, pairs, heads, 0)
                branch = dot_nn(context[m, span], block_of(4))
                summed = h_in[m, span].astype(F32) + branch + vec[0:1, 2 * width : 3 * width]
                norm_out(m, c, summed, gain, offset, big)
                return 0

            lax.fori_loop(0, bigs, attend, 0)
            return 0

        lax.fori_loop(0, micro, forward, 0)

        def backward(m, _):
            def enter(c, _):
                span = span_of(c, big)
                wait_g(m, 2 * c)
                wait_g(m, 2 * c + 1)
                grad, low = norm_back(m, c, gain, (0, 2 * width), big)
                zed[m, span] = grad
                g_in[m, span] = dot_nt(low, block_of(4)).astype(BF)
                return 0

            lax.fori_loop(0, bigs, enter, 0)

            def heads(t, _):
                off = pl.multiple_of(t * PAIR, PAIR)
                left = jnp.concatenate(
                    [qkvp[m, :, pl.ds(off, PAIR)], qkvp[m, :, pl.ds(off + 3 * width, PAIR)]],
                    axis=1,
                )
                right = jnp.concatenate(
                    [kplus[m, :, pl.ds(off, PAIR)], qkvp[m, :, pl.ds(off + width, PAIR)]],
                    axis=1,
                )
                v = qkvp[m, :, pl.ds(off + 2 * width, PAIR)]
                grad_c = g_in[m, :, pl.ds(off, PAIR)]
                got = []
                for side in range(2):
                    mask = lane if side == 0 else jnp.logical_not(lane)
                    at = pl.multiple_of((2 * t + side) * length, length)
                    prob = saved[m, :, pl.ds(at, length)]
                    wide_p = prob.astype(F32)
                    grad_p = dot_nt(jnp.where(mask, grad_c, jnp.zeros_like(grad_c)), v)
                    dot_row = jnp.sum(wide_p * grad_p, axis=1, keepdims=True)
                    grad_s = (wide_p * (grad_p - dot_row)).astype(BF)
                    got.append(
                        (dot_tn(prob, grad_c), dot_nn(grad_s, right), dot_tn(grad_s, left))
                    )
                grad_v = jnp.where(lane, got[0][0], got[1][0]).astype(BF)
                grad_l = jnp.where(lane2, got[0][1], got[1][1])
                grad_r = jnp.where(lane2, got[0][2], got[1][2])
                grad_q = (grad_l[:, :PAIR] * SCORE_SCALE).astype(BF)
                grad_k = ((grad_r[:, :PAIR] + grad_r[:, PAIR:]) * SCORE_SCALE).astype(BF)
                grad_pl = ((grad_l[:, PAIR:] + grad_r[:, :PAIR]) * SCORE_SCALE).astype(BF)
                qkvp[m, :, pl.ds(off, PAIR)] = grad_q
                qkvp[m, :, pl.ds(off + width, PAIR)] = grad_k
                qkvp[m, :, pl.ds(off + 2 * width, PAIR)] = grad_v
                qkvp[m, :, pl.ds(off + 3 * width, PAIR)] = grad_pl
                colsum[0:1, pl.ds(off, PAIR)] += jnp.sum(
                    grad_q.astype(F32), axis=0, keepdims=True
                )
                colsum[0:1, pl.ds(off + width, PAIR)] += jnp.sum(
                    grad_v.astype(F32), axis=0, keepdims=True
                )
                return 0

            lax.fori_loop(0, pairs, heads, 0)

            def leave(c, _):
                span = span_of(c, big)
                total = zed[m, span]
                for i in range(3):
                    total = total + dot_nt(
                        qkvp[m, span, i * width : (i + 1) * width], block_of(i)
                    )
                g_out[m, span] = total.astype(BF)
                send_g(m, 2 * c)
                send_g(m, 2 * c + 1)
                return 0

            lax.fori_loop(0, bigs, leave, 0)
            return 0

        lax.fori_loop(0, micro, backward, 0)

    @pl.when(is_feed)
    def _():
        def forward(idx, _):
            m, c = idx // chunks, idx % chunks
            span = span_of(c)
            wait_h(m, c)
            h = h_in[m, span]
            summed = h.astype(F32) + vec[1:2, :width]
            for f in range(blocks):
                at = f * width
                inner = dot_nn(h, block_of(f)) + vec[0:1, at : at + width]
                value, slope = gelu_and_slope(inner)
                low = value.astype(BF)
                saved[m, span, at : at + width] = low
                saved[m, span, hidden + at : hidden + at + width] = slope.astype(BF)
                summed = summed + dot_nn(low, block_of(blocks + f))
            norm_out(m, c, summed, gain, offset)
            return 0

        lax.fori_loop(0, micro * chunks, forward, 0)

        def backward(idx, _):
            m, c = idx // chunks, idx % chunks
            span = span_of(c)
            wait_g(m, c)
            total, low = norm_back(m, c, gain, (1, 0))
            for f in range(blocks):
                at = f * width
                grad_a = dot_nt(low, block_of(blocks + f)).astype(BF).astype(F32)
                slope = saved[m, span, hidden + at : hidden + at + width].astype(F32)
                grad_i = (grad_a * slope).astype(BF)
                saved[m, span, hidden + at : hidden + at + width] = grad_i
                colsum[0:1, at : at + width] += jnp.sum(
                    grad_i.astype(F32), axis=0, keepdims=True
                )
                total = total + dot_nt(grad_i, block_of(f))
            g_out[m, span] = total.astype(BF)
            send_g(m, c)
            return 0

        lax.fori_loop(0, micro * chunks, backward, 0)

    tokens = micro * length
    stage = r.stage

    def tall(ref, at):
        return ref[:, :, pl.ds(at, width)].reshape(tokens, width)

    if fused:
        table = r.table
        low_half, high_half = pl.ds(0, half), pl.ds(half, half)

        def add(target, other):
            return (target.astype(F32) + other.astype(F32)).astype(BF)

        def give(e, by_chip):
            slot = e % 2
            return to_near(
                stage.at[slot],
                table.at[pl.ds(4, 4), e - 4] if by_chip else table.at[e],
                r.p0_send.at[slot],
                r.p0_recv.at[e],
                near_c,
            )

        def emit(e, value, by_chip):
            slot = e % 2

            @pl.when(e >= 2)
            def _():
                give(e, by_chip).wait_send()

            low = value.astype(BF)
            if by_chip:
                sides = [low[: 4 * part].reshape(4, part, width), low[4 * part :].reshape(4, part, width)]
            else:
                grid = low.reshape(4, 2, part, width)
                sides = [grid[:, 0], grid[:, 1]]
            stage[slot] = jnp.where(core == 0, sides[1], sides[0])
            give(e, by_chip).start()
            kept = jnp.where(core == 0, sides[0], sides[1])
            if by_chip:
                for j in range(4):
                    at = pl.multiple_of(((4 + j) * 4 + e - 4) * part, part)
                    w[pl.ds(at, part), :] = kept[j]
            else:
                at = pl.multiple_of(e * 4 * part, 4 * part)
                w[pl.ds(at, 4 * part), :] = kept.reshape(4 * part, width)

        def finish(count, by_chip):
            give(count - 2, by_chip).wait_send()
            give(count - 1, by_chip).wait_send()

        def one_x(u, y):
            return to_near(
                table.at[u, 2 * y + 1 - cx, low_half],
                r.land_x.at[u, y],
                r.p1x_send.at[u, y],
                r.p1x_recv.at[u, y],
                near_x,
            )

        def one_y(u):
            return to_near(
                table.at[u, pl.ds(2 - 2 * cy, 2), high_half],
                r.land_y.at[u],
                r.p1y_send.at[u],
                r.p1y_recv.at[u],
                near_y,
            )

        def two_y(u):
            return to_near(
                table.at[u, 2 - 2 * cy + cx, low_half],
                r.land_y2.at[u],
                r.p2y_send.at[u],
                r.p2y_recv.at[u],
                near_y,
            )

        def two_x(u):
            return to_near(
                table.at[u, 2 * cy + 1 - cx, high_half],
                r.land_x2.at[u],
                r.p2x_send.at[u],
                r.p2x_recv.at[u],
                near_x,
            )

        def left_own(u):
            return to_section(
                table.at[u, chip],
                r.all_w.at[s, u],
                r.left_send.at[s, u],
                r.all_recv.at[s, u],
                (s - 1 + sections) % sections,
            )

        def left_on(t, u):
            return to_section(
                r.all_w.at[t, u],
                r.all_w.at[t, u],
                r.left_send.at[t, u],
                r.all_recv.at[t, u],
                (s - 1 + sections) % sections,
            )

        def right_own(u):
            return to_section(
                table.at[u, chip],
                r.all_w.at[s, u],
                r.right_send.at[s, u],
                r.all_recv.at[s, u],
                (s + 1) % sections,
            )

        def right_on(t, u):
            return to_section(
                r.all_w.at[t, u],
                r.all_w.at[t, u],
                r.right_send.at[t, u],
                r.all_recv.at[t, u],
                (s + 1) % sections,
            )

        def mine(u):
            return pltpu.make_async_copy(table.at[u, chip], r.all_w.at[s, u], r.own_sem.at[u])

        def merge_core(u):
            @pl.when(u <= 4)
            def _():
                give(u, False).wait_recv()

            @pl.when(jnp.logical_and(u == 4, is_feed))
            def _():
                for e in range(5, 8):
                    give(e, True).wait_recv()

            at = pl.multiple_of(u * 4 * part, 4 * part)
            table[u] = add(table[u], w[pl.ds(at, 4 * part), :].reshape(4, part, width))
            for y in range(2):
                one_x(u, y).start()
            one_y(u).start()

        def merge_one(u):
            for y in range(2):
                one_x(u, y).wait_recv()
                at = 2 * y + cx
                table[u, at, :half] = add(table[u, at, :half], r.land_x[u, y])
            two_y(u).start()
            one_y(u).wait_recv()
            for x in range(2):
                at = 2 * cy + x
                table[u, at, half:] = add(table[u, at, half:], r.land_y[u, x])
            two_x(u).start()

        def merge_two(u):
            two_y(u).wait_recv()
            table[u, chip, :half] = add(table[u, chip, :half], r.land_y2[u])
            two_x(u).wait_recv()
            table[u, chip, half:] = add(table[u, chip, half:], r.land_x2[u])

            @pl.when(s != last)
            def _():
                right_own(u).start()

            @pl.when(s != 0)
            def _():
                left_own(u).start()

            mine(u).start()

        late = 3 * kind

        def at_step(q, merge):
            @pl.when(jnp.logical_and(q >= 0, q < 4))
            def _():
                merge(q)

            @pl.when(jnp.logical_and(q >= 4 + late, q < units + late))
            def _():
                merge(q - late)

        def advance(q):
            at_step(q, merge_core)
            at_step(q - 2, merge_one)
            at_step(q - 4, merge_two)

        beyond = last - s
        hand_on = jnp.where(s > 0, 13 * (beyond // 2) + 8 * (beyond % 2), 0)

        def relay_left(k):
            @pl.when(jnp.logical_and(k >= 0, k < hand_on))
            def _():
                odd = (k % 13) // 8
                t = last - 2 * (k // 13) - odd
                copy = left_on(t, k % 13 - 8 * odd)
                copy.wait_recv()
                copy.start()

        sm = r.small
        for dest in range(8):
            at = dest * part

            @pl.when(is_attn)
            def _(dest=dest, at=at):
                for i in range(3):
                    sm[dest, i : i + 1, :part] = colsum[
                        0:1, i * width + at : i * width + at + part
                    ]

            @pl.when(is_feed)
            def _(dest=dest):
                for i in range(3):
                    lane_at = dest * 4 * part + i * 128
                    sm[dest, i : i + 1, :] = colsum[0:1, lane_at : lane_at + 128]

            for i in range(3):
                sm[dest, 3 + i : 4 + i, :part] = colsum[
                    1:2, i * width + at : i * width + at + part
                ]

        def small_copy(t):
            return to_near(
                sm.at[peer(t)], r.small_in.at[t - 1], r.s_send.at[t - 1], r.s_recv.at[t - 1], peer(t)
            )

        def small_share(by):
            return to_section(
                r.small_sum,
                r.all_s.at[s],
                r.sz_send.at[by - 1],
                r.sz_recv.at[s],
                (s + by) % sections,
            )

        for t in range(1, 8):
            small_copy(t).start()
        over_units(gather_sent)
        for t in range(1, 8):
            vec_copy(t, d).wait_send()
    else:

        def flush(slot, at):
            return pltpu.make_async_copy(
                stage.at[slot], r.dw_o.at[pl.ds(at, width)], r.keep_sem.at[slot]
            )

        def emit(e, value, by_chip):
            slot = e % 2

            @pl.when(e >= 2)
            def _():
                flush(slot, 0).wait()

            stage[slot] = value.astype(BF)
            flush(slot, pl.multiple_of(e * width, width)).start()

        def finish(count, by_chip):
            flush(0, 0).wait()
            flush(1, 0).wait()

        def advance(u):
            pass

        def relay_left(k):
            pass

    @pl.when(is_attn)
    def _():
        def step(e, _):
            at = pl.multiple_of(e * width, width)
            emit(e, dot_tn(tall(h_in, 0), tall(qkvp, at)), False)
            advance(e - 1)
            return 0

        lax.fori_loop(0, 3, step, 0)
        emit(3, dot_tn(tall(place, 0), tall(qkvp, 3 * width)), False)
        advance(jnp.int32(2))
        emit(4, dot_tn(tall(context, 0), tall(db, 0)), False)
        advance(jnp.int32(3))
        finish(5, False)

    @pl.when(is_feed)
    def _():
        def step(e, _):
            at = pl.multiple_of(e * width + hidden, width)
            emit(e, dot_tn(tall(h_in, 0), tall(saved, at)), False)
            advance(e - 1)
            relay_left(e - 2)
            return 0

        lax.fori_loop(0, blocks, step, 0)

        def step_b(i, _):
            at = pl.multiple_of(i * width, width)
            emit(i + blocks, dot_tn(tall(saved, at), tall(db, 0)), True)
            advance(i + blocks - 1)
            relay_left(i + blocks - 2)
            return 0

        lax.fori_loop(0, blocks, step_b, 0)
        finish(2 * blocks, True)

    if not fused:
        r.small_o[...] = colsum[...]

        @pl.when(s == last)
        def _():
            for j in range(sections - 1):
                share(h_out, r.fin_in, r.fin_send, r.fin_recv, micro - 1, j).start()
    else:

        def go_on(q, _):
            advance(q)
            relay_left(kind * (q - 1) + (1 - kind) * (2 * q - 8))
            relay_left((1 - kind) * (2 * q - 7) - kind)
            return 0

        for t in range(1, 8):
            small_copy(t).wait_recv()
        total = sm[d]
        for t in range(7):
            total = total + r.small_in[t]
        r.small_sum[...] = total
        for by in range(1, sections):
            small_share(by).start()
        lax.fori_loop(4 + late, units + late + 4, go_on, 0)

        def rest_left(k, _):
            relay_left(k)
            return 0

        lax.fori_loop(10 + 4 * kind, hand_on, rest_left, 0)

        @pl.when(s == last)
        def _():
            for j in range(sections - 1):
                share(h_out, r.fin_in, r.fin_send, r.fin_recv, micro - 1, j).start()


        for by in range(1, sections):

            @pl.when(s >= by)
            def _(by=by):
                t = s - by

                def relay(u, _):
                    right_on(t, u).wait_recv()

                    @pl.when(s != last)
                    def _():
                        right_on(t, u).start()

                    return 0

                lax.fori_loop(0, 5 + 3 * (t % 2), relay, 0)

        for by in range(1, sections):

            @pl.when(jnp.logical_and(s + by < sections, s == 0))
            def _(by=by):
                t = s + by

                def arrive(u, _):
                    left_on(t, u).wait_recv()
                    return 0

                lax.fori_loop(0, 5 + 3 * (t % 2), arrive, 0)

        for by in range(1, sections):
            t = (s + by) % sections
            to_section(
                r.small_sum, r.all_s.at[t], r.sz_send.at[by - 1], r.sz_recv.at[t], t
            ).wait_recv()
        r.all_s[s] = r.small_sum[...]

        for t in range(1, 8):
            small_copy(t).wait_send()
        for by in range(1, sections):
            small_share(by).wait_send()

        def sent(u, _):
            for y in range(2):
                one_x(u, y).wait_send()
            one_y(u).wait_send()
            two_y(u).wait_send()
            two_x(u).wait_send()
            mine(u).wait()

            @pl.when(s != last)
            def _():
                right_own(u).wait_send()

            @pl.when(s != 0)
            def _():
                left_own(u).wait_send()

            return 0

        lax.fori_loop(0, units, sent, 0)
        for by in range(1, sections):

            @pl.when(jnp.logical_and(s >= by, s != last))
            def _(by=by):
                t = s - by

                def relayed(u, _):
                    right_on(t, u).wait_send()
                    return 0

                lax.fori_loop(0, 5 + 3 * (t % 2), relayed, 0)

        for by in range(1, sections):

            @pl.when(jnp.logical_and(s + by < sections, s != 0))
            def _(by=by):
                t = s + by

                def relayed(u, _):
                    left_on(t, u).wait_send()
                    return 0

                lax.fori_loop(0, 5 + 3 * (t % 2), relayed, 0)

    for m in range(micro):
        for c in range(chunks):

            @pl.when(s != last)
            def _():
                hop(h_out, h_in, r.fsend, r.frecv, m, c, 1).wait_send()

            @pl.when(s != 0)
            def _():
                hop(g_out, g_in, r.bsend, r.brecv, m, c, -1).wait_send()

    @pl.when(s == last)
    def _():
        for m in range(micro):
            for j in range(sections - 1):
                share(h_out, r.fin_in, r.fin_send, r.fin_recv, m, j).wait_send()
            r.final_o[m] = h_out[m, (sections - 1) * quarter :]

    @pl.when(s != last)
    def _():
        for m in range(micro):
            share(h_out, r.fin_in, r.fin_send, r.fin_recv, m, 0).wait_recv()
            r.final_o[m] = r.fin_in[m]

    @pl.when(s == 0)
    def _():
        for m in range(micro):
            for j in range(1, sections):
                share(g_out, r.ig_in, r.ig_send, r.ig_recv, m, j).wait_send()
            r.igrad_o[m] = g_out[m, :quarter].astype(F32)

    @pl.when(s != 0)
    def _():
        for m in range(micro):
            share(g_out, r.ig_in, r.ig_send, r.ig_recv, m, 1).wait_recv()
            r.igrad_o[m] = r.ig_in[m].astype(F32)


def pipeline(fused, hidden, inputs):
    micro, length, width = inputs["pages"].shape
    sections = lax.axis_size("section")
    rows = length // sections
    chunks = length // rows
    quarter = length // sections
    heads = width // HEAD_DIM
    wide = max(2 * hidden, heads * length)
    part = width // 8
    half = part // 2
    hbm = pl.BlockSpec(memory_space=pl.ANY)
    vmem = pl.BlockSpec(memory_space=pltpu.VMEM)
    act = (micro, length, width)
    dma = pltpu.SemaphoreType.DMA
    spec = {name: hbm for name in inputs}
    for name in spec:
        if name not in ("pages", "cot", "w_in", "qkv_w", "pos_w", "out_w", "in_w", "down_w"):
            spec[name] = vmem
    outs = {
        "final_o": (vmem, (micro, quarter, width), BF),
        "igrad_o": (vmem, (micro, quarter, width), F32),
    }
    scratch = {
        "place": pltpu.VMEM(act, BF),
        "hide": pltpu.VMEM((micro, length, length), BF),
        "h_in": pltpu.VMEM(act, BF),
        "g_in": pltpu.VMEM(act, BF),
        "h_out": pltpu.VMEM(act, BF),
        "g_out": pltpu.VMEM(act, BF),
        "saved": pltpu.VMEM((micro, length, wide), BF),
        "qkvp": pltpu.VMEM((micro, length, 4 * width), BF),
        "kplus": pltpu.VMEM(act, BF),
        "context": pltpu.VMEM(act, BF),
        "zed": pltpu.VMEM(act, F32),
        "rstd": pltpu.VMEM((micro, length, 128), F32),
        "db": pltpu.VMEM(act, BF),
        "w": pltpu.VMEM((2 * hidden, width), BF),
        "vec": pltpu.VMEM((8, hidden), F32),
        "colsum": pltpu.VMEM((8, hidden), F32),
        "fin_in": pltpu.VMEM((micro, quarter, width), BF),
        "ig_in": pltpu.VMEM((micro, quarter, width), BF),
        "fsend": dma((micro, chunks)),
        "frecv": dma((micro, chunks)),
        "bsend": dma((micro, chunks)),
        "brecv": dma((micro, chunks)),
        "fin_send": dma((micro, sections)),
        "fin_recv": dma((micro,)),
        "ig_send": dma((micro, sections)),
        "ig_recv": dma((micro,)),
        "keep_sem": dma((2,)),
    }
    if fused:
        outs["all_w"] = (hbm, (sections, 8, part, width), BF)
        outs["all_s"] = (vmem, (sections, 8, 128), F32)
        scratch.update(
            stage=pltpu.VMEM((2, 4, part, width), BF),
            vec_all=pltpu.VMEM((8, 8, 128), F32),
            small=pltpu.VMEM((8, 8, 128), F32),
            small_in=pltpu.VMEM((7, 8, 128), F32),
            small_sum=pltpu.VMEM((8, 128), F32),
            table=pltpu.VMEM((8, 4, part, width), BF),
            land_x=pltpu.VMEM((8, 2, half, width), BF),
            land_y=pltpu.VMEM((8, 2, half, width), BF),
            land_x2=pltpu.VMEM((8, half, width), BF),
            land_y2=pltpu.VMEM((8, half, width), BF),
            own_sem=dma((8,)),
            ag_send=dma((8, 8)),
            ag_recv=dma((8, 8)),
            v_send=dma((7,)),
            v_recv=dma((7,)),
            s_send=dma((7,)),
            s_recv=dma((7,)),
            sz_send=dma((sections - 1,)),
            sz_recv=dma((sections,)),
            p0_send=dma((2,)),
            p0_recv=dma((8,)),
            p1x_send=dma((8, 2)),
            p1x_recv=dma((8, 2)),
            p1y_send=dma((8,)),
            p1y_recv=dma((8,)),
            p2x_send=dma((8,)),
            p2x_recv=dma((8,)),
            p2y_send=dma((8,)),
            p2y_recv=dma((8,)),
            left_send=dma((sections, 8)),
            right_send=dma((sections, 8)),
            all_recv=dma((sections, 8)),
        )
    else:
        outs["dw_o"] = (hbm, (2 * hidden, width), BF)
        outs["small_o"] = (vmem, (8, hidden), F32)
        scratch.update(stage=pltpu.VMEM((2, width, width), BF), own_sem=dma)
    names = [*inputs, *outs, *scratch]
    got = pl.pallas_call(
        partial(pipeline_kernel, names, rows, fused),
        out_shape=tuple(jax.ShapeDtypeStruct(shape, kind) for _, shape, kind in outs.values()),
        in_specs=list(spec.values()),
        out_specs=tuple(where for where, _, _ in outs.values()),
        scratch_shapes=list(scratch.values()),
        compiler_params=pltpu.CompilerParams(
            collective_id=0, has_side_effects=True, vmem_limit_bytes=63 * 1024 * 1024
        ),
        name="pipeline",
    )(*inputs.values())
    return dict(zip(outs, got, strict=True))


def shards(
    pages_in,
    coords,
    boxes,
    qkv_weight,
    attn_bias,
    pos_weight,
    out_weight,
    ffn_in,
    ffn_in_bias,
    ffn_out,
    ffn_out_bias,
    ln_gain,
    ln_bias,
    cotangent,
):
    groups = lax.axis_size("dp")
    s = lax.axis_index("section")
    layer = s // 2
    is_attn = s % 2 == 0
    micro, length, width = pages_in.shape
    hidden = ffn_in.shape[2]
    part = width // groups
    part_h = hidden // groups

    def pick(array):
        return lax.dynamic_index_in_dim(array, layer, 0, keepdims=False)

    inputs = {
        "pages": pages_in,
        "cot": cotangent,
        "coords": coords,
        "boxes": boxes.transpose(0, 2, 1),
        "waves": turns_per_unit(width),
    }
    if groups == 8:
        inputs.update(
            qkv_w=qkv_weight,
            pos_w=pos_weight,
            out_w=out_weight,
            in_w=ffn_in,
            down_w=ffn_out,
            attn_b=attn_bias.transpose(1, 0, 2),
            in_b=ffn_in_bias,
            down_b=ffn_out_bias,
            gain_w=ln_gain,
            offset_w=ln_bias,
        )
        got = pipeline(True, hidden, inputs)
        sections = lax.axis_size("section")
        shares, sums = got["all_w"], got["all_s"]
        attn, feed = shares[0::2], shares[1::2]
        layers = sections // 2

        def side_by_side(blocks):
            return blocks.transpose(0, 2, 1, 3).reshape(layers, part, -1).astype(F32)

        rest = sums[:, 3:6, :part].reshape(layers, 2, 3, part)
        return (
            got["final_o"],
            got["igrad_o"],
            side_by_side(attn[:, :3]),
            sums[0::2, :3, :part],
            attn[:, 3].astype(F32),
            attn[:, 4].astype(F32),
            side_by_side(feed[:, :4]),
            sums[1::2, :3].reshape(layers, part_h),
            feed[:, 4:].reshape(layers, part_h, width).astype(F32),
            rest[:, 1, 0],
            rest[:, :, 1],
            rest[:, :, 2],
        )

    norm_row = s % 2
    gain_own = lax.dynamic_index_in_dim(pick(ln_gain), norm_row, 0, keepdims=False)
    offset_own = lax.dynamic_index_in_dim(pick(ln_bias), norm_row, 0, keepdims=False)
    own_a = jnp.where(
        is_attn, jnp.concatenate([pick(qkv_weight), pick(pos_weight)], axis=1), pick(ffn_in)
    )
    own_b = jnp.where(
        is_attn, jnp.pad(pick(out_weight), ((0, part_h - part), (0, 0))), pick(ffn_out)
    )
    wa = lax.all_gather(own_a, "dp", axis=0, tiled=True)
    wb_all = lax.all_gather(own_b, "dp", axis=0, tiled=False)
    wb = jnp.where(
        is_attn,
        jnp.pad(wb_all[:, :part].reshape(width, width), ((0, hidden - width), (0, 0))),
        wb_all.reshape(hidden, width),
    )
    bias_own = jnp.where(
        is_attn,
        jnp.pad(pick(attn_bias).reshape(-1), (0, part_h - 3 * part)),
        pick(ffn_in_bias),
    )
    vec_own = jnp.concatenate([bias_own, pick(ffn_out_bias), gain_own, offset_own])
    vec_all = lax.all_gather(vec_own, "dp", axis=0, tiled=False).astype(F32)
    first = jnp.where(
        is_attn,
        jnp.pad(
            vec_all[:, : 3 * part].reshape(groups, 3, part).transpose(1, 0, 2).reshape(-1),
            (0, hidden - 3 * width),
        ),
        vec_all[:, :part_h].reshape(-1),
    )
    rest = vec_all[:, part_h:].reshape(groups, 3, part).transpose(1, 0, 2).reshape(-1)
    inputs["vec_in"] = jnp.pad(
        jnp.stack([first, jnp.pad(rest, (0, hidden - 3 * width))]), ((0, 6), (0, 0))
    )
    wide_blocks = wa.reshape(width, hidden // width, width).transpose(1, 0, 2)
    inputs["w_in"] = jnp.concatenate([wide_blocks.reshape(hidden, width), wb], axis=0)
    got = pipeline(False, hidden, inputs)
    final, igrad, dw, small = got["final_o"], got["igrad_o"], got["dw_o"], got["small_o"]
    dwa = dw[:hidden].reshape(hidden // width, width, width).transpose(1, 0, 2)
    dwa = dwa.reshape(width, hidden)
    dwb = dw[hidden:]

    shard_a = lax.psum_scatter(dwa, "dp", scatter_dimension=0, tiled=True)
    dwb_cut = jnp.where(
        is_attn,
        jnp.pad(
            dwb[:width].reshape(groups, part, width), ((0, 0), (0, part_h - part), (0, 0))
        ),
        dwb.reshape(groups, part_h, width),
    )
    shard_b = lax.psum_scatter(dwb_cut, "dp", scatter_dimension=0, tiled=True).reshape(
        part_h, width
    )
    small_first = jnp.where(
        is_attn,
        jnp.pad(
            small[0, : 3 * width].reshape(3, groups, part).transpose(1, 0, 2).reshape(groups, -1),
            ((0, 0), (0, part_h - 3 * part)),
        ),
        small[0].reshape(groups, part_h),
    )
    small_rest = (
        small[1, : 3 * width].reshape(3, groups, part).transpose(1, 0, 2).reshape(groups, -1)
    )
    small_cut = jnp.concatenate([small_first, small_rest], axis=1)
    shard_s = lax.psum_scatter(small_cut, "dp", scatter_dimension=0, tiled=True).reshape(-1)

    all_a = lax.all_gather(shard_a, "section", axis=0, tiled=False)
    all_b = lax.all_gather(shard_b, "section", axis=0, tiled=False)
    all_s = lax.all_gather(shard_s, "section", axis=0, tiled=False)

    attn_a, feed_a = all_a[0::2], all_a[1::2]
    attn_s, feed_s = all_s[0::2], all_s[1::2]
    rest_s = all_s[:, part_h:].reshape(-1, 2, 3, part)
    return (
        final,
        igrad,
        attn_a[:, :, : 3 * width].astype(F32),
        attn_s[:, : 3 * part].reshape(-1, 3, part),
        attn_a[:, :, 3 * width :].astype(F32),
        all_b[0::2, :part].astype(F32),
        feed_a.astype(F32),
        feed_s[:, :part_h],
        all_b[1::2].astype(F32),
        feed_s[:, part_h : part_h + part],
        rest_s[:, :, 1],
        rest_s[:, :, 2],
    )


def solution(mesh):
    in_specs = (
        P("dp", None, None),
        P("dp", None, None),
        P("dp", None, None),
        P(None, "dp", None),
        P(None, None, "dp"),
        P(None, "dp", None),
        P(None, "dp", None),
        P(None, "dp", None),
        P(None, "dp"),
        P(None, "dp", None),
        P(None, "dp"),
        P(None, None, "dp"),
        P(None, None, "dp"),
        P("dp", None, None),
    )
    out_specs = (
        P("dp", "section", None),
        P("dp", "section", None),
        P(None, "dp", None),
        P(None, None, "dp"),
        P(None, "dp", None),
        P(None, "dp", None),
        P(None, "dp", None),
        P(None, "dp"),
        P(None, "dp", None),
        P(None, "dp"),
        P(None, None, "dp"),
        P(None, None, "dp"),
    )
    return jax.shard_map(shards, mesh=mesh, in_specs=in_specs, out_specs=out_specs, check_vma=False)
```

```python
from functools import partial
import math

import jax
import jax.numpy as jnp
import numpy as np
from jax import lax
from jax.experimental import pallas as pl
from jax.experimental.pallas import tpu as pltpu
from jax.sharding import PartitionSpec as P

HEAD_DIM = 64
PAIR = 2 * HEAD_DIM
EPSILON = 1e-06
NEGATIVE = -1e30
LOG2E = math.log2(math.e)
SCORE_SCALE = 1.0 / math.sqrt(3.0 * HEAD_DIM)
MESH = pl.DeviceIdType.MESH
BF = jnp.bfloat16
F32 = jnp.float32


def dot_nn(a, b):
    return jnp.dot(a, b, preferred_element_type=F32)


def dot_nt(a, b):
    return lax.dot_general(a, b, (((1,), (1,)), ((), ())), preferred_element_type=F32)


def dot_tn(a, b):
    return lax.dot_general(a, b, (((0,), (0,)), ((), ())), preferred_element_type=F32)


def gelu_and_slope(x):
    bell = jnp.exp2(x * x * (-0.5 * LOG2E))
    t = 1.0 / (1.0 + (0.3275911 / math.sqrt(2.0)) * jnp.abs(x))
    series = t * (
        0.254829592
        + t * (-0.284496736 + t * (1.421413741 + t * (-1.453152027 + t * 1.061405429)))
    )
    tail = 0.5 * series * bell
    cdf = jnp.where(x >= 0.0, 1.0 - tail, tail)
    return x * cdf, cdf + x * bell * (1.0 / math.sqrt(2.0 * math.pi))


TURN_TERMS = [
    (-1.0) ** n * (2.0 * math.pi) ** (2 * n + 1) / math.factorial(2 * n + 1) for n in range(6)
]


def sine_of_turns(turns):
    rest = turns - jnp.floor(turns + 0.5)
    size = 0.25 - jnp.abs(jnp.abs(rest) - 0.25)
    square = size * size
    series = TURN_TERMS[5]
    for term in TURN_TERMS[4::-1]:
        series = series * square + term
    return jnp.where(rest < 0.0, -size, size) * series


def turns_per_unit(width):
    quarter = width // 4
    wave = 10000.0 ** (-np.arange(quarter) / quarter) / (2.0 * math.pi)
    table = np.zeros((2, width))
    table[0, : 2 * quarter] = np.tile(wave, 2)
    table[1, 2 * quarter :] = np.tile(wave, 2)
    return jnp.asarray(table, F32)


class Refs:
    def __init__(self, names, refs):
        self.__dict__.update(zip(names, refs, strict=True))


def pipeline_kernel(names, rows, fused, *refs):
    r = Refs(names, refs)
    h_in, g_in, h_out, g_out = r.h_in, r.g_in, r.h_out, r.g_out
    saved, qkvp, kplus, context, zed, rstd = r.saved, r.qkvp, r.kplus, r.context, r.zed, r.rstd
    db, w, place, hide = r.db, r.w, r.place, r.hide
    vec, colsum = r.vec, r.colsum
    sections = lax.axis_size("section")
    s = lax.axis_index("section")
    kind = s % 2
    layer = s // 2
    last = sections - 1
    micro, length, width = h_in.shape
    hidden = w.shape[0] // 2
    chunks = length // rows
    big = 2 * rows
    bigs = length // big
    quarter = length // sections
    pairs = width // PAIR
    blocks = hidden // width
    is_attn = kind == 0
    is_feed = kind == 1

    if fused:
        d = lax.axis_index("dp")
        part = width // 8
        half = part // 2
        core, cx, cy = d % 2, (d // 2) % 2, d // 4
        chip = d // 2
        near_c = d + 1 - 2 * core
        near_x = d + 2 - 4 * cx
        near_y = d + 4 - 8 * cy
        diag = near_x + 4 - 8 * cy
        units = 5 + 3 * kind
        tail_units = 1 + 3 * kind

        def peer(t):
            tc, tx, ty = t % 2, (t // 2) % 2, t // 4
            return (
                d + tc * (1 - 2 * core) + 2 * tx * (1 - 2 * cx) + 4 * ty * (1 - 2 * cy)
            )

    barrier = pltpu.get_barrier_semaphore()
    for by in range(1, sections):
        pl.semaphore_signal(
            barrier, inc=1, device_id={"section": (s + by) % sections}, device_id_type=MESH
        )
    if fused:
        for t in range(1, 8):
            pl.semaphore_signal(barrier, inc=1, device_id={"dp": peer(t)}, device_id_type=MESH)

    def to_section(source, target, send, recv, at):
        return pltpu.make_async_remote_copy(
            src_ref=source,
            dst_ref=target,
            send_sem=send,
            recv_sem=recv,
            device_id={"section": at},
            device_id_type=MESH,
        )

    def to_near(source, target, send, recv, near):
        return pltpu.make_async_remote_copy(
            src_ref=source,
            dst_ref=target,
            send_sem=send,
            recv_sem=recv,
            device_id={"dp": near},
            device_id_type=MESH,
        )

    def span_of(c, size=rows):
        return pl.ds(pl.multiple_of(c * size, size), size)

    def local_in(source, target, sem, m, c):
        span = span_of(c)
        return pltpu.make_async_copy(source.at[m, span], target.at[m, span], sem.at[m, c])

    def hop(source, target, send, recv, m, c, by):
        span = span_of(c)
        return to_section(
            source.at[m, span],
            target.at[m, span],
            send.at[m, c],
            recv.at[m, c],
            (s + by + sections) % sections,
        )

    def share(source, target, send, recv, m, j):
        span = pl.ds(pl.multiple_of(j * quarter, quarter), quarter)
        return to_section(source.at[m, span], target.at[m], send.at[m, j], recv.at[m], j)

    @pl.when(s == 0)
    def _():
        for m in range(micro):
            for c in range(chunks):
                local_in(r.pages, h_in, r.frecv, m, c).start()

    @pl.when(s == last)
    def _():
        for m in range(micro):
            for c in range(chunks):
                local_in(r.cot, g_in, r.brecv, m, c).start()

    def wait_h(m, c):
        @pl.when(s == 0)
        def _():
            local_in(r.pages, h_in, r.frecv, m, c).wait()

        @pl.when(s != 0)
        def _():
            hop(h_out, h_in, r.fsend, r.frecv, m, c, 1).wait_recv()

    def wait_g(m, c):
        @pl.when(s == last)
        def _():
            local_in(r.cot, g_in, r.brecv, m, c).wait()

        @pl.when(s != last)
        def _():
            hop(g_out, g_in, r.bsend, r.brecv, m, c, -1).wait_recv()

    def send_h(m, c):
        @pl.when(s != last)
        def _():
            hop(h_out, h_in, r.fsend, r.frecv, m, c, 1).start()


    def send_g(m, c):
        @pl.when(s != 0)
        def _():
            hop(g_out, g_in, r.bsend, r.brecv, m, c, -1).start()

        @pl.when(jnp.logical_and(s == 0, c != s))
        def _():
            share(g_out, r.ig_in, r.ig_send, r.ig_recv, m, c).start()

    def block_of(i):
        return w[i * width : (i + 1) * width, :]

    def spots():
        columns = lax.broadcasted_iota(jnp.int32, (1, width), 1)
        phase = jnp.where((columns // (width // 4)) % 2 == 1, 0.25, 0.0)
        tokens_at = lax.broadcasted_iota(jnp.int32, (length, r.boxes.shape[2]), 0)

        def page(m, _):
            turns = lax.dot_general(
                r.coords[m].astype(F32),
                r.waves[...],
                (((0,), (0,)), ((), ())),
                precision=lax.Precision.HIGHEST,
                preferred_element_type=F32,
            )
            place[m] = sine_of_turns(turns + phase).astype(BF)
            box = r.boxes[m]

            def hit(low, high):
                inside = jnp.logical_and(
                    tokens_at >= box[low : low + 1], tokens_at < box[high : high + 1]
                )
                return jnp.where(inside, 1.0, 0.0)

            covered = dot_nt(hit(0, 1), hit(2, 3))
            hide[m] = jnp.where(covered < 0.5, 0.0, NEGATIVE).astype(BF)
            return 0

        lax.fori_loop(0, micro, page, 0)

    if fused:

        def shard_rows(tail, i, shard, count, first=0):
            if tail:
                at = hidden + shard * (part + 3 * part * kind) + i * part + first
            else:
                at = i * width + shard * part + first
            return pl.ds(pl.multiple_of(at, half), count)

        def gather(tail, i, t, shard, near, count=None, first=0):
            span = shard_rows(tail, i, shard, count or part, first)
            u = 4 + i if tail else i
            return to_near(w.at[span], w.at[span], r.ag_send.at[u, t], r.ag_recv.at[u, t], near)

        def over_units(step):
            def head(i, _):
                step(False, i)
                return 0

            def rest(i, _):
                step(True, i)
                return 0

            lax.fori_loop(0, 4, head, 0)
            lax.fori_loop(0, tail_units, rest, 0)

        def own_copy(source, tail, i):
            u = 4 + i if tail else i
            return pltpu.make_async_copy(
                source, w.at[shard_rows(tail, i, d, part)], r.own_sem.at[u]
            )

        @pl.when(is_attn)
        def _():
            for i in range(3):
                own_copy(
                    r.qkv_w.at[layer, :, pl.ds(i * width, width)], False, i
                ).start()
            own_copy(r.pos_w.at[layer], False, 3).start()
            own_copy(r.out_w.at[layer], True, 0).start()

        @pl.when(is_feed)
        def _():
            for i in range(4):
                own_copy(r.in_w.at[layer, :, pl.ds(i * width, width)], False, i).start()
            for i in range(4):
                own_copy(r.down_w.at[layer, pl.ds(i * part, part), :], True, i).start()

        def first_round(tail, i):
            own_copy(r.pos_w.at[layer], tail, i).wait()
            gather(tail, i, 0, d, near_x).start()
            gather(tail, i, 1, d, near_y).start()
            gather(tail, i, 2, d, near_c).start()

        def second_round(tail, i):
            gather(tail, i, 0, near_x, near_x).wait_recv()
            gather(tail, i, 3, near_x, near_y, half, 0).start()
            gather(tail, i, 5, near_x, near_c).start()
            gather(tail, i, 1, near_y, near_y).wait_recv()
            gather(tail, i, 4, near_y, near_x, half, half).start()
            gather(tail, i, 6, near_y, near_c).start()

        def third_round(tail, i):
            gather(tail, i, 3, diag, near_y, half, 0).wait_recv()
            gather(tail, i, 4, diag, near_x, half, half).wait_recv()
            gather(tail, i, 7, diag, near_c).start()

        def last_round(tail, i):
            flip = 1 - 2 * core
            gather(tail, i, 2, near_c, near_c).wait_recv()
            gather(tail, i, 5, near_x + flip, near_c).wait_recv()
            gather(tail, i, 6, near_y + flip, near_c).wait_recv()
            gather(tail, i, 7, diag + flip, near_c).wait_recv()

        def gather_sent(tail, i):
            for t, (shard, near) in enumerate(((d, near_x), (d, near_y), (d, near_c))):
                gather(tail, i, t, shard, near).wait_send()
            gather(tail, i, 3, near_x, near_y, half, 0).wait_send()
            gather(tail, i, 4, near_y, near_x, half, half).wait_send()
            gather(tail, i, 5, near_x, near_c).wait_send()
            gather(tail, i, 6, near_y, near_c).wait_send()
            gather(tail, i, 7, diag, near_c).wait_send()

        def of_layer(ref):
            whole = ref[...].astype(F32)
            row = whole[0:1]
            for i in range(1, whole.shape[0]):
                row = jnp.where(layer == i, whole[i : i + 1], row)
            return row

        mine_v = r.vec_all.at[d]
        pair = jnp.concatenate([r.gain_w[layer], r.offset_w[layer]], axis=0).astype(F32)
        mine_v[3:4, :part] = of_layer(r.down_b)
        mine_v[4:5, :part] = jnp.where(is_attn, pair[0:1], pair[1:2])
        mine_v[5:6, :part] = jnp.where(is_attn, pair[2:3], pair[3:4])

        @pl.when(is_attn)
        def _():
            for i in range(3):
                mine_v[i : i + 1, :part] = of_layer(r.attn_b.at[i])

        @pl.when(is_feed)
        def _():
            row = of_layer(r.in_b)
            for i in range(3):
                mine_v[i : i + 1, :] = row[:, i * 128 : (i + 1) * 128]

        def vec_copy(t, source):
            return to_near(
                mine_v, r.vec_all.at[source], r.v_send.at[t - 1], r.v_recv.at[t - 1], peer(t)
            )

        pl.semaphore_wait(barrier, sections - 1 + 7)
        for t in range(1, 8):
            vec_copy(t, d).start()
        over_units(first_round)

        @pl.when(is_attn)
        def _():
            spots()

        for t in range(1, 8):
            vec_copy(t, peer(t)).wait_recv()
        for dest in range(8):
            row = r.vec_all[dest]
            at = dest * part

            @pl.when(is_attn)
            def _(row=row, at=at):
                for i in range(3):
                    vec[0:1, i * width + at : i * width + at + part] = row[i : i + 1, :part]

            @pl.when(is_feed)
            def _(row=row, dest=dest):
                for i in range(3):
                    lane_at = dest * 4 * part + i * 128
                    vec[0:1, lane_at : lane_at + 128] = row[i : i + 1, :]

            for i in range(3):
                vec[1:2, i * width + at : i * width + at + part] = row[3 + i : 4 + i, :part]

        over_units(second_round)

        def rounds(tail, i):
            third_round(tail, i)
            last_round(tail, i)

        def over_head(step):
            def head(i, _):
                step(False, i)
                return 0

            lax.fori_loop(0, 4, head, 0)

        @pl.when(is_attn)
        def _():
            over_head(third_round)
            over_head(last_round)

        @pl.when(is_feed)
        def _():
            over_units(third_round)
            over_units(last_round)
    else:
        whole = pltpu.make_async_copy(r.w_in, w, r.own_sem)
        whole.start()
        vec[...] = r.vec_in[...]
        spots()
        pl.semaphore_wait(barrier, sections - 1)
        whole.wait()

    def norm_out(m, c, summed, gain, offset, size=rows):
        span = span_of(c, size)
        mean = jnp.mean(summed, axis=1, keepdims=True)
        center = summed - mean
        spread = jnp.mean(center * center, axis=1, keepdims=True)
        inv = lax.rsqrt(spread + EPSILON)
        z = center * inv
        zed[m, span] = z
        rstd[m, span] = jnp.broadcast_to(inv, (size, 128))
        h_out[m, span] = (z * gain + offset).astype(BF)
        for i in range(size // rows):
            send_h(m, c * (size // rows) + i)

    def norm_back(m, c, gain, bias_at, size=rows):
        span = span_of(c, size)
        g = g_in[m, span].astype(F32)
        z = zed[m, span]
        inv = rstd[m, span][:, :1]
        u = g * gain
        mean_u = jnp.mean(u, axis=1, keepdims=True)
        mean_uz = jnp.mean(u * z, axis=1, keepdims=True)
        grad = (u - mean_u - z * mean_uz) * inv
        low = grad.astype(BF)
        db[m, span] = low
        colsum[1:2, width : 2 * width] += jnp.sum(g * z, axis=0, keepdims=True)
        colsum[1:2, 2 * width : 3 * width] += jnp.sum(g, axis=0, keepdims=True)
        at = bias_at
        colsum[at[0] : at[0] + 1, at[1] : at[1] + width] += jnp.sum(
            low.astype(F32), axis=0, keepdims=True
        )
        return grad, low

    colsum[...] = jnp.zeros_like(colsum)
    gain = vec[1:2, width : 2 * width]
    offset = vec[1:2, 2 * width : 3 * width]

    @pl.when(is_attn)
    def _():
        lane = lax.broadcasted_iota(jnp.int32, (1, PAIR), 1) < HEAD_DIM
        lane2 = lax.broadcasted_iota(jnp.int32, (1, 2 * PAIR), 1) % PAIR < HEAD_DIM

        def places(idx, _):
            m, c = idx // bigs, idx % bigs
            span = span_of(c, big)
            qkvp[m, span, 3 * width :] = dot_nn(place[m, span], block_of(3)).astype(BF)
            return 0

        lax.fori_loop(0, micro * bigs, places, 0)

        def forward(m, _):
            def project(c, _):
                span = span_of(c, big)
                wait_h(m, 2 * c)
                wait_h(m, 2 * c + 1)
                h = h_in[m, span]
                q = dot_nn(h, block_of(0)) + vec[0:1, :width]
                qkvp[m, span, :width] = q.astype(BF)
                k = dot_nn(h, block_of(1)).astype(BF)
                qkvp[m, span, width : 2 * width] = k
                kplus[m, span] = (
                    k.astype(F32) + qkvp[m, span, 3 * width :].astype(F32)
                ).astype(BF)
                v = dot_nn(h, block_of(2)) + vec[0:1, width : 2 * width]
                qkvp[m, span, 2 * width : 3 * width] = v.astype(BF)
                return 0

            lax.fori_loop(0, bigs, project, 0)

            def heads(t, _):
                off = pl.multiple_of(t * PAIR, PAIR)
                left = jnp.concatenate(
                    [qkvp[m, :, pl.ds(off, PAIR)], qkvp[m, :, pl.ds(off + 3 * width, PAIR)]],
                    axis=1,
                )
                right = jnp.concatenate(
                    [kplus[m, :, pl.ds(off, PAIR)], qkvp[m, :, pl.ds(off + width, PAIR)]],
                    axis=1,
                )
                v = qkvp[m, :, pl.ds(off + 2 * width, PAIR)]
                bias = hide[m].astype(F32)
                mixed = []
                blank = jnp.zeros_like(left)
                both = jnp.concatenate(
                    [jnp.where(lane2, left, blank), jnp.where(lane2, blank, left)], axis=0
                )
                raw = dot_nt(both, right)
                for side in range(2):
                    score = raw[side * length : (side + 1) * length] * (SCORE_SCALE * LOG2E) + bias
                    top = jnp.max(score, axis=1, keepdims=True)
                    power = jnp.exp2(score - top)
                    total = jnp.sum(power, axis=1, keepdims=True)
                    prob = (power * (1.0 / total)).astype(BF)
                    at = pl.multiple_of((2 * t + side) * length, length)
                    saved[m, :, pl.ds(at, length)] = prob
                    mixed.append(dot_nn(prob, v))
                context[m, :, pl.ds(off, PAIR)] = jnp.where(lane, mixed[0], mixed[1]).astype(BF)
                return 0

            lax.fori_loop(0, pairs, heads, 0, unroll=2)

            if fused:

                @pl.when(m == 0)
                def _():
                    rounds(True, 0)

            def attend(c, _):
                span = span_of(c, big)
                branch = dot_nn(context[m, span], block_of(4))
                summed = h_in[m, span].astype(F32) + branch + vec[0:1, 2 * width : 3 * width]
                norm_out(m, c, summed, gain, offset, big)
                return 0

            lax.fori_loop(0, bigs, attend, 0)
            return 0

        lax.fori_loop(0, micro, forward, 0)

        def backward(m, _):
            def enter(c, _):
                span = span_of(c, big)
                wait_g(m, 2 * c)
                wait_g(m, 2 * c + 1)
                grad, low = norm_back(m, c, gain, (0, 2 * width), big)
                zed[m, span] = grad
                g_in[m, span] = dot_nt(low, block_of(4)).astype(BF)
                return 0

            lax.fori_loop(0, bigs, enter, 0)

            def heads(t, _):
                off = pl.multiple_of(t * PAIR, PAIR)
                left = jnp.concatenate(
                    [qkvp[m, :, pl.ds(off, PAIR)], qkvp[m, :, pl.ds(off + 3 * width, PAIR)]],
                    axis=1,
                )
                right = jnp.concatenate(
                    [kplus[m, :, pl.ds(off, PAIR)], qkvp[m, :, pl.ds(off + width, PAIR)]],
                    axis=1,
                )
                v = qkvp[m, :, pl.ds(off + 2 * width, PAIR)]
                grad_c = g_in[m, :, pl.ds(off, PAIR)]
                blank = jnp.zeros_like(grad_c)
                both = jnp.concatenate(
                    [jnp.where(lane, grad_c, blank), jnp.where(lane, blank, grad_c)], axis=0
                )
                at = pl.multiple_of(2 * t * length, 2 * length)
                prob = saved[m, :, pl.ds(at, 2 * length)]
                grad_p = dot_nt(both, v)
                grad_s = []
                for side in range(2):
                    wide_p = prob[:, side * length : (side + 1) * length].astype(F32)
                    part_p = grad_p[side * length : (side + 1) * length]
                    dot_row = jnp.sum(wide_p * part_p, axis=1, keepdims=True)
                    grad_s.append((wide_p * (part_p - dot_row)).astype(BF))
                got_v = dot_tn(prob, grad_c)
                got_l = dot_nn(jnp.concatenate(grad_s, axis=0), right)
                got_r = dot_tn(jnp.concatenate(grad_s, axis=1), left)
                grad_v = jnp.where(lane, got_v[:length], got_v[length:]).astype(BF)
                grad_l = jnp.where(lane2, got_l[:length], got_l[length:])
                grad_r = jnp.where(lane2, got_r[:length], got_r[length:])
                grad_q = (grad_l[:, :PAIR] * SCORE_SCALE).astype(BF)
                grad_k = ((grad_r[:, :PAIR] + grad_r[:, PAIR:]) * SCORE_SCALE).astype(BF)
                grad_pl = ((grad_l[:, PAIR:] + grad_r[:, :PAIR]) * SCORE_SCALE).astype(BF)
                qkvp[m, :, pl.ds(off, PAIR)] = grad_q
                qkvp[m, :, pl.ds(off + width, PAIR)] = grad_k
                qkvp[m, :, pl.ds(off + 2 * width, PAIR)] = grad_v
                qkvp[m, :, pl.ds(off + 3 * width, PAIR)] = grad_pl
                colsum[0:1, pl.ds(off, PAIR)] += jnp.sum(
                    grad_q.astype(F32), axis=0, keepdims=True
                )
                colsum[0:1, pl.ds(off + width, PAIR)] += jnp.sum(
                    grad_v.astype(F32), axis=0, keepdims=True
                )
                return 0

            lax.fori_loop(0, pairs, heads, 0, unroll=2)

            def leave(c, _):
                span = span_of(c, big)
                total = zed[m, span]
                for i in range(3):
                    total = total + dot_nt(
                        qkvp[m, span, i * width : (i + 1) * width], block_of(i)
                    )
                g_out[m, span] = total.astype(BF)
                send_g(m, 2 * c)
                send_g(m, 2 * c + 1)
                return 0

            lax.fori_loop(0, bigs, leave, 0)
            return 0

        lax.fori_loop(0, micro, backward, 0)

    @pl.when(is_feed)
    def _():
        def forward(idx, _):
            m, c = idx // chunks, idx % chunks
            span = span_of(c)
            wait_h(m, c)
            h = h_in[m, span]
            summed = h.astype(F32) + vec[1:2, :width]
            for f in range(blocks):
                at = f * width
                inner = dot_nn(h, block_of(f)) + vec[0:1, at : at + width]
                value, slope = gelu_and_slope(inner)
                low = value.astype(BF)
                saved[m, span, at : at + width] = low
                saved[m, span, hidden + at : hidden + at + width] = slope.astype(BF)
                summed = summed + dot_nn(low, block_of(blocks + f))
            norm_out(m, c, summed, gain, offset)
            return 0

        def backward(m, c, size):
            span = span_of(c, size)
            hops = size // rows
            for i in range(hops):
                wait_g(m, c * hops + i)
            total, low = norm_back(m, c, gain, (1, 0), size)
            for f in range(blocks):
                at = f * width
                grad_a = dot_nt(low, block_of(blocks + f)).astype(BF).astype(F32)
                slope = saved[m, span, hidden + at : hidden + at + width].astype(F32)
                grad_i = (grad_a * slope).astype(BF)
                saved[m, span, hidden + at : hidden + at + width] = grad_i
                colsum[0:1, at : at + width] += jnp.sum(
                    grad_i.astype(F32), axis=0, keepdims=True
                )
                total = total + dot_nt(grad_i, block_of(f))
            g_out[m, span] = total.astype(BF)
            for i in range(hops):
                send_g(m, c * hops + i)

        def step(i, _):
            page, c = i // chunks, i % chunks
            turn = jnp.where(s == last, page % 2, page // micro)
            m = jnp.where(s == last, page // 2, page % micro)

            @pl.when(turn == 0)
            def _():
                forward(m * chunks + c, 0)

            @pl.when(jnp.logical_and(turn == 1, s != last))
            def _():
                backward(m, c, rows)

            @pl.when(jnp.logical_and(jnp.logical_and(turn == 1, s == last), c % 2 == 0))
            def _():
                backward(m, c // 2, big)

            return 0

        lax.fori_loop(0, 2 * micro * chunks, step, 0)

    tokens = micro * length
    stage = r.stage

    def tall(ref, at):
        return ref[:, :, pl.ds(at, width)].reshape(tokens, width)

    if fused:
        table = r.table
        low_half, high_half = pl.ds(0, half), pl.ds(half, half)

        def add(target, other):
            return (target.astype(F32) + other.astype(F32)).astype(BF)

        def give(e, by_chip):
            slot = e % 2
            return to_near(
                stage.at[slot],
                table.at[pl.ds(4, 4), e - 4] if by_chip else table.at[e],
                r.p0_send.at[slot],
                r.p0_recv.at[e],
                near_c,
            )

        def emit(e, value, by_chip):
            slot = e % 2

            @pl.when(e >= 2)
            def _():
                give(e, by_chip).wait_send()

            low = value.astype(BF)
            if by_chip:
                sides = [low[: 4 * part].reshape(4, part, width), low[4 * part :].reshape(4, part, width)]
            else:
                grid = low.reshape(4, 2, part, width)
                sides = [grid[:, 0], grid[:, 1]]
            stage[slot] = jnp.where(core == 0, sides[1], sides[0])
            give(e, by_chip).start()
            kept = jnp.where(core == 0, sides[0], sides[1])
            if by_chip:
                for j in range(4):
                    at = pl.multiple_of(((4 + j) * 4 + e - 4) * part, part)
                    w[pl.ds(at, part), :] = kept[j]
            else:
                at = pl.multiple_of(e * 4 * part, 4 * part)
                w[pl.ds(at, 4 * part), :] = kept.reshape(4 * part, width)

        def finish(count, by_chip):
            give(count - 2, by_chip).wait_send()
            give(count - 1, by_chip).wait_send()

        def one_x(u, y):
            return to_near(
                table.at[u, 2 * y + 1 - cx, low_half],
                r.land_x.at[u, y],
                r.p1x_send.at[u, y],
                r.p1x_recv.at[u, y],
                near_x,
            )

        def one_y(u):
            return to_near(
                table.at[u, pl.ds(2 - 2 * cy, 2), high_half],
                r.land_y.at[u],
                r.p1y_send.at[u],
                r.p1y_recv.at[u],
                near_y,
            )

        def two_y(u):
            return to_near(
                table.at[u, 2 - 2 * cy + cx, low_half],
                r.land_y2.at[u],
                r.p2y_send.at[u],
                r.p2y_recv.at[u],
                near_y,
            )

        def two_x(u):
            return to_near(
                table.at[u, 2 * cy + 1 - cx, high_half],
                r.land_x2.at[u],
                r.p2x_send.at[u],
                r.p2x_recv.at[u],
                near_x,
            )

        def left_own(u):
            return to_section(
                table.at[u, chip],
                r.all_w.at[s, u],
                r.left_send.at[s, u],
                r.all_recv.at[s, u],
                (s - 1 + sections) % sections,
            )

        def left_on(t, u):
            return to_section(
                r.all_w.at[t, u],
                r.all_w.at[t, u],
                r.left_send.at[t, u],
                r.all_recv.at[t, u],
                (s - 1 + sections) % sections,
            )

        def right_own(u):
            return to_section(
                table.at[u, chip],
                r.all_w.at[s, u],
                r.right_send.at[s, u],
                r.all_recv.at[s, u],
                (s + 1) % sections,
            )

        def right_on(t, u):
            return to_section(
                r.all_w.at[t, u],
                r.all_w.at[t, u],
                r.right_send.at[t, u],
                r.all_recv.at[t, u],
                (s + 1) % sections,
            )

        def mine(u):
            return pltpu.make_async_copy(table.at[u, chip], r.all_w.at[s, u], r.own_sem.at[u])

        def merge_core(u):
            @pl.when(u <= 4)
            def _():
                give(u, False).wait_recv()

            @pl.when(jnp.logical_and(u == 4, is_feed))
            def _():
                for e in range(5, 8):
                    give(e, True).wait_recv()

            at = pl.multiple_of(u * 4 * part, 4 * part)
            table[u] = add(table[u], w[pl.ds(at, 4 * part), :].reshape(4, part, width))
            for y in range(2):
                one_x(u, y).start()
            one_y(u).start()

        def merge_one(u):
            for y in range(2):
                one_x(u, y).wait_recv()
                at = 2 * y + cx
                table[u, at, :half] = add(table[u, at, :half], r.land_x[u, y])
            two_y(u).start()
            one_y(u).wait_recv()
            for x in range(2):
                at = 2 * cy + x
                table[u, at, half:] = add(table[u, at, half:], r.land_y[u, x])
            two_x(u).start()

        def merge_two(u):
            two_y(u).wait_recv()
            table[u, chip, :half] = add(table[u, chip, :half], r.land_y2[u])
            two_x(u).wait_recv()
            table[u, chip, half:] = add(table[u, chip, half:], r.land_x2[u])

            @pl.when(s != last)
            def _():
                right_own(u).start()

            @pl.when(s == last)
            def _():
                left_own(u).start()

            mine(u).start()

        late = 3 * kind

        def at_step(q, merge):
            @pl.when(jnp.logical_and(q >= 0, q < 4))
            def _():
                merge(q)

            @pl.when(jnp.logical_and(q >= 4 + late, q < units + late))
            def _():
                merge(q - late)

        def advance(q):
            at_step(q, merge_core)
            at_step(q - 2, merge_one)
            at_step(q - 4, merge_two)

        beyond = last - s
        hand_on = jnp.where(s > 0, 13 * (beyond // 2) + 8 * (beyond % 2), 0)

        def relay_left(k):
            @pl.when(jnp.logical_and(k >= 0, k < hand_on))
            def _():
                odd = (k % 13) // 8
                t = last - 2 * (k // 13) - odd
                copy = left_on(t, k % 13 - 8 * odd)
                copy.wait_recv()
                copy.start()

        sm = r.small
        for dest in range(8):
            at = dest * part

            @pl.when(is_attn)
            def _(dest=dest, at=at):
                for i in range(3):
                    sm[dest, i : i + 1, :part] = colsum[
                        0:1, i * width + at : i * width + at + part
                    ]

            @pl.when(is_feed)
            def _(dest=dest):
                for i in range(3):
                    lane_at = dest * 4 * part + i * 128
                    sm[dest, i : i + 1, :] = colsum[0:1, lane_at : lane_at + 128]

            for i in range(3):
                sm[dest, 3 + i : 4 + i, :part] = colsum[
                    1:2, i * width + at : i * width + at + part
                ]

        def small_copy(t):
            return to_near(
                sm.at[peer(t)], r.small_in.at[t - 1], r.s_send.at[t - 1], r.s_recv.at[t - 1], peer(t)
            )

        def small_share(by):
            return to_section(
                r.small_sum,
                r.all_s.at[s],
                r.sz_send.at[by - 1],
                r.sz_recv.at[s],
                (s + by) % sections,
            )

        for t in range(1, 8):
            small_copy(t).start()
        over_units(gather_sent)
        for t in range(1, 8):
            vec_copy(t, d).wait_send()
    else:

        def flush(slot, at):
            return pltpu.make_async_copy(
                stage.at[slot], r.dw_o.at[pl.ds(at, width)], r.keep_sem.at[slot]
            )

        def emit(e, value, by_chip):
            slot = e % 2

            @pl.when(e >= 2)
            def _():
                flush(slot, 0).wait()

            stage[slot] = value.astype(BF)
            flush(slot, pl.multiple_of(e * width, width)).start()

        def finish(count, by_chip):
            flush(0, 0).wait()
            flush(1, 0).wait()

        def advance(u):
            pass

        def relay_left(k):
            pass

    @pl.when(is_attn)
    def _():
        def step(e, _):
            at = pl.multiple_of(e * width, width)
            emit(e, dot_tn(tall(h_in, 0), tall(qkvp, at)), False)
            advance(e - 1)
            return 0

        lax.fori_loop(0, 3, step, 0)
        emit(3, dot_tn(tall(place, 0), tall(qkvp, 3 * width)), False)
        advance(jnp.int32(2))
        emit(4, dot_tn(tall(context, 0), tall(db, 0)), False)
        advance(jnp.int32(3))
        finish(5, False)

    @pl.when(is_feed)
    def _():
        def step(e, _):
            at = pl.multiple_of(e * width + hidden, width)
            emit(e, dot_tn(tall(h_in, 0), tall(saved, at)), False)
            advance(e - 1)
            relay_left(e // 2 - 100 * (e % 2))
            return 0

        lax.fori_loop(0, blocks, step, 0)

        def step_b(i, _):
            at = pl.multiple_of(i * width, width)
            emit(i + blocks, dot_tn(tall(saved, at), tall(db, 0)), True)
            advance(i + blocks - 1)
            relay_left((i + blocks) // 2 - 100 * (i % 2))
            return 0

        lax.fori_loop(0, blocks, step_b, 0)
        finish(2 * blocks, True)

    if not fused:
        r.small_o[...] = colsum[...]

        @pl.when(s == last)
        def _():
            for m in range(micro):
                for j in range(sections - 1):
                    share(h_out, r.fin_in, r.fin_send, r.fin_recv, m, j).start()
    else:

        def go_on(q, _):
            advance(q)
            relay_left(q - 4 + kind)
            return 0

        for t in range(1, 8):
            small_copy(t).wait_recv()
        total = sm[d]
        for t in range(7):
            total = total + r.small_in[t]
        r.small_sum[...] = total
        for by in range(1, sections):
            small_share(by).start()
        lax.fori_loop(4 + late, units + late + 4, go_on, 0)

        def rest_left(k, _):
            relay_left(k)
            return 0

        lax.fori_loop(5 + 7 * kind, hand_on, rest_left, 0)

        @pl.when(jnp.logical_and(s > 0, s < last))
        def _():
            def own_left(u, _):
                left_own(u).start()
                return 0

            lax.fori_loop(0, units, own_left, 0)


        @pl.when(s == last)
        def _():
            for m in range(micro):
                for j in range(sections - 1):
                    share(h_out, r.fin_in, r.fin_send, r.fin_recv, m, j).start()


        for by in range(1, sections):

            @pl.when(s >= by)
            def _(by=by):
                t = s - by

                def relay(u, _):
                    right_on(t, u).wait_recv()

                    @pl.when(s != last)
                    def _():
                        right_on(t, u).start()

                    return 0

                lax.fori_loop(0, 5 + 3 * (t % 2), relay, 0)

        for by in range(1, sections):

            @pl.when(jnp.logical_and(s + by < sections, s == 0))
            def _(by=by):
                t = s + by

                def arrive(u, _):
                    left_on(t, u).wait_recv()
                    return 0

                lax.fori_loop(0, 5 + 3 * (t % 2), arrive, 0)

        for by in range(1, sections):
            t = (s + by) % sections
            to_section(
                r.small_sum, r.all_s.at[t], r.sz_send.at[by - 1], r.sz_recv.at[t], t
            ).wait_recv()
        r.all_s[s] = r.small_sum[...]

        for t in range(1, 8):
            small_copy(t).wait_send()
        for by in range(1, sections):
            small_share(by).wait_send()

        def sent(u, _):
            for y in range(2):
                one_x(u, y).wait_send()
            one_y(u).wait_send()
            two_y(u).wait_send()
            two_x(u).wait_send()
            mine(u).wait()

            @pl.when(s != last)
            def _():
                right_own(u).wait_send()

            @pl.when(s != 0)
            def _():
                left_own(u).wait_send()

            return 0

        lax.fori_loop(0, units, sent, 0)
        for by in range(1, sections):

            @pl.when(jnp.logical_and(s >= by, s != last))
            def _(by=by):
                t = s - by

                def relayed(u, _):
                    right_on(t, u).wait_send()
                    return 0

                lax.fori_loop(0, 5 + 3 * (t % 2), relayed, 0)

        for by in range(1, sections):

            @pl.when(jnp.logical_and(s + by < sections, s != 0))
            def _(by=by):
                t = s + by

                def relayed(u, _):
                    left_on(t, u).wait_send()
                    return 0

                lax.fori_loop(0, 5 + 3 * (t % 2), relayed, 0)

    for m in range(micro):
        for c in range(chunks):

            @pl.when(s != last)
            def _():
                hop(h_out, h_in, r.fsend, r.frecv, m, c, 1).wait_send()

            @pl.when(s != 0)
            def _():
                hop(g_out, g_in, r.bsend, r.brecv, m, c, -1).wait_send()

    @pl.when(s == last)
    def _():
        for m in range(micro):
            for j in range(sections - 1):
                share(h_out, r.fin_in, r.fin_send, r.fin_recv, m, j).wait_send()
            r.final_o[m] = h_out[m, (sections - 1) * quarter :]

    @pl.when(s != last)
    def _():
        for m in range(micro):
            share(h_out, r.fin_in, r.fin_send, r.fin_recv, m, 0).wait_recv()
            r.final_o[m] = r.fin_in[m]

    @pl.when(s == 0)
    def _():
        for m in range(micro):
            for j in range(1, sections):
                share(g_out, r.ig_in, r.ig_send, r.ig_recv, m, j).wait_send()
            r.igrad_o[m] = g_out[m, :quarter].astype(F32)

    @pl.when(s != 0)
    def _():
        for m in range(micro):
            share(g_out, r.ig_in, r.ig_send, r.ig_recv, m, 1).wait_recv()
            r.igrad_o[m] = r.ig_in[m].astype(F32)


def pipeline(fused, hidden, inputs):
    micro, length, width = inputs["pages"].shape
    sections = lax.axis_size("section")
    rows = length // sections
    chunks = length // rows
    quarter = length // sections
    heads = width // HEAD_DIM
    wide = max(2 * hidden, heads * length)
    part = width // 8
    half = part // 2
    hbm = pl.BlockSpec(memory_space=pl.ANY)
    vmem = pl.BlockSpec(memory_space=pltpu.VMEM)
    act = (micro, length, width)
    dma = pltpu.SemaphoreType.DMA
    spec = {name: hbm for name in inputs}
    for name in spec:
        if name not in ("pages", "cot", "w_in", "qkv_w", "pos_w", "out_w", "in_w", "down_w"):
            spec[name] = vmem
    outs = {
        "final_o": (vmem, (micro, quarter, width), BF),
        "igrad_o": (vmem, (micro, quarter, width), F32),
    }
    scratch = {
        "place": pltpu.VMEM(act, BF),
        "hide": pltpu.VMEM((micro, length, length), BF),
        "h_in": pltpu.VMEM(act, BF),
        "g_in": pltpu.VMEM(act, BF),
        "h_out": pltpu.VMEM(act, BF),
        "g_out": pltpu.VMEM(act, BF),
        "saved": pltpu.VMEM((micro, length, wide), BF),
        "qkvp": pltpu.VMEM((micro, length, 4 * width), BF),
        "kplus": pltpu.VMEM(act, BF),
        "context": pltpu.VMEM(act, BF),
        "zed": pltpu.VMEM(act, F32),
        "rstd": pltpu.VMEM((micro, length, 128), F32),
        "db": pltpu.VMEM(act, BF),
        "w": pltpu.VMEM((2 * hidden, width), BF),
        "vec": pltpu.VMEM((8, hidden), F32),
        "colsum": pltpu.VMEM((8, hidden), F32),
        "fin_in": pltpu.VMEM((micro, quarter, width), BF),
        "ig_in": pltpu.VMEM((micro, quarter, width), BF),
        "fsend": dma((micro, chunks)),
        "frecv": dma((micro, chunks)),
        "bsend": dma((micro, chunks)),
        "brecv": dma((micro, chunks)),
        "fin_send": dma((micro, sections)),
        "fin_recv": dma((micro,)),
        "ig_send": dma((micro, sections)),
        "ig_recv": dma((micro,)),
        "keep_sem": dma((2,)),
    }
    if fused:
        outs["all_w"] = (hbm, (sections, 8, part, width), BF)
        outs["all_s"] = (vmem, (sections, 8, 128), F32)
        scratch.update(
            stage=pltpu.VMEM((2, 4, part, width), BF),
            vec_all=pltpu.VMEM((8, 8, 128), F32),
            small=pltpu.VMEM((8, 8, 128), F32),
            small_in=pltpu.VMEM((7, 8, 128), F32),
            small_sum=pltpu.VMEM((8, 128), F32),
            table=pltpu.VMEM((8, 4, part, width), BF),
            land_x=pltpu.VMEM((8, 2, half, width), BF),
            land_y=pltpu.VMEM((8, 2, half, width), BF),
            land_x2=pltpu.VMEM((8, half, width), BF),
            land_y2=pltpu.VMEM((8, half, width), BF),
            own_sem=dma((8,)),
            ag_send=dma((8, 8)),
            ag_recv=dma((8, 8)),
            v_send=dma((7,)),
            v_recv=dma((7,)),
            s_send=dma((7,)),
            s_recv=dma((7,)),
            sz_send=dma((sections - 1,)),
            sz_recv=dma((sections,)),
            p0_send=dma((2,)),
            p0_recv=dma((8,)),
            p1x_send=dma((8, 2)),
            p1x_recv=dma((8, 2)),
            p1y_send=dma((8,)),
            p1y_recv=dma((8,)),
            p2x_send=dma((8,)),
            p2x_recv=dma((8,)),
            p2y_send=dma((8,)),
            p2y_recv=dma((8,)),
            left_send=dma((sections, 8)),
            right_send=dma((sections, 8)),
            all_recv=dma((sections, 8)),
        )
    else:
        outs["dw_o"] = (hbm, (2 * hidden, width), BF)
        outs["small_o"] = (vmem, (8, hidden), F32)
        scratch.update(stage=pltpu.VMEM((2, width, width), BF), own_sem=dma)
    names = [*inputs, *outs, *scratch]
    got = pl.pallas_call(
        partial(pipeline_kernel, names, rows, fused),
        out_shape=tuple(jax.ShapeDtypeStruct(shape, kind) for _, shape, kind in outs.values()),
        in_specs=list(spec.values()),
        out_specs=tuple(where for where, _, _ in outs.values()),
        scratch_shapes=list(scratch.values()),
        compiler_params=pltpu.CompilerParams(
            collective_id=0, has_side_effects=True, vmem_limit_bytes=63 * 1024 * 1024
        ),
        name="pipeline",
    )(*inputs.values())
    return dict(zip(outs, got, strict=True))


def spread_kernel(final, igrad, shares, sums, final_o, igrad_o, qkv, bias, pos, out, into, into_b, down, down_b, gain, offset):
    final_o[...] = final[...]
    igrad_o[...] = igrad[...]
    layers, part, width = pos.shape
    for n in range(layers):
        attn, feed = 2 * n, 2 * n + 1
        for i in range(3):
            qkv[n, :, i * width : (i + 1) * width] = shares[attn, i].astype(F32)
        pos[n] = shares[attn, 3].astype(F32)
        out[n] = shares[attn, 4].astype(F32)
        for i in range(4):
            into[n, :, i * width : (i + 1) * width] = shares[feed, i].astype(F32)
            down[n, i * part : (i + 1) * part, :] = shares[feed, 4 + i].astype(F32)
        bias[n] = sums[attn, 0:3, :part]
        for i in range(3):
            into_b[n : n + 1, i * 128 : (i + 1) * 128] = sums[feed, i : i + 1, :]
        down_b[n : n + 1, :] = sums[feed, 3:4, :part]
        for k in range(2):
            gain[n, k : k + 1, :] = sums[2 * n + k, 4:5, :part]
            offset[n, k : k + 1, :] = sums[2 * n + k, 5:6, :part]


def spread_out(got, part, part_h):
    final, igrad, shares, sums = got["final_o"], got["igrad_o"], got["all_w"], got["all_s"]
    layers, width = shares.shape[0] // 2, shares.shape[3]
    shapes = [
        (layers, part, 3 * width),
        (layers, 3, part),
        (layers, part, width),
        (layers, part, width),
        (layers, part, 4 * width),
        (layers, part_h),
        (layers, part_h, width),
        (layers, part),
        (layers, 2, part),
        (layers, 2, part),
    ]
    vmem = pl.BlockSpec(memory_space=pltpu.VMEM)
    like = jax.ShapeDtypeStruct
    return pl.pallas_call(
        spread_kernel,
        out_shape=(
            like(final.shape, BF),
            like(igrad.shape, F32),
            *[like(shape, F32) for shape in shapes],
        ),
        in_specs=[vmem] * 4,
        out_specs=(vmem,) * 12,
        compiler_params=pltpu.CompilerParams(vmem_limit_bytes=48 * 1024 * 1024),
        name="spread",
    )(final, igrad, shares, sums)


def shards(
    pages_in,
    coords,
    boxes,
    qkv_weight,
    attn_bias,
    pos_weight,
    out_weight,
    ffn_in,
    ffn_in_bias,
    ffn_out,
    ffn_out_bias,
    ln_gain,
    ln_bias,
    cotangent,
):
    groups = lax.axis_size("dp")
    s = lax.axis_index("section")
    layer = s // 2
    is_attn = s % 2 == 0
    micro, length, width = pages_in.shape
    hidden = ffn_in.shape[2]
    part = width // groups
    part_h = hidden // groups

    def pick(array):
        return lax.dynamic_index_in_dim(array, layer, 0, keepdims=False)

    inputs = {
        "pages": pages_in,
        "cot": cotangent,
        "coords": coords,
        "boxes": boxes.transpose(0, 2, 1),
        "waves": turns_per_unit(width),
    }
    if groups == 8:
        inputs.update(
            qkv_w=qkv_weight,
            pos_w=pos_weight,
            out_w=out_weight,
            in_w=ffn_in,
            down_w=ffn_out,
            attn_b=attn_bias.transpose(1, 0, 2),
            in_b=ffn_in_bias,
            down_b=ffn_out_bias,
            gain_w=ln_gain,
            offset_w=ln_bias,
        )
        got = pipeline(True, hidden, inputs)
        return spread_out(got, part, part_h)

    norm_row = s % 2
    gain_own = lax.dynamic_index_in_dim(pick(ln_gain), norm_row, 0, keepdims=False)
    offset_own = lax.dynamic_index_in_dim(pick(ln_bias), norm_row, 0, keepdims=False)
    own_a = jnp.where(
        is_attn, jnp.concatenate([pick(qkv_weight), pick(pos_weight)], axis=1), pick(ffn_in)
    )
    own_b = jnp.where(
        is_attn, jnp.pad(pick(out_weight), ((0, part_h - part), (0, 0))), pick(ffn_out)
    )
    wa = lax.all_gather(own_a, "dp", axis=0, tiled=True)
    wb_all = lax.all_gather(own_b, "dp", axis=0, tiled=False)
    wb = jnp.where(
        is_attn,
        jnp.pad(wb_all[:, :part].reshape(width, width), ((0, hidden - width), (0, 0))),
        wb_all.reshape(hidden, width),
    )
    bias_own = jnp.where(
        is_attn,
        jnp.pad(pick(attn_bias).reshape(-1), (0, part_h - 3 * part)),
        pick(ffn_in_bias),
    )
    vec_own = jnp.concatenate([bias_own, pick(ffn_out_bias), gain_own, offset_own])
    vec_all = lax.all_gather(vec_own, "dp", axis=0, tiled=False).astype(F32)
    first = jnp.where(
        is_attn,
        jnp.pad(
            vec_all[:, : 3 * part].reshape(groups, 3, part).transpose(1, 0, 2).reshape(-1),
            (0, hidden - 3 * width),
        ),
        vec_all[:, :part_h].reshape(-1),
    )
    rest = vec_all[:, part_h:].reshape(groups, 3, part).transpose(1, 0, 2).reshape(-1)
    inputs["vec_in"] = jnp.pad(
        jnp.stack([first, jnp.pad(rest, (0, hidden - 3 * width))]), ((0, 6), (0, 0))
    )
    wide_blocks = wa.reshape(width, hidden // width, width).transpose(1, 0, 2)
    inputs["w_in"] = jnp.concatenate([wide_blocks.reshape(hidden, width), wb], axis=0)
    got = pipeline(False, hidden, inputs)
    final, igrad, dw, small = got["final_o"], got["igrad_o"], got["dw_o"], got["small_o"]
    dwa = dw[:hidden].reshape(hidden // width, width, width).transpose(1, 0, 2)
    dwa = dwa.reshape(width, hidden)
    dwb = dw[hidden:]

    shard_a = lax.psum_scatter(dwa, "dp", scatter_dimension=0, tiled=True)
    dwb_cut = jnp.where(
        is_attn,
        jnp.pad(
            dwb[:width].reshape(groups, part, width), ((0, 0), (0, part_h - part), (0, 0))
        ),
        dwb.reshape(groups, part_h, width),
    )
    shard_b = lax.psum_scatter(dwb_cut, "dp", scatter_dimension=0, tiled=True).reshape(
        part_h, width
    )
    small_first = jnp.where(
        is_attn,
        jnp.pad(
            small[0, : 3 * width].reshape(3, groups, part).transpose(1, 0, 2).reshape(groups, -1),
            ((0, 0), (0, part_h - 3 * part)),
        ),
        small[0].reshape(groups, part_h),
    )
    small_rest = (
        small[1, : 3 * width].reshape(3, groups, part).transpose(1, 0, 2).reshape(groups, -1)
    )
    small_cut = jnp.concatenate([small_first, small_rest], axis=1)
    shard_s = lax.psum_scatter(small_cut, "dp", scatter_dimension=0, tiled=True).reshape(-1)

    all_a = lax.all_gather(shard_a, "section", axis=0, tiled=False)
    all_b = lax.all_gather(shard_b, "section", axis=0, tiled=False)
    all_s = lax.all_gather(shard_s, "section", axis=0, tiled=False)

    attn_a, feed_a = all_a[0::2], all_a[1::2]
    attn_s, feed_s = all_s[0::2], all_s[1::2]
    rest_s = all_s[:, part_h:].reshape(-1, 2, 3, part)
    return (
        final,
        igrad,
        attn_a[:, :, : 3 * width].astype(F32),
        attn_s[:, : 3 * part].reshape(-1, 3, part),
        attn_a[:, :, 3 * width :].astype(F32),
        all_b[0::2, :part].astype(F32),
        feed_a.astype(F32),
        feed_s[:, :part_h],
        all_b[1::2].astype(F32),
        feed_s[:, part_h : part_h + part],
        rest_s[:, :, 1],
        rest_s[:, :, 2],
    )


def solution(mesh):
    in_specs = (
        P("dp", None, None),
        P("dp", None, None),
        P("dp", None, None),
        P(None, "dp", None),
        P(None, None, "dp"),
        P(None, "dp", None),
        P(None, "dp", None),
        P(None, "dp", None),
        P(None, "dp"),
        P(None, "dp", None),
        P(None, "dp"),
        P(None, None, "dp"),
        P(None, None, "dp"),
        P("dp", None, None),
    )
    out_specs = (
        P("dp", "section", None),
        P("dp", "section", None),
        P(None, "dp", None),
        P(None, None, "dp"),
        P(None, "dp", None),
        P(None, "dp", None),
        P(None, "dp", None),
        P(None, "dp"),
        P(None, "dp", None),
        P(None, "dp"),
        P(None, None, "dp"),
        P(None, None, "dp"),
    )
    return jax.shard_map(shards, mesh=mesh, in_specs=in_specs, out_specs=out_specs, check_vma=False)
```

```python
from functools import partial
import math

import jax
import jax.numpy as jnp
import numpy as np
from jax import lax
from jax.experimental import pallas as pl
from jax.experimental.pallas import tpu as pltpu
from jax.sharding import PartitionSpec as P

HEAD_DIM = 64
PAIR = 2 * HEAD_DIM
EPSILON = 1e-06
NEGATIVE = -1e30
LOG2E = math.log2(math.e)
SCORE_SCALE = 1.0 / math.sqrt(3.0 * HEAD_DIM)
MESH = pl.DeviceIdType.MESH
BF = jnp.bfloat16
F32 = jnp.float32


def dot_nn(a, b):
    return jnp.dot(a, b, preferred_element_type=F32)


def dot_nt(a, b):
    return lax.dot_general(a, b, (((1,), (1,)), ((), ())), preferred_element_type=F32)


def dot_tn(a, b):
    return lax.dot_general(a, b, (((0,), (0,)), ((), ())), preferred_element_type=F32)


def gelu_and_slope(x):
    bell = jnp.exp2(x * x * (-0.5 * LOG2E))
    t = 1.0 / (1.0 + (0.3275911 / math.sqrt(2.0)) * jnp.abs(x))
    series = t * (
        0.254829592
        + t * (-0.284496736 + t * (1.421413741 + t * (-1.453152027 + t * 1.061405429)))
    )
    tail = 0.5 * series * bell
    cdf = jnp.where(x >= 0.0, 1.0 - tail, tail)
    return x * cdf, cdf + x * bell * (1.0 / math.sqrt(2.0 * math.pi))


TURN_TERMS = [
    (-1.0) ** n * (2.0 * math.pi) ** (2 * n + 1) / math.factorial(2 * n + 1) for n in range(6)
]


def sine_of_turns(turns):
    rest = turns - jnp.floor(turns + 0.5)
    size = 0.25 - jnp.abs(jnp.abs(rest) - 0.25)
    square = size * size
    series = TURN_TERMS[5]
    for term in TURN_TERMS[4::-1]:
        series = series * square + term
    return jnp.where(rest < 0.0, -size, size) * series


def turns_per_unit(width):
    quarter = width // 4
    wave = 10000.0 ** (-np.arange(quarter) / quarter) / (2.0 * math.pi)
    table = np.zeros((2, width))
    table[0, : 2 * quarter] = np.tile(wave, 2)
    table[1, 2 * quarter :] = np.tile(wave, 2)
    return jnp.asarray(table, F32)


class Refs:
    def __init__(self, names, refs):
        self.__dict__.update(zip(names, refs, strict=True))


def pipeline_kernel(names, rows, fused, *refs):
    r = Refs(names, refs)
    h_in, g_in, h_out, g_out = r.h_in, r.g_in, r.h_out, r.g_out
    saved, qkvp, kplus, context, zed, rstd = r.saved, r.qkvp, r.kplus, r.context, r.zed, r.rstd
    db, w, place, hide = r.db, r.w, r.place, r.hide
    vec, colsum = r.vec, r.colsum
    sections = lax.axis_size("section")
    s = lax.axis_index("section")
    kind = s % 2
    layer = s // 2
    last = sections - 1
    micro, length, width = h_in.shape
    hidden = w.shape[0] // 2
    chunks = length // rows
    big = 2 * rows
    bigs = length // big
    quarter = length // sections
    pairs = width // PAIR
    blocks = hidden // width
    is_attn = kind == 0
    is_feed = kind == 1

    if fused:
        d = lax.axis_index("dp")
        part = width // 8
        half = part // 2
        core, cx, cy = d % 2, (d // 2) % 2, d // 4
        chip = d // 2
        near_c = d + 1 - 2 * core
        near_x = d + 2 - 4 * cx
        near_y = d + 4 - 8 * cy
        diag = near_x + 4 - 8 * cy
        units = 5 + 3 * kind
        tail_units = 1 + 3 * kind

        def peer(t):
            tc, tx, ty = t % 2, (t // 2) % 2, t // 4
            return (
                d + tc * (1 - 2 * core) + 2 * tx * (1 - 2 * cx) + 4 * ty * (1 - 2 * cy)
            )

    barrier = pltpu.get_barrier_semaphore()
    for by in range(1, sections):
        pl.semaphore_signal(
            barrier, inc=1, device_id={"section": (s + by) % sections}, device_id_type=MESH
        )
    if fused:
        for t in range(1, 8):
            pl.semaphore_signal(barrier, inc=1, device_id={"dp": peer(t)}, device_id_type=MESH)

    def to_section(source, target, send, recv, at):
        return pltpu.make_async_remote_copy(
            src_ref=source,
            dst_ref=target,
            send_sem=send,
            recv_sem=recv,
            device_id={"section": at},
            device_id_type=MESH,
        )

    def to_near(source, target, send, recv, near):
        return pltpu.make_async_remote_copy(
            src_ref=source,
            dst_ref=target,
            send_sem=send,
            recv_sem=recv,
            device_id={"dp": near},
            device_id_type=MESH,
        )

    def span_of(c, size=rows):
        return pl.ds(pl.multiple_of(c * size, size), size)

    def local_in(source, target, sem, m, c):
        span = span_of(c)
        return pltpu.make_async_copy(source.at[m, span], target.at[m, span], sem.at[m, c])

    def hop(source, target, send, recv, m, c, by):
        span = span_of(c)
        return to_section(
            source.at[m, span],
            target.at[m, span],
            send.at[m, c],
            recv.at[m, c],
            (s + by + sections) % sections,
        )

    def share(source, target, send, recv, m, j):
        span = pl.ds(pl.multiple_of(j * quarter, quarter), quarter)
        return to_section(source.at[m, span], target.at[m], send.at[m, j], recv.at[m], j)

    @pl.when(s == 0)
    def _():
        for m in range(micro):
            for c in range(chunks):
                local_in(r.pages, h_in, r.frecv, m, c).start()

    @pl.when(s == last)
    def _():
        for m in range(micro):
            for c in range(chunks):
                local_in(r.cot, g_in, r.brecv, m, c).start()

    def wait_h(m, c):
        @pl.when(s == 0)
        def _():
            local_in(r.pages, h_in, r.frecv, m, c).wait()

        @pl.when(s != 0)
        def _():
            hop(h_out, h_in, r.fsend, r.frecv, m, c, 1).wait_recv()

    def wait_g(m, c):
        @pl.when(s == last)
        def _():
            local_in(r.cot, g_in, r.brecv, m, c).wait()

        @pl.when(s != last)
        def _():
            hop(g_out, g_in, r.bsend, r.brecv, m, c, -1).wait_recv()

    def send_h(m, c):
        @pl.when(s != last)
        def _():
            hop(h_out, h_in, r.fsend, r.frecv, m, c, 1).start()


    def send_g(m, c):
        @pl.when(s != 0)
        def _():
            hop(g_out, g_in, r.bsend, r.brecv, m, c, -1).start()

        @pl.when(jnp.logical_and(s == 0, c != s))
        def _():
            share(g_out, r.ig_in, r.ig_send, r.ig_recv, m, c).start()

    def block_of(i):
        return w[i * width : (i + 1) * width, :]

    def spots():
        columns = lax.broadcasted_iota(jnp.int32, (1, width), 1)
        phase = jnp.where((columns // (width // 4)) % 2 == 1, 0.25, 0.0)
        tokens_at = lax.broadcasted_iota(jnp.int32, (length, r.boxes.shape[2]), 0)

        def page(m, _):
            turns = lax.dot_general(
                r.coords[m].astype(F32),
                r.waves[...],
                (((0,), (0,)), ((), ())),
                precision=lax.Precision.HIGHEST,
                preferred_element_type=F32,
            )
            place[m] = sine_of_turns(turns + phase).astype(BF)
            box = r.boxes[m]

            def hit(low, high):
                inside = jnp.logical_and(
                    tokens_at >= box[low : low + 1], tokens_at < box[high : high + 1]
                )
                return jnp.where(inside, 1.0, 0.0)

            covered = dot_nt(hit(0, 1), hit(2, 3))
            hide[m] = jnp.where(covered < 0.5, 0.0, NEGATIVE).astype(BF)
            return 0

        lax.fori_loop(0, micro, page, 0)

    if fused:

        def shard_rows(tail, i, shard, count, first=0):
            if tail:
                at = hidden + shard * (part + 3 * part * kind) + i * part + first
            else:
                at = i * width + shard * part + first
            return pl.ds(pl.multiple_of(at, half), count)

        def gather(tail, i, t, shard, near, count=None, first=0):
            span = shard_rows(tail, i, shard, count or part, first)
            u = 4 + i if tail else i
            return to_near(w.at[span], w.at[span], r.ag_send.at[u, t], r.ag_recv.at[u, t], near)

        def over_units(step):
            def head(i, _):
                step(False, i)
                return 0

            def rest(i, _):
                step(True, i)
                return 0

            lax.fori_loop(0, 4, head, 0)
            lax.fori_loop(0, tail_units, rest, 0)

        def own_copy(source, tail, i):
            u = 4 + i if tail else i
            return pltpu.make_async_copy(
                source, w.at[shard_rows(tail, i, d, part)], r.own_sem.at[u]
            )

        @pl.when(is_attn)
        def _():
            for i in range(3):
                own_copy(
                    r.qkv_w.at[layer, :, pl.ds(i * width, width)], False, i
                ).start()
            own_copy(r.pos_w.at[layer], False, 3).start()
            own_copy(r.out_w.at[layer], True, 0).start()

        @pl.when(is_feed)
        def _():
            for i in range(4):
                own_copy(r.in_w.at[layer, :, pl.ds(i * width, width)], False, i).start()
            for i in range(4):
                own_copy(r.down_w.at[layer, pl.ds(i * part, part), :], True, i).start()

        def first_round(tail, i):
            own_copy(r.pos_w.at[layer], tail, i).wait()
            gather(tail, i, 0, d, near_x).start()
            gather(tail, i, 1, d, near_y).start()
            gather(tail, i, 2, d, near_c).start()

        def second_round(tail, i):
            gather(tail, i, 0, near_x, near_x).wait_recv()
            gather(tail, i, 3, near_x, near_y, half, 0).start()
            gather(tail, i, 5, near_x, near_c).start()
            gather(tail, i, 1, near_y, near_y).wait_recv()
            gather(tail, i, 4, near_y, near_x, half, half).start()
            gather(tail, i, 6, near_y, near_c).start()

        def third_round(tail, i):
            gather(tail, i, 3, diag, near_y, half, 0).wait_recv()
            gather(tail, i, 4, diag, near_x, half, half).wait_recv()
            gather(tail, i, 7, diag, near_c).start()

        def last_round(tail, i):
            flip = 1 - 2 * core
            gather(tail, i, 2, near_c, near_c).wait_recv()
            gather(tail, i, 5, near_x + flip, near_c).wait_recv()
            gather(tail, i, 6, near_y + flip, near_c).wait_recv()
            gather(tail, i, 7, diag + flip, near_c).wait_recv()

        def gather_sent(tail, i):
            for t, (shard, near) in enumerate(((d, near_x), (d, near_y), (d, near_c))):
                gather(tail, i, t, shard, near).wait_send()
            gather(tail, i, 3, near_x, near_y, half, 0).wait_send()
            gather(tail, i, 4, near_y, near_x, half, half).wait_send()
            gather(tail, i, 5, near_x, near_c).wait_send()
            gather(tail, i, 6, near_y, near_c).wait_send()
            gather(tail, i, 7, diag, near_c).wait_send()

        def of_layer(ref):
            whole = ref[...].astype(F32)
            row = whole[0:1]
            for i in range(1, whole.shape[0]):
                row = jnp.where(layer == i, whole[i : i + 1], row)
            return row

        mine_v = r.vec_all.at[d]
        pair = jnp.concatenate([r.gain_w[layer], r.offset_w[layer]], axis=0).astype(F32)
        mine_v[3:4, :part] = of_layer(r.down_b)
        mine_v[4:5, :part] = jnp.where(is_attn, pair[0:1], pair[1:2])
        mine_v[5:6, :part] = jnp.where(is_attn, pair[2:3], pair[3:4])

        @pl.when(is_attn)
        def _():
            for i in range(3):
                mine_v[i : i + 1, :part] = of_layer(r.attn_b.at[i])

        @pl.when(is_feed)
        def _():
            row = of_layer(r.in_b)
            for i in range(3):
                mine_v[i : i + 1, :] = row[:, i * 128 : (i + 1) * 128]

        def vec_copy(t, source):
            return to_near(
                mine_v, r.vec_all.at[source], r.v_send.at[t - 1], r.v_recv.at[t - 1], peer(t)
            )

        pl.semaphore_wait(barrier, sections - 1 + 7)
        for t in range(1, 8):
            vec_copy(t, d).start()
        over_units(first_round)

        @pl.when(is_attn)
        def _():
            spots()

        for t in range(1, 8):
            vec_copy(t, peer(t)).wait_recv()
        for dest in range(8):
            row = r.vec_all[dest]
            at = dest * part

            @pl.when(is_attn)
            def _(row=row, at=at):
                for i in range(3):
                    vec[0:1, i * width + at : i * width + at + part] = row[i : i + 1, :part]

            @pl.when(is_feed)
            def _(row=row, dest=dest):
                for i in range(3):
                    lane_at = dest * 4 * part + i * 128
                    vec[0:1, lane_at : lane_at + 128] = row[i : i + 1, :]

            for i in range(3):
                vec[1:2, i * width + at : i * width + at + part] = row[3 + i : 4 + i, :part]

        over_units(second_round)

        def rounds(tail, i):
            third_round(tail, i)
            last_round(tail, i)

        def over_head(step):
            def head(i, _):
                step(False, i)
                return 0

            lax.fori_loop(0, 4, head, 0)

        @pl.when(is_attn)
        def _():
            over_head(third_round)
            over_head(last_round)

        @pl.when(is_feed)
        def _():
            over_units(third_round)
            over_units(last_round)
    else:
        whole = pltpu.make_async_copy(r.w_in, w, r.own_sem)
        whole.start()
        vec[...] = r.vec_in[...]
        spots()
        pl.semaphore_wait(barrier, sections - 1)
        whole.wait()

    def norm_out(m, c, summed, gain, offset, size=rows):
        span = span_of(c, size)
        mean = jnp.mean(summed, axis=1, keepdims=True)
        center = summed - mean
        spread = jnp.mean(center * center, axis=1, keepdims=True)
        inv = lax.rsqrt(spread + EPSILON)
        z = center * inv
        zed[m, span] = z
        rstd[m, span] = jnp.broadcast_to(inv, (size, 128))
        h_out[m, span] = (z * gain + offset).astype(BF)
        for i in range(size // rows):
            send_h(m, c * (size // rows) + i)

    def norm_back(m, c, gain, bias_at, size=rows):
        span = span_of(c, size)
        g = g_in[m, span].astype(F32)
        z = zed[m, span]
        inv = rstd[m, span][:, :1]
        u = g * gain
        mean_u = jnp.mean(u, axis=1, keepdims=True)
        mean_uz = jnp.mean(u * z, axis=1, keepdims=True)
        grad = (u - mean_u - z * mean_uz) * inv
        low = grad.astype(BF)
        db[m, span] = low
        colsum[1:2, width : 2 * width] += jnp.sum(g * z, axis=0, keepdims=True)
        colsum[1:2, 2 * width : 3 * width] += jnp.sum(g, axis=0, keepdims=True)
        at = bias_at
        colsum[at[0] : at[0] + 1, at[1] : at[1] + width] += jnp.sum(
            low.astype(F32), axis=0, keepdims=True
        )
        return grad, low

    colsum[...] = jnp.zeros_like(colsum)
    gain = vec[1:2, width : 2 * width]
    offset = vec[1:2, 2 * width : 3 * width]

    @pl.when(is_attn)
    def _():
        lane = lax.broadcasted_iota(jnp.int32, (1, PAIR), 1) < HEAD_DIM
        lane2 = lax.broadcasted_iota(jnp.int32, (1, 2 * PAIR), 1) % PAIR < HEAD_DIM

        def places(idx, _):
            m, c = idx // bigs, idx % bigs
            span = span_of(c, big)
            qkvp[m, span, 3 * width :] = dot_nn(place[m, span], block_of(3)).astype(BF)
            return 0

        lax.fori_loop(0, micro * bigs, places, 0)

        def forward(m, _):
            def project(c, _):
                span = span_of(c, big)
                wait_h(m, 2 * c)
                wait_h(m, 2 * c + 1)
                h = h_in[m, span]
                q = dot_nn(h, block_of(0)) + vec[0:1, :width]
                qkvp[m, span, :width] = q.astype(BF)
                k = dot_nn(h, block_of(1)).astype(BF)
                qkvp[m, span, width : 2 * width] = k
                kplus[m, span] = (
                    k.astype(F32) + qkvp[m, span, 3 * width :].astype(F32)
                ).astype(BF)
                v = dot_nn(h, block_of(2)) + vec[0:1, width : 2 * width]
                qkvp[m, span, 2 * width : 3 * width] = v.astype(BF)
                return 0

            lax.fori_loop(0, bigs, project, 0)

            def heads(t, _):
                off = pl.multiple_of(t * PAIR, PAIR)
                left = jnp.concatenate(
                    [qkvp[m, :, pl.ds(off, PAIR)], qkvp[m, :, pl.ds(off + 3 * width, PAIR)]],
                    axis=1,
                )
                right = jnp.concatenate(
                    [kplus[m, :, pl.ds(off, PAIR)], qkvp[m, :, pl.ds(off + width, PAIR)]],
                    axis=1,
                )
                v = qkvp[m, :, pl.ds(off + 2 * width, PAIR)]
                bias = hide[m].astype(F32)
                mixed = []
                blank = jnp.zeros_like(left)
                both = jnp.concatenate(
                    [jnp.where(lane2, left, blank), jnp.where(lane2, blank, left)], axis=0
                )
                raw = dot_nt(both, right)
                for side in range(2):
                    score = raw[side * length : (side + 1) * length] * (SCORE_SCALE * LOG2E) + bias
                    top = jnp.max(score, axis=1, keepdims=True)
                    power = jnp.exp2(score - top)
                    total = jnp.sum(power, axis=1, keepdims=True)
                    prob = (power * (1.0 / total)).astype(BF)
                    at = pl.multiple_of((2 * t + side) * length, length)
                    saved[m, :, pl.ds(at, length)] = prob
                    mixed.append(dot_nn(prob, v))
                context[m, :, pl.ds(off, PAIR)] = jnp.where(lane, mixed[0], mixed[1]).astype(BF)
                return 0

            lax.fori_loop(0, pairs, heads, 0, unroll=2)

            if fused:

                @pl.when(m == 0)
                def _():
                    rounds(True, 0)

            def attend(c, _):
                span = span_of(c, big)
                branch = dot_nn(context[m, span], block_of(4))
                summed = h_in[m, span].astype(F32) + branch + vec[0:1, 2 * width : 3 * width]
                norm_out(m, c, summed, gain, offset, big)
                return 0

            lax.fori_loop(0, bigs, attend, 0)
            return 0

        lax.fori_loop(0, micro, forward, 0)

        def backward(m, _):
            def enter(c, _):
                span = span_of(c, big)
                wait_g(m, 2 * c)
                wait_g(m, 2 * c + 1)
                grad, low = norm_back(m, c, gain, (0, 2 * width), big)
                zed[m, span] = grad
                g_in[m, span] = dot_nt(low, block_of(4)).astype(BF)
                return 0

            lax.fori_loop(0, bigs, enter, 0)

            def heads(t, _):
                off = pl.multiple_of(t * PAIR, PAIR)
                left = jnp.concatenate(
                    [qkvp[m, :, pl.ds(off, PAIR)], qkvp[m, :, pl.ds(off + 3 * width, PAIR)]],
                    axis=1,
                )
                right = jnp.concatenate(
                    [kplus[m, :, pl.ds(off, PAIR)], qkvp[m, :, pl.ds(off + width, PAIR)]],
                    axis=1,
                )
                v = qkvp[m, :, pl.ds(off + 2 * width, PAIR)]
                grad_c = g_in[m, :, pl.ds(off, PAIR)]
                blank = jnp.zeros_like(grad_c)
                both = jnp.concatenate(
                    [jnp.where(lane, grad_c, blank), jnp.where(lane, blank, grad_c)], axis=0
                )
                at = pl.multiple_of(2 * t * length, 2 * length)
                prob = saved[m, :, pl.ds(at, 2 * length)]
                grad_p = dot_nt(both, v)
                grad_s = []
                for side in range(2):
                    wide_p = prob[:, side * length : (side + 1) * length].astype(F32)
                    part_p = grad_p[side * length : (side + 1) * length]
                    dot_row = jnp.sum(wide_p * part_p, axis=1, keepdims=True)
                    grad_s.append((wide_p * (part_p - dot_row)).astype(BF))
                got_v = dot_tn(prob, grad_c)
                got_l = dot_nn(jnp.concatenate(grad_s, axis=0), right)
                got_r = dot_tn(jnp.concatenate(grad_s, axis=1), left)
                grad_v = jnp.where(lane, got_v[:length], got_v[length:]).astype(BF)
                grad_l = jnp.where(lane2, got_l[:length], got_l[length:])
                grad_r = jnp.where(lane2, got_r[:length], got_r[length:])
                grad_q = (grad_l[:, :PAIR] * SCORE_SCALE).astype(BF)
                grad_k = ((grad_r[:, :PAIR] + grad_r[:, PAIR:]) * SCORE_SCALE).astype(BF)
                grad_pl = ((grad_l[:, PAIR:] + grad_r[:, :PAIR]) * SCORE_SCALE).astype(BF)
                qkvp[m, :, pl.ds(off, PAIR)] = grad_q
                qkvp[m, :, pl.ds(off + width, PAIR)] = grad_k
                qkvp[m, :, pl.ds(off + 2 * width, PAIR)] = grad_v
                qkvp[m, :, pl.ds(off + 3 * width, PAIR)] = grad_pl
                colsum[0:1, pl.ds(off, PAIR)] += jnp.sum(
                    grad_q.astype(F32), axis=0, keepdims=True
                )
                colsum[0:1, pl.ds(off + width, PAIR)] += jnp.sum(
                    grad_v.astype(F32), axis=0, keepdims=True
                )
                return 0

            lax.fori_loop(0, pairs, heads, 0, unroll=2)

            def leave(c, _):
                span = span_of(c, big)
                total = zed[m, span]
                for i in range(3):
                    total = total + dot_nt(
                        qkvp[m, span, i * width : (i + 1) * width], block_of(i)
                    )
                g_out[m, span] = total.astype(BF)
                send_g(m, 2 * c)
                send_g(m, 2 * c + 1)
                return 0

            lax.fori_loop(0, bigs, leave, 0)
            return 0

        lax.fori_loop(0, micro, backward, 0)

    @pl.when(is_feed)
    def _():
        def forward(idx, _):
            m, c = idx // chunks, idx % chunks
            span = span_of(c)
            wait_h(m, c)
            h = h_in[m, span]
            summed = h.astype(F32) + vec[1:2, :width]
            for f in range(blocks):
                at = f * width
                inner = dot_nn(h, block_of(f)) + vec[0:1, at : at + width]
                value, slope = gelu_and_slope(inner)
                low = value.astype(BF)
                saved[m, span, at : at + width] = low
                saved[m, span, hidden + at : hidden + at + width] = slope.astype(BF)
                summed = summed + dot_nn(low, block_of(blocks + f))
            norm_out(m, c, summed, gain, offset)
            return 0

        def backward(m, c, size):
            span = span_of(c, size)
            hops = size // rows
            for i in range(hops):
                wait_g(m, c * hops + i)
            total, low = norm_back(m, c, gain, (1, 0), size)
            for f in range(blocks):
                at = f * width
                grad_a = dot_nt(low, block_of(blocks + f)).astype(BF).astype(F32)
                slope = saved[m, span, hidden + at : hidden + at + width].astype(F32)
                grad_i = (grad_a * slope).astype(BF)
                saved[m, span, hidden + at : hidden + at + width] = grad_i
                colsum[0:1, at : at + width] += jnp.sum(
                    grad_i.astype(F32), axis=0, keepdims=True
                )
                total = total + dot_nt(grad_i, block_of(f))
            g_out[m, span] = total.astype(BF)
            for i in range(hops):
                send_g(m, c * hops + i)

        def step(i, _):
            page, c = i // chunks, i % chunks
            turn = jnp.where(s == last, page % 2, page // micro)
            m = jnp.where(s == last, page // 2, page % micro)

            @pl.when(turn == 0)
            def _():
                forward(m * chunks + c, 0)

            @pl.when(jnp.logical_and(turn == 1, s != last))
            def _():
                backward(m, c, rows)

            @pl.when(jnp.logical_and(jnp.logical_and(turn == 1, s == last), c % 2 == 0))
            def _():
                backward(m, c // 2, big)

            return 0

        lax.fori_loop(0, 2 * micro * chunks, step, 0)

    tokens = micro * length
    stage = r.stage

    def tall(ref, at):
        return ref[:, :, pl.ds(at, width)].reshape(tokens, width)

    if fused:
        table = r.table
        low_half, high_half = pl.ds(0, half), pl.ds(half, half)

        def add(target, other):
            return (target.astype(F32) + other.astype(F32)).astype(BF)

        def give(e, by_chip):
            slot = e % 2
            return to_near(
                stage.at[slot],
                table.at[pl.ds(4, 4), e - 4] if by_chip else table.at[e],
                r.p0_send.at[slot],
                r.p0_recv.at[e],
                near_c,
            )

        def emit(e, value, by_chip):
            slot = e % 2

            @pl.when(e >= 2)
            def _():
                give(e, by_chip).wait_send()

            low = value.astype(BF)
            if by_chip:
                sides = [low[: 4 * part].reshape(4, part, width), low[4 * part :].reshape(4, part, width)]
            else:
                grid = low.reshape(4, 2, part, width)
                sides = [grid[:, 0], grid[:, 1]]
            stage[slot] = jnp.where(core == 0, sides[1], sides[0])
            give(e, by_chip).start()
            kept = jnp.where(core == 0, sides[0], sides[1])
            if by_chip:
                for j in range(4):
                    at = pl.multiple_of(((4 + j) * 4 + e - 4) * part, part)
                    w[pl.ds(at, part), :] = kept[j]
            else:
                at = pl.multiple_of(e * 4 * part, 4 * part)
                w[pl.ds(at, 4 * part), :] = kept.reshape(4 * part, width)

        def finish(count, by_chip):
            give(count - 2, by_chip).wait_send()
            give(count - 1, by_chip).wait_send()

        def one_x(u, y):
            return to_near(
                table.at[u, 2 * y + 1 - cx, low_half],
                r.land_x.at[u, y],
                r.p1x_send.at[u, y],
                r.p1x_recv.at[u, y],
                near_x,
            )

        def one_y(u):
            return to_near(
                table.at[u, pl.ds(2 - 2 * cy, 2), high_half],
                r.land_y.at[u],
                r.p1y_send.at[u],
                r.p1y_recv.at[u],
                near_y,
            )

        def two_y(u):
            return to_near(
                table.at[u, 2 - 2 * cy + cx, low_half],
                r.land_y2.at[u],
                r.p2y_send.at[u],
                r.p2y_recv.at[u],
                near_y,
            )

        def two_x(u):
            return to_near(
                table.at[u, 2 * cy + 1 - cx, high_half],
                r.land_x2.at[u],
                r.p2x_send.at[u],
                r.p2x_recv.at[u],
                near_x,
            )

        def left_own(u):
            return to_section(
                table.at[u, chip],
                r.all_w.at[s, u],
                r.left_send.at[s, u],
                r.all_recv.at[s, u],
                (s - 1 + sections) % sections,
            )

        def left_on(t, u):
            return to_section(
                r.all_w.at[t, u],
                r.all_w.at[t, u],
                r.left_send.at[t, u],
                r.all_recv.at[t, u],
                (s - 1 + sections) % sections,
            )

        def right_own(u):
            return to_section(
                table.at[u, chip],
                r.all_w.at[s, u],
                r.right_send.at[s, u],
                r.all_recv.at[s, u],
                (s + 1) % sections,
            )

        def right_on(t, u):
            return to_section(
                r.all_w.at[t, u],
                r.all_w.at[t, u],
                r.right_send.at[t, u],
                r.all_recv.at[t, u],
                (s + 1) % sections,
            )

        def mine(u):
            return pltpu.make_async_copy(table.at[u, chip], r.all_w.at[s, u], r.own_sem.at[u])

        def merge_core(u):
            @pl.when(u <= 4)
            def _():
                give(u, False).wait_recv()

            @pl.when(jnp.logical_and(u == 4, is_feed))
            def _():
                for e in range(5, 8):
                    give(e, True).wait_recv()

            at = pl.multiple_of(u * 4 * part, 4 * part)
            table[u] = add(table[u], w[pl.ds(at, 4 * part), :].reshape(4, part, width))
            for y in range(2):
                one_x(u, y).start()
            one_y(u).start()

        def merge_one(u):
            for y in range(2):
                one_x(u, y).wait_recv()
                at = 2 * y + cx
                table[u, at, :half] = add(table[u, at, :half], r.land_x[u, y])
            two_y(u).start()
            one_y(u).wait_recv()
            for x in range(2):
                at = 2 * cy + x
                table[u, at, half:] = add(table[u, at, half:], r.land_y[u, x])
            two_x(u).start()

        def merge_two(u):
            two_y(u).wait_recv()
            table[u, chip, :half] = add(table[u, chip, :half], r.land_y2[u])
            two_x(u).wait_recv()
            table[u, chip, half:] = add(table[u, chip, half:], r.land_x2[u])

            @pl.when(s != last)
            def _():
                right_own(u).start()

            @pl.when(s == last)
            def _():
                left_own(u).start()

            mine(u).start()

        late = 3 * kind

        def at_step(q, merge):
            @pl.when(jnp.logical_and(q >= 0, q < 4))
            def _():
                merge(q)

            @pl.when(jnp.logical_and(q >= 4 + late, q < units + late))
            def _():
                merge(q - late)

        def advance(q):
            at_step(q, merge_core)
            at_step(q - 2, merge_one)
            at_step(q - 4, merge_two)

        beyond = last - s
        hand_on = jnp.where(s > 0, 13 * (beyond // 2) + 8 * (beyond % 2), 0)

        def relay_left(k):
            @pl.when(jnp.logical_and(k >= 0, k < hand_on))
            def _():
                odd = (k % 13) // 8
                t = last - 2 * (k // 13) - odd
                copy = left_on(t, k % 13 - 8 * odd)
                copy.wait_recv()
                copy.start()

        sm = r.small
        for dest in range(8):
            at = dest * part

            @pl.when(is_attn)
            def _(dest=dest, at=at):
                for i in range(3):
                    sm[dest, i : i + 1, :part] = colsum[
                        0:1, i * width + at : i * width + at + part
                    ]

            @pl.when(is_feed)
            def _(dest=dest):
                for i in range(3):
                    lane_at = dest * 4 * part + i * 128
                    sm[dest, i : i + 1, :] = colsum[0:1, lane_at : lane_at + 128]

            for i in range(3):
                sm[dest, 3 + i : 4 + i, :part] = colsum[
                    1:2, i * width + at : i * width + at + part
                ]

        def small_copy(t):
            return to_near(
                sm.at[peer(t)], r.small_in.at[t - 1], r.s_send.at[t - 1], r.s_recv.at[t - 1], peer(t)
            )

        def small_share(by):
            return to_section(
                r.small_sum,
                r.all_s.at[s],
                r.sz_send.at[by - 1],
                r.sz_recv.at[s],
                (s + by) % sections,
            )

        for t in range(1, 8):
            small_copy(t).start()
        over_units(gather_sent)
        for t in range(1, 8):
            vec_copy(t, d).wait_send()
    else:

        def flush(slot, at):
            return pltpu.make_async_copy(
                stage.at[slot], r.dw_o.at[pl.ds(at, width)], r.keep_sem.at[slot]
            )

        def emit(e, value, by_chip):
            slot = e % 2

            @pl.when(e >= 2)
            def _():
                flush(slot, 0).wait()

            stage[slot] = value.astype(BF)
            flush(slot, pl.multiple_of(e * width, width)).start()

        def finish(count, by_chip):
            flush(0, 0).wait()
            flush(1, 0).wait()

        def advance(u):
            pass

        def relay_left(k):
            pass

    @pl.when(is_attn)
    def _():
        def step(e, _):
            at = pl.multiple_of(e * width, width)
            emit(e, dot_tn(tall(h_in, 0), tall(qkvp, at)), False)
            advance(e - 1)
            return 0

        lax.fori_loop(0, 3, step, 0)
        emit(3, dot_tn(tall(place, 0), tall(qkvp, 3 * width)), False)
        advance(jnp.int32(2))
        emit(4, dot_tn(tall(context, 0), tall(db, 0)), False)
        advance(jnp.int32(3))
        finish(5, False)

    @pl.when(is_feed)
    def _():
        def step(e, _):
            at = pl.multiple_of(e * width + hidden, width)
            emit(e, dot_tn(tall(h_in, 0), tall(saved, at)), False)
            advance(e - 1)
            relay_left(e - 1)
            return 0

        lax.fori_loop(0, blocks, step, 0)

        def step_b(i, _):
            at = pl.multiple_of(i * width, width)
            emit(i + blocks, dot_tn(tall(saved, at), tall(db, 0)), True)
            advance(i + blocks - 1)
            relay_left(i + blocks - 1)
            return 0

        lax.fori_loop(0, blocks, step_b, 0)
        finish(2 * blocks, True)

    if not fused:
        r.small_o[...] = colsum[...]

        @pl.when(s == last)
        def _():
            for m in range(micro):
                for j in range(sections - 1):
                    share(h_out, r.fin_in, r.fin_send, r.fin_recv, m, j).start()
    else:

        def go_on(q, _):
            advance(q)
            relay_left(q - 4 + 4 * kind)

            @pl.when(jnp.logical_and(jnp.logical_and(is_feed, s < last), q >= 9))
            def _():
                left_own(q - 9).start()

            return 0

        for t in range(1, 8):
            small_copy(t).wait_recv()
        total = sm[d]
        for t in range(7):
            total = total + r.small_in[t]
        r.small_sum[...] = total
        for by in range(1, sections):
            small_share(by).start()
        lax.fori_loop(4 + late, units + late + 4, go_on, 0)

        def rest_left(k, _):
            relay_left(k)
            return 0

        lax.fori_loop(5 + 10 * kind, hand_on, rest_left, 0)

        @pl.when(jnp.logical_and(s > 0, s < last))
        def _():
            def own_left(u, _):
                left_own(u).start()
                return 0

            lax.fori_loop(6 * kind, units, own_left, 0)


        for by in range(1, sections):

            @pl.when(s >= by)
            def _(by=by):
                t = s - by

                def relay(u, _, by=by):
                    right_on(t, u).wait_recv()
                    if by == 2:
                        @pl.when(jnp.logical_and(s == last, u == 3))
                        def _():
                            for m in range(micro):
                                for j in range(sections - 1):
                                    share(h_out, r.fin_in, r.fin_send, r.fin_recv, m, j).start()

                    @pl.when(s != last)
                    def _():
                        right_on(t, u).start()

                    return 0

                lax.fori_loop(0, 5 + 3 * (t % 2), relay, 0)

        for by in range(1, sections):

            @pl.when(jnp.logical_and(s + by < sections, s == 0))
            def _(by=by):
                t = s + by

                def arrive(u, _):
                    left_on(t, u).wait_recv()
                    return 0

                lax.fori_loop(0, 5 + 3 * (t % 2), arrive, 0)

        for by in range(1, sections):
            t = (s + by) % sections
            to_section(
                r.small_sum, r.all_s.at[t], r.sz_send.at[by - 1], r.sz_recv.at[t], t
            ).wait_recv()
        r.all_s[s] = r.small_sum[...]

        for t in range(1, 8):
            small_copy(t).wait_send()
        for by in range(1, sections):
            small_share(by).wait_send()

        def sent(u, _):
            for y in range(2):
                one_x(u, y).wait_send()
            one_y(u).wait_send()
            two_y(u).wait_send()
            two_x(u).wait_send()
            mine(u).wait()

            @pl.when(s != last)
            def _():
                right_own(u).wait_send()

            @pl.when(s != 0)
            def _():
                left_own(u).wait_send()

            return 0

        lax.fori_loop(0, units, sent, 0)
        for by in range(1, sections):

            @pl.when(jnp.logical_and(s >= by, s != last))
            def _(by=by):
                t = s - by

                def relayed(u, _):
                    right_on(t, u).wait_send()
                    return 0

                lax.fori_loop(0, 5 + 3 * (t % 2), relayed, 0)

        for by in range(1, sections):

            @pl.when(jnp.logical_and(s + by < sections, s != 0))
            def _(by=by):
                t = s + by

                def relayed(u, _):
                    left_on(t, u).wait_send()
                    return 0

                lax.fori_loop(0, 5 + 3 * (t % 2), relayed, 0)

    for m in range(micro):
        for c in range(chunks):

            @pl.when(s != last)
            def _():
                hop(h_out, h_in, r.fsend, r.frecv, m, c, 1).wait_send()

            @pl.when(s != 0)
            def _():
                hop(g_out, g_in, r.bsend, r.brecv, m, c, -1).wait_send()

    @pl.when(s == last)
    def _():
        for m in range(micro):
            for j in range(sections - 1):
                share(h_out, r.fin_in, r.fin_send, r.fin_recv, m, j).wait_send()
            r.final_o[m] = h_out[m, (sections - 1) * quarter :]

    @pl.when(s != last)
    def _():
        for m in range(micro):
            share(h_out, r.fin_in, r.fin_send, r.fin_recv, m, 0).wait_recv()
            r.final_o[m] = r.fin_in[m]

    @pl.when(s == 0)
    def _():
        for m in range(micro):
            for j in range(1, sections):
                share(g_out, r.ig_in, r.ig_send, r.ig_recv, m, j).wait_send()
            r.igrad_o[m] = g_out[m, :quarter].astype(F32)

    @pl.when(s != 0)
    def _():
        for m in range(micro):
            share(g_out, r.ig_in, r.ig_send, r.ig_recv, m, 1).wait_recv()
            r.igrad_o[m] = r.ig_in[m].astype(F32)


def pipeline(fused, hidden, inputs):
    micro, length, width = inputs["pages"].shape
    sections = lax.axis_size("section")
    rows = length // sections
    chunks = length // rows
    quarter = length // sections
    heads = width // HEAD_DIM
    wide = max(2 * hidden, heads * length)
    part = width // 8
    half = part // 2
    hbm = pl.BlockSpec(memory_space=pl.ANY)
    vmem = pl.BlockSpec(memory_space=pltpu.VMEM)
    act = (micro, length, width)
    dma = pltpu.SemaphoreType.DMA
    spec = {name: hbm for name in inputs}
    for name in spec:
        if name not in ("pages", "cot", "w_in", "qkv_w", "pos_w", "out_w", "in_w", "down_w"):
            spec[name] = vmem
    outs = {
        "final_o": (vmem, (micro, quarter, width), BF),
        "igrad_o": (vmem, (micro, quarter, width), F32),
    }
    scratch = {
        "place": pltpu.VMEM(act, BF),
        "hide": pltpu.VMEM((micro, length, length), BF),
        "h_in": pltpu.VMEM(act, BF),
        "g_in": pltpu.VMEM(act, BF),
        "h_out": pltpu.VMEM(act, BF),
        "g_out": pltpu.VMEM(act, BF),
        "saved": pltpu.VMEM((micro, length, wide), BF),
        "qkvp": pltpu.VMEM((micro, length, 4 * width), BF),
        "kplus": pltpu.VMEM(act, BF),
        "context": pltpu.VMEM(act, BF),
        "zed": pltpu.VMEM(act, F32),
        "rstd": pltpu.VMEM((micro, length, 128), F32),
        "db": pltpu.VMEM(act, BF),
        "w": pltpu.VMEM((2 * hidden, width), BF),
        "vec": pltpu.VMEM((8, hidden), F32),
        "colsum": pltpu.VMEM((8, hidden), F32),
        "fin_in": pltpu.VMEM((micro, quarter, width), BF),
        "ig_in": pltpu.VMEM((micro, quarter, width), BF),
        "fsend": dma((micro, chunks)),
        "frecv": dma((micro, chunks)),
        "bsend": dma((micro, chunks)),
        "brecv": dma((micro, chunks)),
        "fin_send": dma((micro, sections)),
        "fin_recv": dma((micro,)),
        "ig_send": dma((micro, sections)),
        "ig_recv": dma((micro,)),
        "keep_sem": dma((2,)),
    }
    if fused:
        outs["all_w"] = (hbm, (sections, 8, part, width), BF)
        outs["all_s"] = (vmem, (sections, 8, 128), F32)
        scratch.update(
            stage=pltpu.VMEM((2, 4, part, width), BF),
            vec_all=pltpu.VMEM((8, 8, 128), F32),
            small=pltpu.VMEM((8, 8, 128), F32),
            small_in=pltpu.VMEM((7, 8, 128), F32),
            small_sum=pltpu.VMEM((8, 128), F32),
            table=pltpu.VMEM((8, 4, part, width), BF),
            land_x=pltpu.VMEM((8, 2, half, width), BF),
            land_y=pltpu.VMEM((8, 2, half, width), BF),
            land_x2=pltpu.VMEM((8, half, width), BF),
            land_y2=pltpu.VMEM((8, half, width), BF),
            own_sem=dma((8,)),
            ag_send=dma((8, 8)),
            ag_recv=dma((8, 8)),
            v_send=dma((7,)),
            v_recv=dma((7,)),
            s_send=dma((7,)),
            s_recv=dma((7,)),
            sz_send=dma((sections - 1,)),
            sz_recv=dma((sections,)),
            p0_send=dma((2,)),
            p0_recv=dma((8,)),
            p1x_send=dma((8, 2)),
            p1x_recv=dma((8, 2)),
            p1y_send=dma((8,)),
            p1y_recv=dma((8,)),
            p2x_send=dma((8,)),
            p2x_recv=dma((8,)),
            p2y_send=dma((8,)),
            p2y_recv=dma((8,)),
            left_send=dma((sections, 8)),
            right_send=dma((sections, 8)),
            all_recv=dma((sections, 8)),
        )
    else:
        outs["dw_o"] = (hbm, (2 * hidden, width), BF)
        outs["small_o"] = (vmem, (8, hidden), F32)
        scratch.update(stage=pltpu.VMEM((2, width, width), BF), own_sem=dma)
    names = [*inputs, *outs, *scratch]
    got = pl.pallas_call(
        partial(pipeline_kernel, names, rows, fused),
        out_shape=tuple(jax.ShapeDtypeStruct(shape, kind) for _, shape, kind in outs.values()),
        in_specs=list(spec.values()),
        out_specs=tuple(where for where, _, _ in outs.values()),
        scratch_shapes=list(scratch.values()),
        compiler_params=pltpu.CompilerParams(
            collective_id=0, has_side_effects=True, vmem_limit_bytes=63 * 1024 * 1024
        ),
        name="pipeline",
    )(*inputs.values())
    return dict(zip(outs, got, strict=True))


def spread_kernel(
    final,
    igrad,
    shares,
    sums,
    final_o,
    igrad_o,
    qkv_o,
    bias,
    pos_o,
    out_o,
    into_o,
    into_b,
    down_o,
    down_b,
    gain,
    offset,
    got,
    qkv,
    pos,
    out,
    into,
    down,
    load_sem,
    save_sem,
):
    layers, part, width = pos.shape

    def load(t):
        return pltpu.make_async_copy(shares.at[t], got.at[t], load_sem.at[t])

    def save(n, i):
        source, target = (
            (qkv, qkv_o),
            (pos, pos_o),
            (out, out_o),
            (into, into_o),
            (down, down_o),
        )[i]
        return pltpu.make_async_copy(source.at[n], target.at[n], save_sem.at[n, i])

    for t in range(2 * layers):
        load(t).start()
    for n in range(layers):
        attn, feed = 2 * n, 2 * n + 1
        load(attn).wait()
        for i in range(3):
            qkv[n, :, i * width : (i + 1) * width] = got[attn, i].astype(F32)
        save(n, 0).start()
        pos[n] = got[attn, 3].astype(F32)
        save(n, 1).start()
        out[n] = got[attn, 4].astype(F32)
        save(n, 2).start()
        load(feed).wait()
        for i in range(4):
            into[n, :, i * width : (i + 1) * width] = got[feed, i].astype(F32)
        save(n, 3).start()
        for i in range(4):
            down[n, i * part : (i + 1) * part, :] = got[feed, 4 + i].astype(F32)
        save(n, 4).start()
        bias[n] = sums[attn, 0:3, :part]
        for i in range(3):
            into_b[n : n + 1, i * 128 : (i + 1) * 128] = sums[feed, i : i + 1, :]
        down_b[n : n + 1, :] = sums[feed, 3:4, :part]
        for k in range(2):
            gain[n, k : k + 1, :] = sums[2 * n + k, 4:5, :part]
            offset[n, k : k + 1, :] = sums[2 * n + k, 5:6, :part]
    for n in range(layers):
        for i in range(5):
            save(n, i).wait()
    final_o[...] = final[...]
    igrad_o[...] = igrad[...]


def spread_out(got, part, part_h):
    final, igrad, shares, sums = got["final_o"], got["igrad_o"], got["all_w"], got["all_s"]
    layers, width = shares.shape[0] // 2, shares.shape[3]
    vmem = pl.BlockSpec(memory_space=pltpu.VMEM)
    hbm = pl.BlockSpec(memory_space=pl.ANY)
    outs = [
        (vmem, final.shape, BF),
        (vmem, igrad.shape, F32),
        (hbm, (layers, part, 3 * width), F32),
        (vmem, (layers, 3, part), F32),
        (hbm, (layers, part, width), F32),
        (hbm, (layers, part, width), F32),
        (hbm, (layers, part, 4 * width), F32),
        (vmem, (layers, part_h), F32),
        (hbm, (layers, part_h, width), F32),
        (vmem, (layers, part), F32),
        (vmem, (layers, 2, part), F32),
        (vmem, (layers, 2, part), F32),
    ]
    return pl.pallas_call(
        spread_kernel,
        out_shape=tuple(jax.ShapeDtypeStruct(shape, kind) for _, shape, kind in outs),
        in_specs=[vmem, vmem, hbm, vmem],
        out_specs=tuple(where for where, _, _ in outs),
        scratch_shapes=[
            pltpu.VMEM(shares.shape, BF),
            *[pltpu.VMEM(outs[i][1], F32) for i in (2, 4, 5, 6, 8)],
            pltpu.SemaphoreType.DMA((2 * layers,)),
            pltpu.SemaphoreType.DMA((layers, 5)),
        ],
        compiler_params=pltpu.CompilerParams(vmem_limit_bytes=62 * 1024 * 1024),
        name="spread",
    )(final, igrad, shares, sums)


def shards(
    pages_in,
    coords,
    boxes,
    qkv_weight,
    attn_bias,
    pos_weight,
    out_weight,
    ffn_in,
    ffn_in_bias,
    ffn_out,
    ffn_out_bias,
    ln_gain,
    ln_bias,
    cotangent,
):
    groups = lax.axis_size("dp")
    s = lax.axis_index("section")
    layer = s // 2
    is_attn = s % 2 == 0
    micro, length, width = pages_in.shape
    hidden = ffn_in.shape[2]
    part = width // groups
    part_h = hidden // groups

    def pick(array):
        return lax.dynamic_index_in_dim(array, layer, 0, keepdims=False)

    inputs = {
        "pages": pages_in,
        "cot": cotangent,
        "coords": coords,
        "boxes": boxes.transpose(0, 2, 1),
        "waves": turns_per_unit(width),
    }
    if groups == 8:
        inputs.update(
            qkv_w=qkv_weight,
            pos_w=pos_weight,
            out_w=out_weight,
            in_w=ffn_in,
            down_w=ffn_out,
            attn_b=attn_bias.transpose(1, 0, 2),
            in_b=ffn_in_bias,
            down_b=ffn_out_bias,
            gain_w=ln_gain,
            offset_w=ln_bias,
        )
        got = pipeline(True, hidden, inputs)
        return spread_out(got, part, part_h)

    norm_row = s % 2
    gain_own = lax.dynamic_index_in_dim(pick(ln_gain), norm_row, 0, keepdims=False)
    offset_own = lax.dynamic_index_in_dim(pick(ln_bias), norm_row, 0, keepdims=False)
    own_a = jnp.where(
        is_attn, jnp.concatenate([pick(qkv_weight), pick(pos_weight)], axis=1), pick(ffn_in)
    )
    own_b = jnp.where(
        is_attn, jnp.pad(pick(out_weight), ((0, part_h - part), (0, 0))), pick(ffn_out)
    )
    wa = lax.all_gather(own_a, "dp", axis=0, tiled=True)
    wb_all = lax.all_gather(own_b, "dp", axis=0, tiled=False)
    wb = jnp.where(
        is_attn,
        jnp.pad(wb_all[:, :part].reshape(width, width), ((0, hidden - width), (0, 0))),
        wb_all.reshape(hidden, width),
    )
    bias_own = jnp.where(
        is_attn,
        jnp.pad(pick(attn_bias).reshape(-1), (0, part_h - 3 * part)),
        pick(ffn_in_bias),
    )
    vec_own = jnp.concatenate([bias_own, pick(ffn_out_bias), gain_own, offset_own])
    vec_all = lax.all_gather(vec_own, "dp", axis=0, tiled=False).astype(F32)
    first = jnp.where(
        is_attn,
        jnp.pad(
            vec_all[:, : 3 * part].reshape(groups, 3, part).transpose(1, 0, 2).reshape(-1),
            (0, hidden - 3 * width),
        ),
        vec_all[:, :part_h].reshape(-1),
    )
    rest = vec_all[:, part_h:].reshape(groups, 3, part).transpose(1, 0, 2).reshape(-1)
    inputs["vec_in"] = jnp.pad(
        jnp.stack([first, jnp.pad(rest, (0, hidden - 3 * width))]), ((0, 6), (0, 0))
    )
    wide_blocks = wa.reshape(width, hidden // width, width).transpose(1, 0, 2)
    inputs["w_in"] = jnp.concatenate([wide_blocks.reshape(hidden, width), wb], axis=0)
    got = pipeline(False, hidden, inputs)
    final, igrad, dw, small = got["final_o"], got["igrad_o"], got["dw_o"], got["small_o"]
    dwa = dw[:hidden].reshape(hidden // width, width, width).transpose(1, 0, 2)
    dwa = dwa.reshape(width, hidden)
    dwb = dw[hidden:]

    shard_a = lax.psum_scatter(dwa, "dp", scatter_dimension=0, tiled=True)
    dwb_cut = jnp.where(
        is_attn,
        jnp.pad(
            dwb[:width].reshape(groups, part, width), ((0, 0), (0, part_h - part), (0, 0))
        ),
        dwb.reshape(groups, part_h, width),
    )
    shard_b = lax.psum_scatter(dwb_cut, "dp", scatter_dimension=0, tiled=True).reshape(
        part_h, width
    )
    small_first = jnp.where(
        is_attn,
        jnp.pad(
            small[0, : 3 * width].reshape(3, groups, part).transpose(1, 0, 2).reshape(groups, -1),
            ((0, 0), (0, part_h - 3 * part)),
        ),
        small[0].reshape(groups, part_h),
    )
    small_rest = (
        small[1, : 3 * width].reshape(3, groups, part).transpose(1, 0, 2).reshape(groups, -1)
    )
    small_cut = jnp.concatenate([small_first, small_rest], axis=1)
    shard_s = lax.psum_scatter(small_cut, "dp", scatter_dimension=0, tiled=True).reshape(-1)

    all_a = lax.all_gather(shard_a, "section", axis=0, tiled=False)
    all_b = lax.all_gather(shard_b, "section", axis=0, tiled=False)
    all_s = lax.all_gather(shard_s, "section", axis=0, tiled=False)

    attn_a, feed_a = all_a[0::2], all_a[1::2]
    attn_s, feed_s = all_s[0::2], all_s[1::2]
    rest_s = all_s[:, part_h:].reshape(-1, 2, 3, part)
    return (
        final,
        igrad,
        attn_a[:, :, : 3 * width].astype(F32),
        attn_s[:, : 3 * part].reshape(-1, 3, part),
        attn_a[:, :, 3 * width :].astype(F32),
        all_b[0::2, :part].astype(F32),
        feed_a.astype(F32),
        feed_s[:, :part_h],
        all_b[1::2].astype(F32),
        feed_s[:, part_h : part_h + part],
        rest_s[:, :, 1],
        rest_s[:, :, 2],
    )


def solution(mesh):
    in_specs = (
        P("dp", None, None),
        P("dp", None, None),
        P("dp", None, None),
        P(None, "dp", None),
        P(None, None, "dp"),
        P(None, "dp", None),
        P(None, "dp", None),
        P(None, "dp", None),
        P(None, "dp"),
        P(None, "dp", None),
        P(None, "dp"),
        P(None, None, "dp"),
        P(None, None, "dp"),
        P("dp", None, None),
    )
    out_specs = (
        P("dp", "section", None),
        P("dp", "section", None),
        P(None, "dp", None),
        P(None, None, "dp"),
        P(None, "dp", None),
        P(None, "dp", None),
        P(None, "dp", None),
        P(None, "dp"),
        P(None, "dp", None),
        P(None, "dp"),
        P(None, None, "dp"),
        P(None, None, "dp"),
    )
    return jax.shard_map(shards, mesh=mesh, in_specs=in_specs, out_specs=out_specs, check_vma=False)
```

```python
from functools import partial
import math

import jax
import jax.numpy as jnp
import numpy as np
from jax import lax
from jax.experimental import pallas as pl
from jax.experimental.pallas import tpu as pltpu
from jax.sharding import PartitionSpec as P

HEAD_DIM = 64
PAIR = 2 * HEAD_DIM
EPSILON = 1e-06
NEGATIVE = -1e30
LOG2E = math.log2(math.e)
SCORE_SCALE = 1.0 / math.sqrt(3.0 * HEAD_DIM)
MESH = pl.DeviceIdType.MESH
BF = jnp.bfloat16
F32 = jnp.float32


def dot_nn(a, b):
    return jnp.dot(a, b, preferred_element_type=F32)


def dot_nt(a, b):
    return lax.dot_general(a, b, (((1,), (1,)), ((), ())), preferred_element_type=F32)


def dot_tn(a, b):
    return lax.dot_general(a, b, (((0,), (0,)), ((), ())), preferred_element_type=F32)


def gelu_and_slope(x):
    bell = jnp.exp2(x * x * (-0.5 * LOG2E))
    t = 1.0 / (1.0 + (0.3275911 / math.sqrt(2.0)) * jnp.abs(x))
    series = t * (
        0.254829592
        + t * (-0.284496736 + t * (1.421413741 + t * (-1.453152027 + t * 1.061405429)))
    )
    tail = 0.5 * series * bell
    cdf = jnp.where(x >= 0.0, 1.0 - tail, tail)
    return x * cdf, cdf + x * bell * (1.0 / math.sqrt(2.0 * math.pi))


TURN_TERMS = [
    (-1.0) ** n * (2.0 * math.pi) ** (2 * n + 1) / math.factorial(2 * n + 1) for n in range(6)
]


def sine_of_turns(turns):
    rest = turns - jnp.floor(turns + 0.5)
    size = 0.25 - jnp.abs(jnp.abs(rest) - 0.25)
    square = size * size
    series = TURN_TERMS[5]
    for term in TURN_TERMS[4::-1]:
        series = series * square + term
    return jnp.where(rest < 0.0, -size, size) * series


def turns_per_unit(width):
    quarter = width // 4
    wave = 10000.0 ** (-np.arange(quarter) / quarter) / (2.0 * math.pi)
    table = np.zeros((2, width))
    table[0, : 2 * quarter] = np.tile(wave, 2)
    table[1, 2 * quarter :] = np.tile(wave, 2)
    return jnp.asarray(table, F32)


class Refs:
    def __init__(self, names, refs):
        self.__dict__.update(zip(names, refs, strict=True))


def pipeline_kernel(names, rows, fused, *refs):
    r = Refs(names, refs)
    h_in, g_in, h_out, g_out = r.h_in, r.g_in, r.h_out, r.g_out
    saved, qkvp, kplus, context, zed, rstd = r.saved, r.qkvp, r.kplus, r.context, r.zed, r.rstd
    db, w, place, hide = r.db, r.w, r.place, r.hide
    vec, colsum = r.vec, r.colsum
    sections = lax.axis_size("section")
    s = lax.axis_index("section")
    kind = s % 2
    layer = s // 2
    last = sections - 1
    micro, length, width = h_in.shape
    hidden = w.shape[0] // 2
    chunks = length // rows
    big = 2 * rows
    bigs = length // big
    quarter = length // sections
    pairs = width // PAIR
    blocks = hidden // width
    is_attn = kind == 0
    is_feed = kind == 1

    if fused:
        d = lax.axis_index("dp")
        part = width // 8
        half = part // 2
        core, cx, cy = d % 2, (d // 2) % 2, d // 4
        chip = d // 2
        near_c = d + 1 - 2 * core
        near_x = d + 2 - 4 * cx
        near_y = d + 4 - 8 * cy
        diag = near_x + 4 - 8 * cy
        units = 5 + 3 * kind
        tail_units = 1 + 3 * kind

        def peer(t):
            tc, tx, ty = t % 2, (t // 2) % 2, t // 4
            return (
                d + tc * (1 - 2 * core) + 2 * tx * (1 - 2 * cx) + 4 * ty * (1 - 2 * cy)
            )

    barrier = pltpu.get_barrier_semaphore()
    for by in range(1, sections):
        pl.semaphore_signal(
            barrier, inc=1, device_id={"section": (s + by) % sections}, device_id_type=MESH
        )
    if fused:
        for t in range(1, 8):
            pl.semaphore_signal(barrier, inc=1, device_id={"dp": peer(t)}, device_id_type=MESH)

    def to_section(source, target, send, recv, at):
        return pltpu.make_async_remote_copy(
            src_ref=source,
            dst_ref=target,
            send_sem=send,
            recv_sem=recv,
            device_id={"section": at},
            device_id_type=MESH,
        )

    def to_near(source, target, send, recv, near):
        return pltpu.make_async_remote_copy(
            src_ref=source,
            dst_ref=target,
            send_sem=send,
            recv_sem=recv,
            device_id={"dp": near},
            device_id_type=MESH,
        )

    def span_of(c, size=rows):
        return pl.ds(pl.multiple_of(c * size, size), size)

    def local_in(source, target, sem, m, c):
        span = span_of(c)
        return pltpu.make_async_copy(source.at[m, span], target.at[m, span], sem.at[m, c])

    def hop(source, target, send, recv, m, c, by):
        span = span_of(c)
        return to_section(
            source.at[m, span],
            target.at[m, span],
            send.at[m, c],
            recv.at[m, c],
            (s + by + sections) % sections,
        )

    def share(source, target, send, recv, m, j):
        span = pl.ds(pl.multiple_of(j * quarter, quarter), quarter)
        return to_section(source.at[m, span], target.at[m], send.at[m, j], recv.at[m], j)

    @pl.when(s == 0)
    def _():
        for m in range(micro):
            for c in range(chunks):
                local_in(r.pages, h_in, r.frecv, m, c).start()

    @pl.when(s == last)
    def _():
        for m in range(micro):
            for c in range(chunks):
                local_in(r.cot, g_in, r.brecv, m, c).start()

    def wait_h(m, c):
        @pl.when(s == 0)
        def _():
            local_in(r.pages, h_in, r.frecv, m, c).wait()

        @pl.when(s != 0)
        def _():
            hop(h_out, h_in, r.fsend, r.frecv, m, c, 1).wait_recv()

    def wait_g(m, c):
        @pl.when(s == last)
        def _():
            local_in(r.cot, g_in, r.brecv, m, c).wait()

        @pl.when(s != last)
        def _():
            hop(g_out, g_in, r.bsend, r.brecv, m, c, -1).wait_recv()

    def send_h(m, c):
        @pl.when(s != last)
        def _():
            hop(h_out, h_in, r.fsend, r.frecv, m, c, 1).start()


    def send_g(m, c):
        @pl.when(s != 0)
        def _():
            hop(g_out, g_in, r.bsend, r.brecv, m, c, -1).start()

        @pl.when(jnp.logical_and(s == 0, c != s))
        def _():
            share(g_out, r.ig_in, r.ig_send, r.ig_recv, m, c).start()

    def block_of(i):
        return w[i * width : (i + 1) * width, :]

    def spots():
        columns = lax.broadcasted_iota(jnp.int32, (1, width), 1)
        phase = jnp.where((columns // (width // 4)) % 2 == 1, 0.25, 0.0)
        tokens_at = lax.broadcasted_iota(jnp.int32, (length, r.boxes.shape[2]), 0)

        def page(m, _):
            turns = lax.dot_general(
                r.coords[m].astype(F32),
                r.waves[...],
                (((0,), (0,)), ((), ())),
                precision=lax.Precision.HIGHEST,
                preferred_element_type=F32,
            )
            place[m] = sine_of_turns(turns + phase).astype(BF)
            box = r.boxes[m]

            def hit(low, high):
                inside = jnp.logical_and(
                    tokens_at >= box[low : low + 1], tokens_at < box[high : high + 1]
                )
                return jnp.where(inside, 1.0, 0.0)

            covered = dot_nt(hit(0, 1), hit(2, 3))
            hide[m] = jnp.where(covered < 0.5, 0.0, NEGATIVE).astype(BF)
            return 0

        lax.fori_loop(0, micro, page, 0)

    if fused:

        def shard_rows(tail, i, shard, count, first=0):
            if tail:
                at = hidden + shard * (part + 3 * part * kind) + i * part + first
            else:
                at = i * width + shard * part + first
            return pl.ds(pl.multiple_of(at, half), count)

        def gather(tail, i, t, shard, near, count=None, first=0):
            span = shard_rows(tail, i, shard, count or part, first)
            u = 4 + i if tail else i
            return to_near(w.at[span], w.at[span], r.ag_send.at[u, t], r.ag_recv.at[u, t], near)

        def over_units(step):
            def head(i, _):
                step(False, i)
                return 0

            def rest(i, _):
                step(True, i)
                return 0

            lax.fori_loop(0, 4, head, 0)
            lax.fori_loop(0, tail_units, rest, 0)

        def own_copy(source, tail, i):
            u = 4 + i if tail else i
            return pltpu.make_async_copy(
                source, w.at[shard_rows(tail, i, d, part)], r.own_sem.at[u]
            )

        @pl.when(is_attn)
        def _():
            for i in range(3):
                own_copy(
                    r.qkv_w.at[layer, :, pl.ds(i * width, width)], False, i
                ).start()
            own_copy(r.pos_w.at[layer], False, 3).start()
            own_copy(r.out_w.at[layer], True, 0).start()

        @pl.when(is_feed)
        def _():
            for i in range(4):
                own_copy(r.in_w.at[layer, :, pl.ds(i * width, width)], False, i).start()
            for i in range(4):
                own_copy(r.down_w.at[layer, pl.ds(i * part, part), :], True, i).start()

        def first_round(tail, i):
            own_copy(r.pos_w.at[layer], tail, i).wait()
            gather(tail, i, 0, d, near_x).start()
            gather(tail, i, 1, d, near_y).start()
            gather(tail, i, 2, d, near_c).start()

        def second_round(tail, i):
            gather(tail, i, 0, near_x, near_x).wait_recv()
            gather(tail, i, 3, near_x, near_y, half, 0).start()
            gather(tail, i, 5, near_x, near_c).start()
            gather(tail, i, 1, near_y, near_y).wait_recv()
            gather(tail, i, 4, near_y, near_x, half, half).start()
            gather(tail, i, 6, near_y, near_c).start()

        def third_round(tail, i):
            gather(tail, i, 3, diag, near_y, half, 0).wait_recv()
            gather(tail, i, 4, diag, near_x, half, half).wait_recv()
            gather(tail, i, 7, diag, near_c).start()

        def last_round(tail, i):
            flip = 1 - 2 * core
            gather(tail, i, 2, near_c, near_c).wait_recv()
            gather(tail, i, 5, near_x + flip, near_c).wait_recv()
            gather(tail, i, 6, near_y + flip, near_c).wait_recv()
            gather(tail, i, 7, diag + flip, near_c).wait_recv()

        def gather_sent(tail, i):
            for t, (shard, near) in enumerate(((d, near_x), (d, near_y), (d, near_c))):
                gather(tail, i, t, shard, near).wait_send()
            gather(tail, i, 3, near_x, near_y, half, 0).wait_send()
            gather(tail, i, 4, near_y, near_x, half, half).wait_send()
            gather(tail, i, 5, near_x, near_c).wait_send()
            gather(tail, i, 6, near_y, near_c).wait_send()
            gather(tail, i, 7, diag, near_c).wait_send()

        def of_layer(ref):
            whole = ref[...].astype(F32)
            row = whole[0:1]
            for i in range(1, whole.shape[0]):
                row = jnp.where(layer == i, whole[i : i + 1], row)
            return row

        mine_v = r.vec_all.at[d]
        pair = jnp.concatenate([r.gain_w[layer], r.offset_w[layer]], axis=0).astype(F32)
        mine_v[3:4, :part] = of_layer(r.down_b)
        mine_v[4:5, :part] = jnp.where(is_attn, pair[0:1], pair[1:2])
        mine_v[5:6, :part] = jnp.where(is_attn, pair[2:3], pair[3:4])

        @pl.when(is_attn)
        def _():
            for i in range(3):
                mine_v[i : i + 1, :part] = of_layer(r.attn_b.at[i])

        @pl.when(is_feed)
        def _():
            row = of_layer(r.in_b)
            for i in range(3):
                mine_v[i : i + 1, :] = row[:, i * 128 : (i + 1) * 128]

        def vec_copy(t, source):
            return to_near(
                mine_v, r.vec_all.at[source], r.v_send.at[t - 1], r.v_recv.at[t - 1], peer(t)
            )

        pl.semaphore_wait(barrier, sections - 1 + 7)
        for t in range(1, 8):
            vec_copy(t, d).start()
        over_units(first_round)

        @pl.when(is_attn)
        def _():
            spots()

        for t in range(1, 8):
            vec_copy(t, peer(t)).wait_recv()
        for dest in range(8):
            row = r.vec_all[dest]
            at = dest * part

            @pl.when(is_attn)
            def _(row=row, at=at):
                for i in range(3):
                    vec[0:1, i * width + at : i * width + at + part] = row[i : i + 1, :part]

            @pl.when(is_feed)
            def _(row=row, dest=dest):
                for i in range(3):
                    lane_at = dest * 4 * part + i * 128
                    vec[0:1, lane_at : lane_at + 128] = row[i : i + 1, :]

            for i in range(3):
                vec[1:2, i * width + at : i * width + at + part] = row[3 + i : 4 + i, :part]

        over_units(second_round)

        def rounds(tail, i):
            third_round(tail, i)
            last_round(tail, i)

        def over_head(step):
            def head(i, _):
                step(False, i)
                return 0

            lax.fori_loop(0, 4, head, 0)

        @pl.when(is_attn)
        def _():
            over_head(third_round)
            over_head(last_round)

        @pl.when(is_feed)
        def _():
            over_units(third_round)
            over_units(last_round)
    else:
        whole = pltpu.make_async_copy(r.w_in, w, r.own_sem)
        whole.start()
        vec[...] = r.vec_in[...]
        spots()
        pl.semaphore_wait(barrier, sections - 1)
        whole.wait()

    def norm_out(m, c, summed, gain, offset, size=rows):
        span = span_of(c, size)
        mean = jnp.mean(summed, axis=1, keepdims=True)
        center = summed - mean
        spread = jnp.mean(center * center, axis=1, keepdims=True)
        inv = lax.rsqrt(spread + EPSILON)
        z = center * inv
        zed[m, span] = z
        rstd[m, span] = jnp.broadcast_to(inv, (size, 128))
        h_out[m, span] = (z * gain + offset).astype(BF)
        for i in range(size // rows):
            send_h(m, c * (size // rows) + i)

    def norm_back(m, c, gain, bias_at, size=rows):
        span = span_of(c, size)
        g = g_in[m, span].astype(F32)
        z = zed[m, span]
        inv = rstd[m, span][:, :1]
        u = g * gain
        mean_u = jnp.mean(u, axis=1, keepdims=True)
        mean_uz = jnp.mean(u * z, axis=1, keepdims=True)
        grad = (u - mean_u - z * mean_uz) * inv
        low = grad.astype(BF)
        db[m, span] = low
        colsum[1:2, width : 2 * width] += jnp.sum(g * z, axis=0, keepdims=True)
        colsum[1:2, 2 * width : 3 * width] += jnp.sum(g, axis=0, keepdims=True)
        at = bias_at
        colsum[at[0] : at[0] + 1, at[1] : at[1] + width] += jnp.sum(
            low.astype(F32), axis=0, keepdims=True
        )
        return grad, low

    colsum[...] = jnp.zeros_like(colsum)
    gain = vec[1:2, width : 2 * width]
    offset = vec[1:2, 2 * width : 3 * width]

    @pl.when(is_attn)
    def _():
        lane = lax.broadcasted_iota(jnp.int32, (1, PAIR), 1) < HEAD_DIM
        lane2 = lax.broadcasted_iota(jnp.int32, (1, 2 * PAIR), 1) % PAIR < HEAD_DIM

        def places(idx, _):
            m, c = idx // bigs, idx % bigs
            span = span_of(c, big)
            qkvp[m, span, 3 * width :] = dot_nn(place[m, span], block_of(3)).astype(BF)
            return 0

        lax.fori_loop(0, micro * bigs, places, 0)

        def forward(m, _):
            def project(c, _):
                span = span_of(c, big)
                wait_h(m, 2 * c)
                wait_h(m, 2 * c + 1)
                h = h_in[m, span]
                q = dot_nn(h, block_of(0)) + vec[0:1, :width]
                qkvp[m, span, :width] = q.astype(BF)
                k = dot_nn(h, block_of(1)).astype(BF)
                qkvp[m, span, width : 2 * width] = k
                kplus[m, span] = (
                    k.astype(F32) + qkvp[m, span, 3 * width :].astype(F32)
                ).astype(BF)
                v = dot_nn(h, block_of(2)) + vec[0:1, width : 2 * width]
                qkvp[m, span, 2 * width : 3 * width] = v.astype(BF)
                return 0

            lax.fori_loop(0, bigs, project, 0)

            def heads(t, _):
                off = pl.multiple_of(t * PAIR, PAIR)
                left = jnp.concatenate(
                    [qkvp[m, :, pl.ds(off, PAIR)], qkvp[m, :, pl.ds(off + 3 * width, PAIR)]],
                    axis=1,
                )
                right = jnp.concatenate(
                    [kplus[m, :, pl.ds(off, PAIR)], qkvp[m, :, pl.ds(off + width, PAIR)]],
                    axis=1,
                )
                v = qkvp[m, :, pl.ds(off + 2 * width, PAIR)]
                bias = hide[m].astype(F32)
                mixed = []
                blank = jnp.zeros_like(left)
                both = jnp.concatenate(
                    [jnp.where(lane2, left, blank), jnp.where(lane2, blank, left)], axis=0
                )
                raw = dot_nt(both, right)
                for side in range(2):
                    score = raw[side * length : (side + 1) * length] * (SCORE_SCALE * LOG2E) + bias
                    top = jnp.max(score, axis=1, keepdims=True)
                    power = jnp.exp2(score - top)
                    total = jnp.sum(power, axis=1, keepdims=True)
                    prob = (power * (1.0 / total)).astype(BF)
                    at = pl.multiple_of((2 * t + side) * length, length)
                    saved[m, :, pl.ds(at, length)] = prob
                    mixed.append(dot_nn(prob, v))
                context[m, :, pl.ds(off, PAIR)] = jnp.where(lane, mixed[0], mixed[1]).astype(BF)
                return 0

            lax.fori_loop(0, pairs, heads, 0, unroll=2)

            if fused:

                @pl.when(m == 0)
                def _():
                    rounds(True, 0)

            def attend(c, _):
                span = span_of(c, big)
                branch = dot_nn(context[m, span], block_of(4))
                summed = h_in[m, span].astype(F32) + branch + vec[0:1, 2 * width : 3 * width]
                norm_out(m, c, summed, gain, offset, big)
                return 0

            lax.fori_loop(0, bigs, attend, 0)
            return 0

        lax.fori_loop(0, micro, forward, 0)

        def backward(m, _):
            def enter(c, _):
                span = span_of(c, big)
                wait_g(m, 2 * c)
                wait_g(m, 2 * c + 1)
                grad, low = norm_back(m, c, gain, (0, 2 * width), big)
                zed[m, span] = grad
                g_in[m, span] = dot_nt(low, block_of(4)).astype(BF)
                return 0

            lax.fori_loop(0, bigs, enter, 0)

            def heads(t, _):
                off = pl.multiple_of(t * PAIR, PAIR)
                left = jnp.concatenate(
                    [qkvp[m, :, pl.ds(off, PAIR)], qkvp[m, :, pl.ds(off + 3 * width, PAIR)]],
                    axis=1,
                )
                right = jnp.concatenate(
                    [kplus[m, :, pl.ds(off, PAIR)], qkvp[m, :, pl.ds(off + width, PAIR)]],
                    axis=1,
                )
                v = qkvp[m, :, pl.ds(off + 2 * width, PAIR)]
                grad_c = g_in[m, :, pl.ds(off, PAIR)]
                blank = jnp.zeros_like(grad_c)
                both = jnp.concatenate(
                    [jnp.where(lane, grad_c, blank), jnp.where(lane, blank, grad_c)], axis=0
                )
                at = pl.multiple_of(2 * t * length, 2 * length)
                prob = saved[m, :, pl.ds(at, 2 * length)]
                grad_p = dot_nt(both, v)
                grad_s = []
                for side in range(2):
                    wide_p = prob[:, side * length : (side + 1) * length].astype(F32)
                    part_p = grad_p[side * length : (side + 1) * length]
                    dot_row = jnp.sum(wide_p * part_p, axis=1, keepdims=True)
                    grad_s.append((wide_p * (part_p - dot_row)).astype(BF))
                got_v = dot_tn(prob, grad_c)
                got_l = dot_nn(jnp.concatenate(grad_s, axis=0), right)
                got_r = dot_tn(jnp.concatenate(grad_s, axis=1), left)
                grad_v = jnp.where(lane, got_v[:length], got_v[length:]).astype(BF)
                grad_l = jnp.where(lane2, got_l[:length], got_l[length:])
                grad_r = jnp.where(lane2, got_r[:length], got_r[length:])
                grad_q = (grad_l[:, :PAIR] * SCORE_SCALE).astype(BF)
                grad_k = ((grad_r[:, :PAIR] + grad_r[:, PAIR:]) * SCORE_SCALE).astype(BF)
                grad_pl = ((grad_l[:, PAIR:] + grad_r[:, :PAIR]) * SCORE_SCALE).astype(BF)
                qkvp[m, :, pl.ds(off, PAIR)] = grad_q
                qkvp[m, :, pl.ds(off + width, PAIR)] = grad_k
                qkvp[m, :, pl.ds(off + 2 * width, PAIR)] = grad_v
                qkvp[m, :, pl.ds(off + 3 * width, PAIR)] = grad_pl
                colsum[0:1, pl.ds(off, PAIR)] += jnp.sum(
                    grad_q.astype(F32), axis=0, keepdims=True
                )
                colsum[0:1, pl.ds(off + width, PAIR)] += jnp.sum(
                    grad_v.astype(F32), axis=0, keepdims=True
                )
                return 0

            lax.fori_loop(0, pairs, heads, 0, unroll=2)

            def leave(c, _):
                span = span_of(c, big)
                total = zed[m, span]
                for i in range(3):
                    total = total + dot_nt(
                        qkvp[m, span, i * width : (i + 1) * width], block_of(i)
                    )
                g_out[m, span] = total.astype(BF)
                send_g(m, 2 * c)
                send_g(m, 2 * c + 1)
                return 0

            lax.fori_loop(0, bigs, leave, 0)
            return 0

        lax.fori_loop(0, micro, backward, 0)

    @pl.when(is_feed)
    def _():
        def forward(idx, _):
            m, c = idx // chunks, idx % chunks
            span = span_of(c)
            wait_h(m, c)
            h = h_in[m, span]
            summed = h.astype(F32) + vec[1:2, :width]
            for f in range(blocks):
                at = f * width
                inner = dot_nn(h, block_of(f)) + vec[0:1, at : at + width]
                value, slope = gelu_and_slope(inner)
                low = value.astype(BF)
                saved[m, span, at : at + width] = low
                saved[m, span, hidden + at : hidden + at + width] = slope.astype(BF)
                summed = summed + dot_nn(low, block_of(blocks + f))
            norm_out(m, c, summed, gain, offset)
            return 0

        def backward(m, c, size):
            span = span_of(c, size)
            hops = size // rows
            for i in range(hops):
                wait_g(m, c * hops + i)
            total, low = norm_back(m, c, gain, (1, 0), size)
            for f in range(blocks):
                at = f * width
                grad_a = dot_nt(low, block_of(blocks + f)).astype(BF).astype(F32)
                slope = saved[m, span, hidden + at : hidden + at + width].astype(F32)
                grad_i = (grad_a * slope).astype(BF)
                saved[m, span, hidden + at : hidden + at + width] = grad_i
                colsum[0:1, at : at + width] += jnp.sum(
                    grad_i.astype(F32), axis=0, keepdims=True
                )
                total = total + dot_nt(grad_i, block_of(f))
            g_out[m, span] = total.astype(BF)
            for i in range(hops):
                send_g(m, c * hops + i)

        def step(i, _):
            page, c = i // chunks, i % chunks
            turn = jnp.where(s == last, page % 2, page // micro)
            m = jnp.where(s == last, page // 2, page % micro)

            @pl.when(turn == 0)
            def _():
                forward(m * chunks + c, 0)

            @pl.when(jnp.logical_and(turn == 1, s != last))
            def _():
                backward(m, c, rows)

            @pl.when(jnp.logical_and(jnp.logical_and(turn == 1, s == last), c % 2 == 0))
            def _():
                backward(m, c // 2, big)

            return 0

        lax.fori_loop(0, 2 * micro * chunks, step, 0)

    tokens = micro * length
    stage = r.stage

    def tall(ref, at):
        return ref[:, :, pl.ds(at, width)].reshape(tokens, width)

    if fused:
        table = r.table
        low_half, high_half = pl.ds(0, half), pl.ds(half, half)

        def add(target, other):
            return (target.astype(F32) + other.astype(F32)).astype(BF)

        def give(e, by_chip):
            slot = e % 2
            return to_near(
                stage.at[slot],
                table.at[pl.ds(4, 4), e - 4] if by_chip else table.at[e],
                r.p0_send.at[slot],
                r.p0_recv.at[e],
                near_c,
            )

        def emit(e, value, by_chip):
            slot = e % 2

            @pl.when(e >= 2)
            def _():
                give(e, by_chip).wait_send()

            low = value.astype(BF)
            if by_chip:
                sides = [low[: 4 * part].reshape(4, part, width), low[4 * part :].reshape(4, part, width)]
            else:
                grid = low.reshape(4, 2, part, width)
                sides = [grid[:, 0], grid[:, 1]]
            stage[slot] = jnp.where(core == 0, sides[1], sides[0])
            give(e, by_chip).start()
            kept = jnp.where(core == 0, sides[0], sides[1])
            if by_chip:
                for j in range(4):
                    at = pl.multiple_of(((4 + j) * 4 + e - 4) * part, part)
                    w[pl.ds(at, part), :] = kept[j]
            else:
                at = pl.multiple_of(e * 4 * part, 4 * part)
                w[pl.ds(at, 4 * part), :] = kept.reshape(4 * part, width)

        def finish(count, by_chip):
            give(count - 2, by_chip).wait_send()
            give(count - 1, by_chip).wait_send()

        def one_x(u, y):
            return to_near(
                table.at[u, 2 * y + 1 - cx, low_half],
                r.land_x.at[u, y],
                r.p1x_send.at[u, y],
                r.p1x_recv.at[u, y],
                near_x,
            )

        def one_y(u):
            return to_near(
                table.at[u, pl.ds(2 - 2 * cy, 2), high_half],
                r.land_y.at[u],
                r.p1y_send.at[u],
                r.p1y_recv.at[u],
                near_y,
            )

        def two_y(u):
            return to_near(
                table.at[u, 2 - 2 * cy + cx, low_half],
                r.land_y2.at[u],
                r.p2y_send.at[u],
                r.p2y_recv.at[u],
                near_y,
            )

        def two_x(u):
            return to_near(
                table.at[u, 2 * cy + 1 - cx, high_half],
                r.land_x2.at[u],
                r.p2x_send.at[u],
                r.p2x_recv.at[u],
                near_x,
            )

        def left_own(u):
            return to_section(
                table.at[u, chip],
                r.all_w.at[s, u],
                r.left_send.at[s, u],
                r.all_recv.at[s, u],
                (s - 1 + sections) % sections,
            )

        def left_on(t, u):
            return to_section(
                r.all_w.at[t, u],
                r.all_w.at[t, u],
                r.left_send.at[t, u],
                r.all_recv.at[t, u],
                (s - 1 + sections) % sections,
            )

        def right_own(u):
            return to_section(
                table.at[u, chip],
                r.all_w.at[s, u],
                r.right_send.at[s, u],
                r.all_recv.at[s, u],
                (s + 1) % sections,
            )

        def right_on(t, u):
            return to_section(
                r.all_w.at[t, u],
                r.all_w.at[t, u],
                r.right_send.at[t, u],
                r.all_recv.at[t, u],
                (s + 1) % sections,
            )

        def mine(u):
            return pltpu.make_async_copy(table.at[u, chip], r.all_w.at[s, u], r.own_sem.at[u])

        def merge_core(u):
            @pl.when(u <= 4)
            def _():
                give(u, False).wait_recv()

            @pl.when(jnp.logical_and(u == 4, is_feed))
            def _():
                for e in range(5, 8):
                    give(e, True).wait_recv()

            at = pl.multiple_of(u * 4 * part, 4 * part)
            table[u] = add(table[u], w[pl.ds(at, 4 * part), :].reshape(4, part, width))
            for y in range(2):
                one_x(u, y).start()
            one_y(u).start()

        def merge_one(u):
            for y in range(2):
                one_x(u, y).wait_recv()
                at = 2 * y + cx
                table[u, at, :half] = add(table[u, at, :half], r.land_x[u, y])
            two_y(u).start()
            one_y(u).wait_recv()
            for x in range(2):
                at = 2 * cy + x
                table[u, at, half:] = add(table[u, at, half:], r.land_y[u, x])
            two_x(u).start()

        def merge_two(u):
            two_y(u).wait_recv()
            table[u, chip, :half] = add(table[u, chip, :half], r.land_y2[u])
            two_x(u).wait_recv()
            table[u, chip, half:] = add(table[u, chip, half:], r.land_x2[u])

            @pl.when(s != last)
            def _():
                right_own(u).start()

            @pl.when(s == last)
            def _():
                left_own(u).start()

            mine(u).start()

        late = 3 * kind

        def at_step(q, merge):
            @pl.when(jnp.logical_and(q >= 0, q < 4))
            def _():
                merge(q)

            @pl.when(jnp.logical_and(q >= 4 + late, q < units + late))
            def _():
                merge(q - late)

        def advance(q):
            at_step(q, merge_core)
            at_step(q - 2, merge_one)
            at_step(q - 4, merge_two)

        beyond = last - s
        hand_on = jnp.where(s > 0, 13 * (beyond // 2) + 8 * (beyond % 2), 0)

        def relay_left(k):
            @pl.when(jnp.logical_and(k >= 0, k < hand_on))
            def _():
                odd = (k % 13) // 8
                t = last - 2 * (k // 13) - odd
                copy = left_on(t, k % 13 - 8 * odd)
                copy.wait_recv()
                copy.start()

        sm = r.small
        for dest in range(8):
            at = dest * part

            @pl.when(is_attn)
            def _(dest=dest, at=at):
                for i in range(3):
                    sm[dest, i : i + 1, :part] = colsum[
                        0:1, i * width + at : i * width + at + part
                    ]

            @pl.when(is_feed)
            def _(dest=dest):
                for i in range(3):
                    lane_at = dest * 4 * part + i * 128
                    sm[dest, i : i + 1, :] = colsum[0:1, lane_at : lane_at + 128]

            for i in range(3):
                sm[dest, 3 + i : 4 + i, :part] = colsum[
                    1:2, i * width + at : i * width + at + part
                ]

        def small_copy(t):
            return to_near(
                sm.at[peer(t)], r.small_in.at[t - 1], r.s_send.at[t - 1], r.s_recv.at[t - 1], peer(t)
            )

        def small_share(by):
            return to_section(
                r.small_sum,
                r.all_s.at[s],
                r.sz_send.at[by - 1],
                r.sz_recv.at[s],
                (s + by) % sections,
            )

        for t in range(1, 8):
            small_copy(t).start()
        over_units(gather_sent)
        for t in range(1, 8):
            vec_copy(t, d).wait_send()
    else:

        def flush(slot, at):
            return pltpu.make_async_copy(
                stage.at[slot], r.dw_o.at[pl.ds(at, width)], r.keep_sem.at[slot]
            )

        def emit(e, value, by_chip):
            slot = e % 2

            @pl.when(e >= 2)
            def _():
                flush(slot, 0).wait()

            stage[slot] = value.astype(BF)
            flush(slot, pl.multiple_of(e * width, width)).start()

        def finish(count, by_chip):
            flush(0, 0).wait()
            flush(1, 0).wait()

        def advance(u):
            pass

        def relay_left(k):
            pass

    @pl.when(is_attn)
    def _():
        def step(e, _):
            at = pl.multiple_of(e * width, width)
            emit(e, dot_tn(tall(h_in, 0), tall(qkvp, at)), False)
            advance(e - 1)
            return 0

        lax.fori_loop(0, 3, step, 0)
        emit(3, dot_tn(tall(place, 0), tall(qkvp, 3 * width)), False)
        advance(jnp.int32(2))
        emit(4, dot_tn(tall(context, 0), tall(db, 0)), False)
        advance(jnp.int32(3))
        finish(5, False)

    @pl.when(is_feed)
    def _():
        def step(e, _):
            at = pl.multiple_of(e * width + hidden, width)
            emit(e, dot_tn(tall(h_in, 0), tall(saved, at)), False)
            advance(e - 1)
            relay_left(e - 1)
            return 0

        lax.fori_loop(0, blocks, step, 0)

        def step_b(i, _):
            at = pl.multiple_of(i * width, width)
            emit(i + blocks, dot_tn(tall(saved, at), tall(db, 0)), True)
            advance(i + blocks - 1)
            relay_left(i + blocks - 1)
            return 0

        lax.fori_loop(0, blocks, step_b, 0)
        finish(2 * blocks, True)

    if not fused:
        r.small_o[...] = colsum[...]

        @pl.when(s == last)
        def _():
            for m in range(micro):
                for j in range(sections - 1):
                    share(h_out, r.fin_in, r.fin_send, r.fin_recv, m, j).start()
    else:

        def go_on(q, _):
            advance(q)
            relay_left(kind * q + (1 - kind) * (2 * q - 8))
            relay_left((1 - kind) * (2 * q - 7) - kind)

            @pl.when(jnp.logical_and(jnp.logical_and(is_feed, s < last), q >= 8))
            def _():
                left_own(q - 8).start()

            return 0

        for t in range(1, 8):
            small_copy(t).wait_recv()
        total = sm[d]
        for t in range(7):
            total = total + r.small_in[t]
        r.small_sum[...] = total
        for by in range(1, sections):
            small_share(by).start()
        lax.fori_loop(4 + late, units + late + 4, go_on, 0)

        def rest_left(k, _):
            relay_left(k)
            return 0

        lax.fori_loop(10 + 5 * kind, hand_on, rest_left, 0)

        @pl.when(jnp.logical_and(s > 0, s < last))
        def _():
            def own_left(u, _):
                left_own(u).start()
                return 0

            lax.fori_loop(7 * kind, units, own_left, 0)


        for by in range(1, sections):

            @pl.when(s >= by)
            def _(by=by):
                t = s - by

                def relay(u, _, by=by):
                    right_on(t, u).wait_recv()
                    if by == 2:
                        @pl.when(jnp.logical_and(s == last, u == 3))
                        def _():
                            for m in range(micro):
                                for j in range(sections - 1):
                                    share(h_out, r.fin_in, r.fin_send, r.fin_recv, m, j).start()

                    @pl.when(s != last)
                    def _():
                        right_on(t, u).start()

                    return 0

                lax.fori_loop(0, 5 + 3 * (t % 2), relay, 0)

        for by in range(1, sections):

            @pl.when(jnp.logical_and(s + by < sections, s == 0))
            def _(by=by):
                t = s + by

                def arrive(u, _):
                    left_on(t, u).wait_recv()
                    return 0

                lax.fori_loop(0, 5 + 3 * (t % 2), arrive, 0)

        for by in range(1, sections):
            t = (s + by) % sections
            to_section(
                r.small_sum, r.all_s.at[t], r.sz_send.at[by - 1], r.sz_recv.at[t], t
            ).wait_recv()
        r.all_s[s] = r.small_sum[...]

        for t in range(1, 8):
            small_copy(t).wait_send()
        for by in range(1, sections):
            small_share(by).wait_send()

        def sent(u, _):
            for y in range(2):
                one_x(u, y).wait_send()
            one_y(u).wait_send()
            two_y(u).wait_send()
            two_x(u).wait_send()
            mine(u).wait()

            @pl.when(s != last)
            def _():
                right_own(u).wait_send()

            @pl.when(s != 0)
            def _():
                left_own(u).wait_send()

            return 0

        lax.fori_loop(0, units, sent, 0)
        for by in range(1, sections):

            @pl.when(jnp.logical_and(s >= by, s != last))
            def _(by=by):
                t = s - by

                def relayed(u, _):
                    right_on(t, u).wait_send()
                    return 0

                lax.fori_loop(0, 5 + 3 * (t % 2), relayed, 0)

        for by in range(1, sections):

            @pl.when(jnp.logical_and(s + by < sections, s != 0))
            def _(by=by):
                t = s + by

                def relayed(u, _):
                    left_on(t, u).wait_send()
                    return 0

                lax.fori_loop(0, 5 + 3 * (t % 2), relayed, 0)

    for m in range(micro):
        for c in range(chunks):

            @pl.when(s != last)
            def _():
                hop(h_out, h_in, r.fsend, r.frecv, m, c, 1).wait_send()

            @pl.when(s != 0)
            def _():
                hop(g_out, g_in, r.bsend, r.brecv, m, c, -1).wait_send()

    @pl.when(s == last)
    def _():
        for m in range(micro):
            for j in range(sections - 1):
                share(h_out, r.fin_in, r.fin_send, r.fin_recv, m, j).wait_send()
            r.final_o[m] = h_out[m, (sections - 1) * quarter :]

    @pl.when(s != last)
    def _():
        for m in range(micro):
            share(h_out, r.fin_in, r.fin_send, r.fin_recv, m, 0).wait_recv()
            r.final_o[m] = r.fin_in[m]

    @pl.when(s == 0)
    def _():
        for m in range(micro):
            for j in range(1, sections):
                share(g_out, r.ig_in, r.ig_send, r.ig_recv, m, j).wait_send()
            r.igrad_o[m] = g_out[m, :quarter].astype(F32)

    @pl.when(s != 0)
    def _():
        for m in range(micro):
            share(g_out, r.ig_in, r.ig_send, r.ig_recv, m, 1).wait_recv()
            r.igrad_o[m] = r.ig_in[m].astype(F32)


def pipeline(fused, hidden, inputs):
    micro, length, width = inputs["pages"].shape
    sections = lax.axis_size("section")
    rows = length // sections
    chunks = length // rows
    quarter = length // sections
    heads = width // HEAD_DIM
    wide = max(2 * hidden, heads * length)
    part = width // 8
    half = part // 2
    hbm = pl.BlockSpec(memory_space=pl.ANY)
    vmem = pl.BlockSpec(memory_space=pltpu.VMEM)
    act = (micro, length, width)
    dma = pltpu.SemaphoreType.DMA
    spec = {name: hbm for name in inputs}
    for name in spec:
        if name not in ("pages", "cot", "w_in", "qkv_w", "pos_w", "out_w", "in_w", "down_w"):
            spec[name] = vmem
    outs = {
        "final_o": (vmem, (micro, quarter, width), BF),
        "igrad_o": (vmem, (micro, quarter, width), F32),
    }
    scratch = {
        "place": pltpu.VMEM(act, BF),
        "hide": pltpu.VMEM((micro, length, length), BF),
        "h_in": pltpu.VMEM(act, BF),
        "g_in": pltpu.VMEM(act, BF),
        "h_out": pltpu.VMEM(act, BF),
        "g_out": pltpu.VMEM(act, BF),
        "saved": pltpu.VMEM((micro, length, wide), BF),
        "qkvp": pltpu.VMEM((micro, length, 4 * width), BF),
        "kplus": pltpu.VMEM(act, BF),
        "context": pltpu.VMEM(act, BF),
        "zed": pltpu.VMEM(act, F32),
        "rstd": pltpu.VMEM((micro, length, 128), F32),
        "db": pltpu.VMEM(act, BF),
        "w": pltpu.VMEM((2 * hidden, width), BF),
        "vec": pltpu.VMEM((8, hidden), F32),
        "colsum": pltpu.VMEM((8, hidden), F32),
        "fin_in": pltpu.VMEM((micro, quarter, width), BF),
        "ig_in": pltpu.VMEM((micro, quarter, width), BF),
        "fsend": dma((micro, chunks)),
        "frecv": dma((micro, chunks)),
        "bsend": dma((micro, chunks)),
        "brecv": dma((micro, chunks)),
        "fin_send": dma((micro, sections)),
        "fin_recv": dma((micro,)),
        "ig_send": dma((micro, sections)),
        "ig_recv": dma((micro,)),
        "keep_sem": dma((2,)),
    }
    if fused:
        outs["all_w"] = (hbm, (sections, 8, part, width), BF)
        outs["all_s"] = (vmem, (sections, 8, 128), F32)
        scratch.update(
            stage=pltpu.VMEM((2, 4, part, width), BF),
            vec_all=pltpu.VMEM((8, 8, 128), F32),
            small=pltpu.VMEM((8, 8, 128), F32),
            small_in=pltpu.VMEM((7, 8, 128), F32),
            small_sum=pltpu.VMEM((8, 128), F32),
            table=pltpu.VMEM((8, 4, part, width), BF),
            land_x=pltpu.VMEM((8, 2, half, width), BF),
            land_y=pltpu.VMEM((8, 2, half, width), BF),
            land_x2=pltpu.VMEM((8, half, width), BF),
            land_y2=pltpu.VMEM((8, half, width), BF),
            own_sem=dma((8,)),
            ag_send=dma((8, 8)),
            ag_recv=dma((8, 8)),
            v_send=dma((7,)),
            v_recv=dma((7,)),
            s_send=dma((7,)),
            s_recv=dma((7,)),
            sz_send=dma((sections - 1,)),
            sz_recv=dma((sections,)),
            p0_send=dma((2,)),
            p0_recv=dma((8,)),
            p1x_send=dma((8, 2)),
            p1x_recv=dma((8, 2)),
            p1y_send=dma((8,)),
            p1y_recv=dma((8,)),
            p2x_send=dma((8,)),
            p2x_recv=dma((8,)),
            p2y_send=dma((8,)),
            p2y_recv=dma((8,)),
            left_send=dma((sections, 8)),
            right_send=dma((sections, 8)),
            all_recv=dma((sections, 8)),
        )
    else:
        outs["dw_o"] = (hbm, (2 * hidden, width), BF)
        outs["small_o"] = (vmem, (8, hidden), F32)
        scratch.update(stage=pltpu.VMEM((2, width, width), BF), own_sem=dma)
    names = [*inputs, *outs, *scratch]
    got = pl.pallas_call(
        partial(pipeline_kernel, names, rows, fused),
        out_shape=tuple(jax.ShapeDtypeStruct(shape, kind) for _, shape, kind in outs.values()),
        in_specs=list(spec.values()),
        out_specs=tuple(where for where, _, _ in outs.values()),
        scratch_shapes=list(scratch.values()),
        compiler_params=pltpu.CompilerParams(
            collective_id=0, has_side_effects=True, vmem_limit_bytes=63 * 1024 * 1024
        ),
        name="pipeline",
    )(*inputs.values())
    return dict(zip(outs, got, strict=True))


def spread_kernel(
    final,
    igrad,
    shares,
    sums,
    final_o,
    igrad_o,
    qkv_o,
    bias,
    pos_o,
    out_o,
    into_o,
    into_b,
    down_o,
    down_b,
    gain,
    offset,
    got,
    qkv,
    pos,
    out,
    into,
    down,
    load_sem,
    save_sem,
):
    layers, part, width = pos.shape

    def load(t):
        return pltpu.make_async_copy(shares.at[t], got.at[t], load_sem.at[t])

    def save(n, i):
        source, target = (
            (qkv, qkv_o),
            (pos, pos_o),
            (out, out_o),
            (into, into_o),
            (down, down_o),
        )[i]
        return pltpu.make_async_copy(source.at[n], target.at[n], save_sem.at[n, i])

    for t in range(2 * layers):
        load(t).start()
    for n in range(layers):
        attn, feed = 2 * n, 2 * n + 1
        load(attn).wait()
        for i in range(3):
            qkv[n, :, i * width : (i + 1) * width] = got[attn, i].astype(F32)
        save(n, 0).start()
        pos[n] = got[attn, 3].astype(F32)
        save(n, 1).start()
        out[n] = got[attn, 4].astype(F32)
        save(n, 2).start()
        load(feed).wait()
        for i in range(4):
            into[n, :, i * width : (i + 1) * width] = got[feed, i].astype(F32)
        save(n, 3).start()
        for i in range(4):
            down[n, i * part : (i + 1) * part, :] = got[feed, 4 + i].astype(F32)
        save(n, 4).start()
        bias[n] = sums[attn, 0:3, :part]
        for i in range(3):
            into_b[n : n + 1, i * 128 : (i + 1) * 128] = sums[feed, i : i + 1, :]
        down_b[n : n + 1, :] = sums[feed, 3:4, :part]
        for k in range(2):
            gain[n, k : k + 1, :] = sums[2 * n + k, 4:5, :part]
            offset[n, k : k + 1, :] = sums[2 * n + k, 5:6, :part]
    for n in range(layers):
        for i in range(5):
            save(n, i).wait()
    final_o[...] = final[...]
    igrad_o[...] = igrad[...]


def spread_out(got, part, part_h):
    final, igrad, shares, sums = got["final_o"], got["igrad_o"], got["all_w"], got["all_s"]
    layers, width = shares.shape[0] // 2, shares.shape[3]
    vmem = pl.BlockSpec(memory_space=pltpu.VMEM)
    hbm = pl.BlockSpec(memory_space=pl.ANY)
    outs = [
        (vmem, final.shape, BF),
        (vmem, igrad.shape, F32),
        (hbm, (layers, part, 3 * width), F32),
        (vmem, (layers, 3, part), F32),
        (hbm, (layers, part, width), F32),
        (hbm, (layers, part, width), F32),
        (hbm, (layers, part, 4 * width), F32),
        (vmem, (layers, part_h), F32),
        (hbm, (layers, part_h, width), F32),
        (vmem, (layers, part), F32),
        (vmem, (layers, 2, part), F32),
        (vmem, (layers, 2, part), F32),
    ]
    return pl.pallas_call(
        spread_kernel,
        out_shape=tuple(jax.ShapeDtypeStruct(shape, kind) for _, shape, kind in outs),
        in_specs=[vmem, vmem, hbm, vmem],
        out_specs=tuple(where for where, _, _ in outs),
        scratch_shapes=[
            pltpu.VMEM(shares.shape, BF),
            *[pltpu.VMEM(outs[i][1], F32) for i in (2, 4, 5, 6, 8)],
            pltpu.SemaphoreType.DMA((2 * layers,)),
            pltpu.SemaphoreType.DMA((layers, 5)),
        ],
        compiler_params=pltpu.CompilerParams(vmem_limit_bytes=62 * 1024 * 1024),
        name="spread",
    )(final, igrad, shares, sums)


def shards(
    pages_in,
    coords,
    boxes,
    qkv_weight,
    attn_bias,
    pos_weight,
    out_weight,
    ffn_in,
    ffn_in_bias,
    ffn_out,
    ffn_out_bias,
    ln_gain,
    ln_bias,
    cotangent,
):
    groups = lax.axis_size("dp")
    s = lax.axis_index("section")
    layer = s // 2
    is_attn = s % 2 == 0
    micro, length, width = pages_in.shape
    hidden = ffn_in.shape[2]
    part = width // groups
    part_h = hidden // groups

    def pick(array):
        return lax.dynamic_index_in_dim(array, layer, 0, keepdims=False)

    inputs = {
        "pages": pages_in,
        "cot": cotangent,
        "coords": coords,
        "boxes": boxes.transpose(0, 2, 1),
        "waves": turns_per_unit(width),
    }
    if groups == 8:
        inputs.update(
            qkv_w=qkv_weight,
            pos_w=pos_weight,
            out_w=out_weight,
            in_w=ffn_in,
            down_w=ffn_out,
            attn_b=attn_bias.transpose(1, 0, 2),
            in_b=ffn_in_bias,
            down_b=ffn_out_bias,
            gain_w=ln_gain,
            offset_w=ln_bias,
        )
        got = pipeline(True, hidden, inputs)
        return spread_out(got, part, part_h)

    norm_row = s % 2
    gain_own = lax.dynamic_index_in_dim(pick(ln_gain), norm_row, 0, keepdims=False)
    offset_own = lax.dynamic_index_in_dim(pick(ln_bias), norm_row, 0, keepdims=False)
    own_a = jnp.where(
        is_attn, jnp.concatenate([pick(qkv_weight), pick(pos_weight)], axis=1), pick(ffn_in)
    )
    own_b = jnp.where(
        is_attn, jnp.pad(pick(out_weight), ((0, part_h - part), (0, 0))), pick(ffn_out)
    )
    wa = lax.all_gather(own_a, "dp", axis=0, tiled=True)
    wb_all = lax.all_gather(own_b, "dp", axis=0, tiled=False)
    wb = jnp.where(
        is_attn,
        jnp.pad(wb_all[:, :part].reshape(width, width), ((0, hidden - width), (0, 0))),
        wb_all.reshape(hidden, width),
    )
    bias_own = jnp.where(
        is_attn,
        jnp.pad(pick(attn_bias).reshape(-1), (0, part_h - 3 * part)),
        pick(ffn_in_bias),
    )
    vec_own = jnp.concatenate([bias_own, pick(ffn_out_bias), gain_own, offset_own])
    vec_all = lax.all_gather(vec_own, "dp", axis=0, tiled=False).astype(F32)
    first = jnp.where(
        is_attn,
        jnp.pad(
            vec_all[:, : 3 * part].reshape(groups, 3, part).transpose(1, 0, 2).reshape(-1),
            (0, hidden - 3 * width),
        ),
        vec_all[:, :part_h].reshape(-1),
    )
    rest = vec_all[:, part_h:].reshape(groups, 3, part).transpose(1, 0, 2).reshape(-1)
    inputs["vec_in"] = jnp.pad(
        jnp.stack([first, jnp.pad(rest, (0, hidden - 3 * width))]), ((0, 6), (0, 0))
    )
    wide_blocks = wa.reshape(width, hidden // width, width).transpose(1, 0, 2)
    inputs["w_in"] = jnp.concatenate([wide_blocks.reshape(hidden, width), wb], axis=0)
    got = pipeline(False, hidden, inputs)
    final, igrad, dw, small = got["final_o"], got["igrad_o"], got["dw_o"], got["small_o"]
    dwa = dw[:hidden].reshape(hidden // width, width, width).transpose(1, 0, 2)
    dwa = dwa.reshape(width, hidden)
    dwb = dw[hidden:]

    shard_a = lax.psum_scatter(dwa, "dp", scatter_dimension=0, tiled=True)
    dwb_cut = jnp.where(
        is_attn,
        jnp.pad(
            dwb[:width].reshape(groups, part, width), ((0, 0), (0, part_h - part), (0, 0))
        ),
        dwb.reshape(groups, part_h, width),
    )
    shard_b = lax.psum_scatter(dwb_cut, "dp", scatter_dimension=0, tiled=True).reshape(
        part_h, width
    )
    small_first = jnp.where(
        is_attn,
        jnp.pad(
            small[0, : 3 * width].reshape(3, groups, part).transpose(1, 0, 2).reshape(groups, -1),
            ((0, 0), (0, part_h - 3 * part)),
        ),
        small[0].reshape(groups, part_h),
    )
    small_rest = (
        small[1, : 3 * width].reshape(3, groups, part).transpose(1, 0, 2).reshape(groups, -1)
    )
    small_cut = jnp.concatenate([small_first, small_rest], axis=1)
    shard_s = lax.psum_scatter(small_cut, "dp", scatter_dimension=0, tiled=True).reshape(-1)

    all_a = lax.all_gather(shard_a, "section", axis=0, tiled=False)
    all_b = lax.all_gather(shard_b, "section", axis=0, tiled=False)
    all_s = lax.all_gather(shard_s, "section", axis=0, tiled=False)

    attn_a, feed_a = all_a[0::2], all_a[1::2]
    attn_s, feed_s = all_s[0::2], all_s[1::2]
    rest_s = all_s[:, part_h:].reshape(-1, 2, 3, part)
    return (
        final,
        igrad,
        attn_a[:, :, : 3 * width].astype(F32),
        attn_s[:, : 3 * part].reshape(-1, 3, part),
        attn_a[:, :, 3 * width :].astype(F32),
        all_b[0::2, :part].astype(F32),
        feed_a.astype(F32),
        feed_s[:, :part_h],
        all_b[1::2].astype(F32),
        feed_s[:, part_h : part_h + part],
        rest_s[:, :, 1],
        rest_s[:, :, 2],
    )


def solution(mesh):
    in_specs = (
        P("dp", None, None),
        P("dp", None, None),
        P("dp", None, None),
        P(None, "dp", None),
        P(None, None, "dp"),
        P(None, "dp", None),
        P(None, "dp", None),
        P(None, "dp", None),
        P(None, "dp"),
        P(None, "dp", None),
        P(None, "dp"),
        P(None, None, "dp"),
        P(None, None, "dp"),
        P("dp", None, None),
    )
    out_specs = (
        P("dp", "section", None),
        P("dp", "section", None),
        P(None, "dp", None),
        P(None, None, "dp"),
        P(None, "dp", None),
        P(None, "dp", None),
        P(None, "dp", None),
        P(None, "dp"),
        P(None, "dp", None),
        P(None, "dp"),
        P(None, None, "dp"),
        P(None, None, "dp"),
    )
    return jax.shard_map(shards, mesh=mesh, in_specs=in_specs, out_specs=out_specs, check_vma=False)
```
